32 devices in a mesh: dp: 8 (over y, x, core), tensor: 4 (over z).
Axes of the slice: x: 2, y: 2, z: 4, core: 2. Of those that a mesh axis runs over, the one named last changes fastest.
Arguments:
- tokens: bfloat16 [8192, 2048], P('dp', 'tensor'), may hold values from -6 to 6
- cotangent: bfloat16 [8192, 2048], P('dp', 'tensor'), may hold values from -6 to 6
- norm_gain: bfloat16 [2048], replicated, may hold values from 0.099609375 to 1.8984375
- gate_proj: bfloat16 [2048, 4096], P(None, 'tensor'), may hold values from -0.125 to 0.125
- value_proj: bfloat16 [2048, 4096], P(None, 'tensor'), may hold values from -0.125 to 0.125
- state_proj: bfloat16 [2048, 256], replicated, may hold values from -0.125 to 0.125
- step_proj: bfloat16 [2048, 64], P(None, 'tensor'), may hold values from -0.125 to 0.125
- conv_value: bfloat16 [4, 4096], P(None, 'tensor'), may hold values from -3 to 3
- conv_value_bias: bfloat16 [4096], P('tensor'), may hold values from -3 to 3
- conv_state: bfloat16 [4, 256], replicated, may hold values from -3 to 3
- conv_state_bias: bfloat16 [256], replicated, may hold values from -3 to 3
- step_bias: float32 [64], P('tensor'), may hold values from -4 to -1
- decay_log: float32 [64], P('tensor'), may hold values from -7 to 1
- skip_gain: float32 [64], P('tensor'), may hold values from 0.5 to 2
- gate_gain: bfloat16 [4096], P('tensor'), may hold values from 0.099609375 to 1.8984375
- out_proj: bfloat16 [2048, 4096], P(None, 'tensor'), may hold values from -0.09375 to 0.09375
- token_order: int32 [8192], replicated, may hold values from 0 to 8191, as said below
- lengths: int32 [8, 3], P('dp'), may hold values from 1 to 768, 1024 in all within a row
Outputs:
- layer_output: bfloat16 [8192, 2048], P('dp', 'tensor')
- tokens_grad: bfloat16 [8192, 2048], P('dp', 'tensor')
- norm_gain_grad: float32 [2048], P('tensor')
- gate_proj_grad: float32 [2048, 4096], P('dp', 'tensor')
- value_proj_grad: float32 [2048, 4096], P('dp', 'tensor')
- state_proj_grad: float32 [2048, 256], P(('dp', 'tensor'))
- step_proj_grad: float32 [2048, 64], P('dp', 'tensor')
- conv_value_grad: float32 [4, 4096], P(None, 'tensor')
- conv_value_bias_grad: float32 [4096], P('tensor')
- conv_state_grad: float32 [4, 256], replicated
- conv_state_bias_grad: float32 [256], replicated
- step_bias_grad: float32 [64], P('tensor')
- decay_log_grad: float32 [64], P('tensor')
- skip_gain_grad: float32 [64], P('tensor')
- gate_gain_grad: float32 [4096], P('tensor')
- out_proj_grad: float32 [2048, 4096], P('dp', 'tensor')
The draws below stay inside these ranges and needn't reach their ends.
Inputs may be any that keep to these rules, and one draw needn't show every extreme that they name: `token_order`: A permutation. Each group's 1024 packed positions hold runs of 256 consecutive given-order tokens, each run from another group of given-order rows, so that a group receives exactly 256 tokens from each of 4 groups and none from the others. Each group's 3 lengths sum to 1024; its longest is exactly 768.
All inputs are finite; a program needn't handle non-finite values.
Results may differ from the reference program's by a relative error of at most 0.0092.
Values may be sent and summed in bfloat16 or wider, within the bound.
A program may use at most 192 MiB of HBM per device.

```python
import math
import jax
import jax.numpy as jnp
import numpy as np
from jax import lax

D = 2048
HEADS = 64
STATE = 128
CONV = 4
SPAN = 256
SEQS = 3
TOK_DEV = 1024
INNER = 4096
MAXLEN = 768
TOKENS = 8192
N_DP = 8


def draw_token_order(key, part):
    key = jax.random.fold_in(key, 7)
    first_key, second_key, third_key = jax.random.split(key, 3)
    half_count = N_DP // 2
    piece_len = 2 * TOK_DEV // N_DP
    source_perm = jax.random.permutation(first_key, N_DP)
    inverse_source = jnp.argsort(source_perm)
    offsets = jax.random.permutation(second_key, N_DP)[:half_count]
    piece_order = jax.random.permutation(third_key, half_count)
    target_ids = jnp.arange(N_DP)[:, None]
    piece_index = piece_order[None, :]
    source_ids = inverse_source[(target_ids - offsets[piece_index]) % N_DP]
    starts = source_ids * TOK_DEV + piece_index * piece_len
    order_all = starts[:, :, None] + jnp.arange(piece_len)[None, None, :]
    return order_all.reshape(-1).astype(jnp.int32)


def block_levels(key, extent, cuts, low, high):
    def one(axis_at, blocks):
        heights = jax.random.uniform(jax.random.fold_in(jax.random.fold_in(key, 6), axis_at), (blocks,), jnp.float32, low / len(cuts), high / len(cuts))
        return jnp.repeat(jnp.exp(heights), extent[axis_at] // blocks).reshape((-1,) + (1,) * (len(extent) - axis_at - 1))

    loudness = one(*cuts[0])
    for cut in cuts[1:]:
        loudness = loudness * one(*cut)
    return loudness


def split_up(count, total, reach, lean):
    loads = [(1 << 20) // math.isqrt(grade ** lean) + 1 for grade in range(2, count + 1)]
    spare, holding = total - reach - (count - 1), [1] * (count - 1)
    while spare > 0:
        free = [i for i in range(count - 1) if holding[i] < reach]
        mass, budget = sum([loads[i] for i in free]), spare
        for i in free:
            extra = min(reach - holding[i], max(1, budget * loads[i] // mass), spare)
            holding[i] = holding[i] + extra
            spare = spare - extra
    return np.array([reach] + holding)


def ragged(rng, count, total, most, lean):
    if count == 2:
        one = jax.random.randint(rng, (), max(1, total - most), min(most, total - 1) + 1)
        return jnp.stack([one, total - one])
    sizes = jnp.asarray(split_up(count, total, most, lean), jnp.int32)
    couples = (count - 1) // 2
    donor, receiver = sizes[1:1 + 2 * couples:2], sizes[2:2 + 2 * couples:2]
    slack = jnp.minimum(donor - 1, most - receiver)
    passed = jax.random.randint(jax.random.fold_in(rng, 1), (couples,), 0, 1 << 20) % (slack + 1)
    sizes = sizes.at[1:1 + 2 * couples:2].set(donor - passed).at[2:2 + 2 * couples:2].set(receiver + passed)
    return sizes[jax.random.permutation(jax.random.fold_in(rng, 2), count)]


def noise(stream_key, dims, scale, reach, shards=(), held_as=jnp.bfloat16):
    values = jax.random.normal(stream_key, dims, jnp.float32) * scale
    if len(shards) > 0:
        values = block_levels(stream_key, dims, shards, -0.22, 0.18) * values
    return jnp.clip(values, min=-reach, max=reach).astype(held_as)


def setup_inputs(seed: int = 0) -> dict:
    splits = jax.random.split(jax.random.key(seed), 19)
    return {
        "tokens": noise(splits[0], (TOKENS, D), 1.0, 6.0, ((0, 8), (1, 4))),
        "cotangent": noise(splits[1], (TOKENS, D), 1.0, 6.0, ((0, 8), (1, 4))),
        "norm_gain": jnp.clip(1.0 + 0.18 * jax.random.normal(splits[2], (D,), jnp.float32), 0.099609375, 1.8984375).astype(jnp.bfloat16),
        "gate_proj": noise(splits[3], (D, INNER), D ** -0.5, 0.125, ((1, 4),)),
        "value_proj": noise(splits[4], (D, INNER), D ** -0.5, 0.125, ((1, 4),)),
        "state_proj": noise(splits[5], (D, 2 * STATE), D ** -0.5, 0.125),
        "step_proj": noise(splits[6], (D, HEADS), D ** -0.5, 0.125, ((1, 4),)),
        "conv_value": noise(splits[7], (CONV, INNER), 0.5, 3.0, ((1, 4),)),
        "conv_value_bias": noise(splits[8], (INNER,), 0.5, 3.0, ((0, 4),)),
        "conv_state": noise(splits[9], (CONV, 2 * STATE), 0.5, 3.0),
        "conv_state_bias": noise(splits[10], (2 * STATE,), 0.5, 3.0),
        "step_bias": jnp.clip(-4.0 + 3.0 * jax.random.uniform(splits[11], (HEADS,), jnp.float32) ** block_levels(splits[11], (HEADS,), ((0, 4),), -0.2, 0.2), -4.0, -1.0),
        "decay_log": jnp.clip(-7.0 + 8.0 * jax.random.uniform(splits[12], (HEADS,), jnp.float32) ** block_levels(splits[12], (HEADS,), ((0, 4),), -0.2, 0.2), -7.0, 1.0),
        "skip_gain": jnp.clip(0.5 + 1.5 * jax.random.uniform(splits[13], (HEADS,), jnp.float32) ** block_levels(splits[13], (HEADS,), ((0, 4),), -0.2, 0.2), 0.5, 2.0),
        "gate_gain": jnp.clip(1.0 + 0.18 * jax.random.normal(splits[14], (INNER,), jnp.float32), 0.099609375, 1.8984375).astype(jnp.bfloat16),
        "out_proj": noise(splits[15], (D, INNER), INNER ** -0.5, 0.09375, ((1, 4),)),
        "token_order": draw_token_order(jax.random.fold_in(splits[18], 71), 0),
        "lengths": jax.vmap(lambda own: ragged(own, SEQS, TOK_DEV, MAXLEN, 2))(jax.random.split(splits[17], N_DP)).reshape((N_DP, SEQS)).astype(jnp.int32),
    }


epsilon = 1e-05
highest = lax.Precision.HIGHEST

@jax.custom_vjp
def low(v):
    return lax.optimization_barrier(v.astype(jnp.bfloat16)).astype(jnp.float32)

@jax.custom_vjp
def low_back(v):
    return v

def low_keep(v):
    return (low(v), None)

def low_pass(kept, grad):
    return (grad,)

def back_keep(v):
    return (v, None)

def back_low(kept, grad):
    return (low(grad),)
low.defvjp(low_keep, low_pass)
low_back.defvjp(back_keep, back_low)

def segment_ids(length_row, row_total):
    length_ends = jnp.cumsum(length_row).astype(jnp.int32)
    position = jnp.arange(row_total, dtype=jnp.int32)
    return lax.optimization_barrier(jnp.sum((position[:, None] >= length_ends[None, :]).astype(jnp.int32), axis=1)).astype(jnp.int32)

def causal_conv(values, tap_weights, seg_ids):
    row_count = values.shape[0]
    summed = jnp.zeros_like(values)
    for tap_index in range(tap_weights.shape[0]):
        offset = tap_weights.shape[0] - 1 - tap_index
        shifted = jnp.pad(values, ((offset, 0), (0, 0)))[:row_count]
        earlier = jnp.pad(seg_ids, (offset, 0), constant_values=-1)[:row_count]
        keep_mask = (earlier == seg_ids).astype(values.dtype)
        summed = summed + tap_weights[tap_index][None, :] * shifted * keep_mask[:, None]
    return summed

def span_step(carry_state, pieces):
    value_block, step_block, decay_block, entry_block, exit_block, segment_block, segment_before = pieces
    cumulative = jnp.cumsum(decay_block, axis=0)
    cum_heads = cumulative.T
    position = jnp.arange(segment_block.shape[0], dtype=jnp.int32)
    allowed = (segment_block[:, None] == segment_block[None, :]) & (position[:, None] >= position[None, :])
    spread = cum_heads[:, :, None] - cum_heads[:, None, :]
    decay_mask = jnp.exp(jnp.where(allowed[None], spread, -1e+30))
    scores = jnp.dot(exit_block, entry_block.T, precision=highest)
    weighted = value_block * step_block[:, :, None]
    inside = jnp.einsum('ij,hij,jhp->ihp', scores, decay_mask, weighted, precision=highest)
    segment_last = segment_block[-1]
    to_end = jnp.exp(cumulative[-1][None, :] - cumulative) * (segment_block == segment_last).astype(cumulative.dtype)[:, None]
    local_state = jnp.einsum('jn,jh,jhp->hnp', entry_block, to_end, weighted, precision=highest)
    from_start = jnp.exp(cumulative) * (segment_block == segment_before).astype(cumulative.dtype)[:, None]
    carried = jnp.einsum('in,hnp->ihp', exit_block, carry_state, precision=highest) * from_start[:, :, None]
    carry_factor = jnp.exp(cumulative[-1]) * (segment_last == segment_before).astype(cumulative.dtype)
    new_state = carry_factor[:, None, None] * carry_state + local_state
    return (new_state, inside + carried)

def scan_ssd(per_head, step_sizes, log_decay, entry_mat, exit_mat, seg_ids):
    blocks = per_head.shape[0] // SPAN
    before_all = jnp.concatenate([jnp.full((1,), -1, dtype=jnp.int32), seg_ids[:-1]])
    before_first = before_all.reshape(blocks, SPAN)[:, 0]

    def split_blocks(values):
        return values.reshape((blocks, SPAN) + values.shape[1:])
    pieces = (split_blocks(per_head), split_blocks(step_sizes), split_blocks(log_decay), split_blocks(entry_mat), split_blocks(exit_mat), split_blocks(seg_ids), before_first)
    initial = jnp.zeros((per_head.shape[1], entry_mat.shape[1], per_head.shape[2]), per_head.dtype)
    final_state, outputs = lax.scan(jax.checkpoint(span_step), initial, pieces)
    return outputs.reshape(per_head.shape)

def mixer(gate_raw, value_raw, state_raw, step_raw, conv_value, conv_value_bias, conv_state, conv_state_bias, step_bias, decay_log, skip_gain, seg_ids):
    value_conv = jax.nn.silu(causal_conv(value_raw, conv_value, seg_ids) + conv_value_bias)
    state_conv = jax.nn.silu(causal_conv(state_raw, conv_state, seg_ids) + conv_state_bias)
    half_state = state_conv.shape[1] // 2
    step_sizes = jax.nn.softplus(step_raw + step_bias)
    log_decay = -step_sizes * jnp.exp(decay_log)
    head_count = step_sizes.shape[1]
    per_head = value_conv.reshape(value_conv.shape[0], head_count, -1)
    ssd_out = scan_ssd(per_head, step_sizes, log_decay, state_conv[:, :half_state], state_conv[:, half_state:], seg_ids)
    ssd_out = ssd_out + skip_gain[None, :, None] * per_head
    return ssd_out.reshape(value_conv.shape) * jax.nn.silu(gate_raw)

def forward(tokens, norm_gain, gate_proj, value_proj, state_proj, step_proj, conv_value, conv_value_bias, conv_state, conv_state_bias, step_bias, decay_log, skip_gain, gate_gain, out_proj, token_order, lengths):
    packed = tokens[token_order]
    inv_rms = lax.rsqrt(lax.optimization_barrier(jnp.mean(packed * packed, axis=-1, keepdims=True)) + epsilon)
    normed = low(packed * inv_rms * norm_gain)
    gate_raw = low_back(jnp.dot(normed, gate_proj, precision=highest))
    value_raw = low_back(jnp.dot(normed, value_proj, precision=highest))
    state_raw = low_back(jnp.dot(normed, state_proj, precision=highest))
    step_raw = low_back(jnp.dot(normed, step_proj, precision=highest))
    group_count = lengths.shape[0]
    per_group = packed.shape[0] // group_count

    def regroup(values):
        return values.reshape((group_count, per_group) + values.shape[1:])

    def one_group(pieces):
        gate_part, value_part, state_part, step_part, length_row = pieces
        seg_ids = segment_ids(length_row, per_group)
        return mixer(gate_part, value_part, state_part, step_part, conv_value, conv_value_bias, conv_state, conv_state_bias, step_bias, decay_log, skip_gain, seg_ids)
    gated = lax.map(one_group, (regroup(gate_raw), regroup(value_raw), regroup(state_raw), regroup(step_raw), lengths))
    gated = gated.reshape(packed.shape[0], -1)
    inner_rms = lax.rsqrt(lax.optimization_barrier(jnp.mean(gated * gated, axis=-1, keepdims=True)) + epsilon)
    scaled = low(gated * inner_rms * gate_gain)
    result = packed + jnp.dot(scaled, out_proj.T, precision=highest)
    return jnp.zeros_like(result).at[token_order].set(result)

def reference(tokens, cotangent, norm_gain, gate_proj, value_proj, state_proj, step_proj, conv_value, conv_value_bias, conv_state, conv_state_bias, step_bias, decay_log, skip_gain, gate_gain, out_proj, token_order, lengths):
    floats = [values.astype(jnp.float32) for values in (tokens, norm_gain, gate_proj, value_proj, state_proj, step_proj, conv_value, conv_value_bias, conv_state, conv_state_bias, step_bias, decay_log, skip_gain, gate_gain, out_proj)]

    def wrapped(*values):
        return forward(*values, token_order, lengths)
    layer_output, pullback = jax.vjp(wrapped, *floats)
    gradients = pullback(cotangent.astype(jnp.float32))
    return (layer_output.astype(jnp.bfloat16), gradients[0].astype(jnp.bfloat16), gradients[1], gradients[2], gradients[3], gradients[4], gradients[5], gradients[6], gradients[7], gradients[8], gradients[9], gradients[10], gradients[11], gradients[12], gradients[13], gradients[14])
```

```python
import jax
import jax.numpy as jnp
from jax import lax
from jax.experimental import pallas as pl
from jax.experimental.pallas import tpu as pltpu
from jax.sharding import PartitionSpec as P

f32 = jnp.float32
bf16 = jnp.bfloat16
Q = 256
LANES = 128
HEAD_DIM = 64
highest = lax.Precision.HIGHEST
epsilon = 1e-05


def dot_nn(a, b, precision=None):
    return lax.dot_general(a, b, (((1,), (0,)), ((), ())), precision=precision, preferred_element_type=f32)


def dot_nt(a, b, precision=None):
    return lax.dot_general(a, b, (((1,), (1,)), ((), ())), precision=precision, preferred_element_type=f32)


def halves(values):
    high = values.astype(bf16)
    return jnp.concatenate([high, (values - high.astype(f32)).astype(bf16)], axis=1)


def dot_halves(a, values):
    both = dot_nn(a, halves(values))
    return both[:, :LANES] + both[:, LANES:]


def sigmoid(values):
    return 1.0 / (1.0 + jnp.exp(-values))


def fold_rows(values):
    return jnp.sum(values.reshape(-1, 8, values.shape[-1]), axis=0)


def segment_at(position, lengths_ref):
    total = lengths_ref[0, 0]
    seg = (position >= total).astype(jnp.int32)
    for index in range(1, lengths_ref.shape[1]):
        total = total + lengths_ref[0, index]
        seg = seg + (position >= total).astype(jnp.int32)
    return seg


def tap_mask(start, shift, rows, lengths_ref):
    position = start + lax.broadcasted_iota(jnp.int32, (rows, LANES), 0)
    same = (segment_at(position, lengths_ref) == segment_at(position - shift, lengths_ref)) & (position >= shift)
    return same.astype(f32)


def triangle(start, lengths_ref, transposed):
    first = lax.broadcasted_iota(jnp.int32, (Q, Q), 0)
    second = lax.broadcasted_iota(jnp.int32, (Q, Q), 1)
    same = segment_at(start + first, lengths_ref) == segment_at(start + second, lengths_ref)
    order = (second >= first) if transposed else (first >= second)
    return same & order


def head_columns(cum, step, cum_cols, step_cols):
    lane = lax.broadcasted_iota(jnp.int32, (Q, LANES), 1)
    for head in range(cum_cols.shape[0]):
        cum_cols[head] = jnp.broadcast_to(cum[:, head : head + 1], (Q, LANES))
    for pair in range(step_cols.shape[0]):
        even = jnp.broadcast_to(step[:, 2 * pair : 2 * pair + 1], (Q, LANES))
        odd = jnp.broadcast_to(step[:, 2 * pair + 1 : 2 * pair + 2], (Q, LANES))
        step_cols[pair] = jnp.where(lane < HEAD_DIM, even, odd)


def boundary(start, lengths_ref):
    position = start + lax.broadcasted_iota(jnp.int32, (Q, LANES), 0)
    seg = segment_at(position, lengths_ref)
    last = segment_at(jnp.full((1, LANES), start + Q - 1, jnp.int32), lengths_ref)
    before = segment_at(jnp.full((1, LANES), start - 1, jnp.int32), lengths_ref)
    before = jnp.where(start > 0, before, -1)
    return (seg == last), (seg == before), (last == before)


def softplus(values):
    return jnp.maximum(values, 0.0) + jnp.log1p(jnp.exp(-jnp.abs(values)))


def causal_taps(ext_ref, taps, bias, start, lengths_ref, columns):
    total = taps[3:4] * ext_ref[pl.ds(8, Q), columns]
    for shift in range(1, 4):
        mask = tap_mask(start, shift, Q, lengths_ref)
        total = total + taps[3 - shift : 4 - shift] * (ext_ref[pl.ds(8 - shift, Q), columns] * mask)
    return total + bias


def chunk_scalars(start, step_in, rate, lengths_ref, causal):
    step = softplus(step_in)
    log_decay = -step * jnp.exp(rate)
    cum = dot_nn(causal, log_decay, highest)
    return step, log_decay, cum


def fwd_kernel(
    lengths_ref, x_ref, gain_ref, wg_ref, wv_ref, ws_ref, wt_ref, tapv_ref, biasv_ref, taps_ref, biass_ref,
    stepb_ref, rate_ref, skip_ref,
    normed_ref, inv_ref, gate_ref, vraw_ref, pre_ref, y_ref, sraw_ref, spre_ref, stepin_ref, state_ref, sq_ref,
    carry, vext, sext, cum_cols, step_cols, cum_rows, neg_bias, scores, gated_sq,
):
    chunk = pl.program_id(0)
    start = chunk * Q
    pairs = carry.shape[0]

    @pl.when(chunk == 0)
    def _():
        carry[...] = jnp.zeros_like(carry)
        vext[pl.ds(0, 8)] = jnp.zeros((8, vext.shape[1]), f32)
        sext[pl.ds(0, 8)] = jnp.zeros((8, sext.shape[1]), f32)

    @pl.when(chunk > 0)
    def _():
        vext[pl.ds(0, 8)] = vext[pl.ds(Q, 8)]
        sext[pl.ds(0, 8)] = sext[pl.ds(Q, 8)]

    wide = x_ref[...].astype(f32)
    inv = lax.rsqrt(jnp.mean(wide * wide, axis=1, keepdims=True) + epsilon)
    normed = (wide * inv * gain_ref[...]).astype(bf16)
    normed_ref[...] = normed
    inv_ref[...] = inv
    gate_ref[...] = dot_nn(normed, wg_ref[...])
    vext[pl.ds(8, Q)] = dot_nn(normed, wv_ref[...])
    sext[pl.ds(8, Q)] = dot_nn(normed, ws_ref[...])
    step_in = dot_nn(normed, wt_ref[...]) + stepb_ref[...]
    stepin_ref[...] = step_in
    vraw_ref[...] = vext[pl.ds(8, Q)]
    sraw_ref[...] = sext[pl.ds(8, Q)]

    can_see = triangle(start, lengths_ref, False)
    neg_bias[...] = jnp.where(can_see, 0.0, -1e30)
    row = lax.broadcasted_iota(jnp.int32, (Q, Q), 0)
    col = lax.broadcasted_iota(jnp.int32, (Q, Q), 1)
    step, log_decay, cum = chunk_scalars(start, step_in, rate_ref[...], lengths_ref, (row >= col).astype(f32))
    cum_rows[...] = cum.T
    head_columns(cum, step, cum_cols, step_cols)

    for half in range(2):
        columns = slice(half * LANES, (half + 1) * LANES)
        spre_ref[:, columns] = causal_taps(
            sext, taps_ref[:, columns], biass_ref[:, columns], start, lengths_ref, columns
        )
    spre = spre_ref[...]
    state_conv = spre * sigmoid(spre)
    entry = state_conv[:, :LANES]
    leave = state_conv[:, LANES:]
    scores[...] = dot_nt(leave, entry, highest)
    entry_t = entry.T.astype(bf16)
    leave_low = leave.astype(bf16)
    with_last, with_before, through = boundary(start, lengths_ref)
    to_last = with_last.astype(f32)
    from_before = with_before.astype(f32)
    passes = through.astype(f32)
    lane = lax.broadcasted_iota(jnp.int32, (Q, LANES), 1)
    gated_sq[...] = jnp.zeros_like(gated_sq)

    def one_pair(pair, nothing):
        columns = pl.ds(pl.multiple_of(pair * LANES, LANES), LANES)
        pre = causal_taps(vext, tapv_ref[:, columns], biasv_ref[:, columns], start, lengths_ref, columns)
        pre_ref[:, columns] = pre
        x = pre * sigmoid(pre)
        weighted = x * step_cols[pair]
        both = halves(weighted)
        results = []
        for half in range(2):
            head = 2 * pair + half
            c_col = cum_cols[head]
            c_row = cum_rows[pl.ds(head, 1), :]
            top = scores[:LANES, :LANES] * jnp.exp(c_col[:LANES] - c_row[:, :LANES] + neg_bias[:LANES, :LANES])
            low_left = scores[LANES:, :LANES] * jnp.exp(c_col[LANES:] - c_row[:, :LANES] + neg_bias[LANES:, :LANES])
            low_right = scores[LANES:, LANES:] * jnp.exp(c_col[LANES:] - c_row[:, LANES:] + neg_bias[LANES:, LANES:])
            upper = dot_nn(top.astype(bf16), both[:LANES])
            lower = dot_nn(jnp.concatenate([low_left, low_right], axis=1).astype(bf16), both)
            out = jnp.concatenate([upper, lower], axis=0)
            results.append(out[:, :LANES] + out[:, LANES:])
        inside = jnp.where(lane < HEAD_DIM, results[0], results[1])
        cum_pair = jnp.where(lane < HEAD_DIM, cum_cols[2 * pair], cum_cols[2 * pair + 1])
        cum_last = cum_pair[Q - 1 :]
        held = carry[pair]
        state_ref[0, pair] = held
        carried = dot_halves(leave_low, held) * (jnp.exp(cum_pair) * from_before)
        y = inside + carried + skip_ref[:, columns] * x
        y_ref[:, columns] = y
        to_end = jnp.exp(cum_last - cum_pair) * to_last
        carry[pair] = held * (jnp.exp(cum_last) * passes) + dot_halves(entry_t, to_end * weighted)
        gate = gate_ref[:, columns]
        gated = y * (gate * sigmoid(gate))
        gated_sq[...] += gated * gated
        return nothing

    lax.fori_loop(0, pairs, one_pair, 0)
    sq_ref[...] = jnp.sum(gated_sq[...], axis=1, keepdims=True)


def bwd_kernel(
    lengths_ref, dsc_ref, rms_ref, coef_ref, gain_ref, gate_ref, vraw_ref, pre_ref, y_ref, sraw_ref, spre_ref,
    stepin_ref, state_ref, next_ref, tapv_ref, taps_ref, stepb_ref, rate_ref, skip_ref,
    dgate_ref, dvalue_ref, dstate_ref, dstep_ref, dot_ref, sumv_ref, sums_ref, sumh_ref,
    d_carry, dvext, dsext, cum_cols, step_cols, cum_rows, neg_bias, scores, d_scores, d_entry, d_leave, acc_step,
    acc_cum, acc_dot,
):
    index = pl.program_id(0)
    chunks = pl.num_programs(0)
    chunk = chunks - 1 - index
    start = chunk * Q
    pairs = d_carry.shape[0]

    @pl.when(index == 0)
    def _():
        d_carry[...] = jnp.zeros_like(d_carry)
        dvext[pl.ds(Q, 8)] = jnp.zeros((8, dvext.shape[1]), f32)
        dsext[pl.ds(Q, 8)] = jnp.zeros((8, dsext.shape[1]), f32)
        sumv_ref[...] = jnp.zeros_like(sumv_ref)
        sums_ref[...] = jnp.zeros_like(sums_ref)
        sumh_ref[...] = jnp.zeros_like(sumh_ref)

    @pl.when(index > 0)
    def _():
        dvext[pl.ds(Q, 8)] = dvext[pl.ds(0, 8)]
        dsext[pl.ds(Q, 8)] = dsext[pl.ds(0, 8)]

    can_see = triangle(start, lengths_ref, True)
    neg_bias[...] = jnp.where(can_see, 0.0, -1e30)
    row = lax.broadcasted_iota(jnp.int32, (Q, Q), 0)
    col = lax.broadcasted_iota(jnp.int32, (Q, Q), 1)
    step_in = stepin_ref[...]
    step, log_decay, cum = chunk_scalars(start, step_in, rate_ref[...], lengths_ref, (row >= col).astype(f32))
    cum_rows[...] = cum.T
    head_columns(cum, step, cum_cols, step_cols)

    spre = spre_ref[...]
    spre_sig = sigmoid(spre)
    state_conv = spre * spre_sig
    entry = state_conv[:, :LANES]
    leave = state_conv[:, LANES:]
    scores[...] = dot_nt(entry, leave, highest)
    entry_low = entry.astype(bf16)
    leave_low = leave.astype(bf16)
    leave_t = leave.T.astype(bf16)
    with_last, with_before, through = boundary(start, lengths_ref)
    to_last = with_last.astype(f32)
    from_before = with_before.astype(f32)
    passes = through.astype(f32)
    lane = lax.broadcasted_iota(jnp.int32, (Q, LANES), 1)
    first_half = lane < HEAD_DIM
    row_lane = lax.broadcasted_iota(jnp.int32, (Q, LANES), 0)
    for ref in (d_scores, d_entry, d_leave, acc_step, acc_cum, acc_dot):
        ref[...] = jnp.zeros_like(ref)
    rms = rms_ref[...]
    coef = coef_ref[...]

    def one_pair(pair, nothing):
        columns = pl.ds(pl.multiple_of(pair * LANES, LANES), LANES)
        pre = pre_ref[:, columns]
        pre_sig = sigmoid(pre)
        x = pre * pre_sig
        step_pair = step_cols[pair]
        weighted = x * step_pair
        gate = gate_ref[:, columns]
        gate_sig = sigmoid(gate)
        gate_silu = gate * gate_sig
        y = y_ref[:, columns]
        gated = y * gate_silu
        d_scaled = dsc_ref[:, columns].astype(f32)
        d_gated = rms * (d_scaled * gain_ref[:, columns]) - gated * coef
        sumv_ref[pl.ds(0, 8), columns] += fold_rows(d_scaled * gated * rms)
        d_gate = (d_gated * y * (gate_sig + gate_silu * (1.0 - gate_sig))).astype(bf16)
        dgate_ref[:, columns] = d_gate
        acc_dot[...] += d_gate.astype(f32) * gate
        d_y = d_gated * gate_silu
        skip = skip_ref[:, columns]
        sumv_ref[pl.ds(8, 8), columns] += fold_rows(d_y * x)
        y_scan = y - skip * x

        d_y_low = d_y.astype(bf16)
        d_y_t = d_y.T.astype(bf16)
        d_y_both = halves(d_y)
        weighted_low = weighted.astype(bf16)
        results = []
        for half in range(2):
            head = 2 * pair + half
            own = jnp.where(first_half if half == 0 else ~first_half, weighted_low, jnp.zeros_like(weighted_low))
            d_m_top = dot_nn(own[:LANES], d_y_t)
            d_m_low = dot_nn(own[LANES:], d_y_t[:, LANES:])
            c_col = cum_cols[head]
            c_row = cum_rows[pl.ds(head, 1), :]
            l_top = jnp.exp(c_row - jnp.concatenate([c_col[:LANES]] * 2, axis=1) + neg_bias[:LANES])
            l_low = jnp.exp(c_row[:, LANES:] - c_col[LANES:] + neg_bias[LANES:, LANES:])
            d_scores[:LANES] += d_m_top * l_top
            d_scores[LANES:, LANES:] += d_m_low * l_low
            m_top = (scores[:LANES] * l_top).astype(bf16)
            m_low = (scores[LANES:, LANES:] * l_low).astype(bf16)
            upper = dot_nn(m_top, d_y_both)
            lower = dot_nn(m_low, d_y_both[LANES:])
            out = jnp.concatenate([upper, lower], axis=0)
            results.append(out[:, :LANES] + out[:, LANES:])
        d_weighted = jnp.where(first_half, results[0], results[1])
        cum_pair = jnp.where(first_half, cum_cols[2 * pair], cum_cols[2 * pair + 1])
        cum_last = cum_pair[Q - 1 :]
        to_end = jnp.exp(cum_last - cum_pair) * to_last
        from_start = jnp.exp(cum_pair) * from_before
        d_state = d_carry[pair]
        held = state_ref[0, pair]
        d_weighted = d_weighted + dot_halves(entry_low, d_state) * to_end
        d_entry[...] += dot_nt((to_end * weighted).astype(bf16), d_state.astype(bf16))
        moved = from_start * d_y
        d_leave[...] += dot_nt(moved.astype(bf16), held.astype(bf16))
        state_dot = jnp.sum(next_ref[0, pair] * d_state, axis=0, keepdims=True)
        d_carry[pair] = d_state * (jnp.exp(cum_last) * passes) + dot_halves(leave_t, moved)

        to_step = d_weighted * x
        to_cum = d_y * y_scan - to_step * step_pair + jnp.where(row_lane == Q - 1, state_dot, 0.0)
        place = lax.broadcasted_iota(jnp.int32, (2 * LANES, LANES), 1)
        source = lax.broadcasted_iota(jnp.int32, (2 * LANES, LANES), 0)
        source = (lax.rem(source, LANES) >= HEAD_DIM).astype(jnp.int32) + 2 * pair
        gather = (place == source).astype(bf16)
        acc_step[...] += dot_nn(halves(to_step), gather)
        acc_cum[...] += dot_nn(halves(to_cum), gather)

        d_x = d_weighted * step_pair + skip * d_y
        d_pre = d_x * (pre_sig + x * (1.0 - pre_sig))
        dvext[pl.ds(0, Q), columns] = d_pre
        sumv_ref[pl.ds(16, 8), columns] += fold_rows(d_pre)
        vraw = vraw_ref[:, columns]
        total = tapv_ref[3:4, columns] * d_pre
        sumv_ref[pl.ds(24, 8), columns] += fold_rows(vraw * d_pre)
        for shift in range(1, 4):
            moved_back = dvext[pl.ds(shift, Q), columns] * later_mask(start, shift)
            total = total + tapv_ref[3 - shift : 4 - shift, columns] * moved_back
            sumv_ref[pl.ds(24 + 8 * shift, 8), columns] += fold_rows(vraw * moved_back)
        d_value = total.astype(bf16)
        dvalue_ref[:, columns] = d_value
        acc_dot[...] += d_value.astype(f32) * vraw
        return nothing

    def later_mask(begin, shift):
        position = begin + lax.broadcasted_iota(jnp.int32, (Q, LANES), 0)
        same = segment_at(position, lengths_ref) == segment_at(position + shift, lengths_ref)
        return (same & (position + shift < chunks * Q)).astype(f32)

    lax.fori_loop(0, pairs, one_pair, 0)

    d_cum = acc_cum[...]
    d_log = dot_nn(can_see.astype(f32), d_cum, highest)
    rate = jnp.exp(rate_ref[...])
    d_step_in = (acc_step[...] - d_log * rate) * sigmoid(step_in)
    d_step = d_step_in.astype(bf16)
    dstep_ref[...] = d_step
    step_raw = step_in - stepb_ref[...]
    real = lane < 2 * pairs
    acc_dot[...] += jnp.where(real, d_step.astype(f32) * step_raw, 0.0)
    sumh_ref[pl.ds(0, 8)] += fold_rows(d_step_in)
    sumh_ref[pl.ds(8, 8)] += fold_rows(d_log * log_decay)

    d_scores_low = d_scores[...]
    d_b = d_entry[...] + dot_halves(d_scores_low.astype(bf16), leave)
    d_c = d_leave[...] + dot_halves(d_scores_low.T.astype(bf16), entry)
    for half, grad in enumerate((d_b, d_c)):
        columns = slice(half * LANES, (half + 1) * LANES)
        part = spre_sig[:, columns]
        d_pre = grad * (part + state_conv[:, columns] * (1.0 - part))
        dsext[pl.ds(0, Q), columns] = d_pre
        sums_ref[pl.ds(0, 8), columns] += fold_rows(d_pre)
        sraw = sraw_ref[:, columns]
        total = taps_ref[3:4, columns] * d_pre
        sums_ref[pl.ds(8, 8), columns] += fold_rows(sraw * d_pre)
        for shift in range(1, 4):
            moved_back = dsext[pl.ds(shift, Q), columns] * later_mask(start, shift)
            total = total + taps_ref[3 - shift : 4 - shift, columns] * moved_back
            sums_ref[pl.ds(8 + 8 * shift, 8), columns] += fold_rows(sraw * moved_back)
        d_state_raw = total.astype(bf16)
        dstate_ref[:, columns] = d_state_raw
        acc_dot[...] += d_state_raw.astype(f32) * sraw
    dot_ref[...] = jnp.sum(acc_dot[...], axis=1, keepdims=True)


def whole(shape):
    zeros = (0,) * len(shape)
    return pl.BlockSpec(shape, lambda i: zeros, pipeline_mode=pl.Buffered(1))


def forward_mixer(lengths, x, gain, wg, wv, ws, wt, tapv, biasv, taps, biass, stepb, rate, skip):
    rows, model = x.shape
    inner = wg.shape[1]
    chunks, pairs = rows // Q, inner // LANES

    def by_chunk(width):
        return pl.BlockSpec((Q, width), lambda i: (i, 0))

    out_shape = [
        jax.ShapeDtypeStruct((rows, model), bf16),
        jax.ShapeDtypeStruct((rows, 1), f32),
        jax.ShapeDtypeStruct((rows, inner), f32),
        jax.ShapeDtypeStruct((rows, inner), f32),
        jax.ShapeDtypeStruct((rows, inner), f32),
        jax.ShapeDtypeStruct((rows, inner), f32),
        jax.ShapeDtypeStruct((rows, 2 * LANES), f32),
        jax.ShapeDtypeStruct((rows, 2 * LANES), f32),
        jax.ShapeDtypeStruct((rows, LANES), f32),
        jax.ShapeDtypeStruct((chunks, pairs, LANES, LANES), f32),
        jax.ShapeDtypeStruct((rows, 1), f32),
    ]
    out_specs = [
        by_chunk(model), by_chunk(1), by_chunk(inner), by_chunk(inner), by_chunk(inner), by_chunk(inner),
        by_chunk(2 * LANES), by_chunk(2 * LANES), by_chunk(LANES),
        pl.BlockSpec((1, pairs, LANES, LANES), lambda i: (i, 0, 0, 0)),
        by_chunk(1),
    ]
    return pl.pallas_call(
        fwd_kernel,
        grid=(chunks,),
        out_shape=out_shape,
        in_specs=[pl.BlockSpec(memory_space=pltpu.SMEM), by_chunk(model)] + [
            whole(v.shape) for v in (gain, wg, wv, ws, wt, tapv, biasv, taps, biass, stepb, rate, skip)
        ],
        out_specs=out_specs,
        scratch_shapes=[
            pltpu.VMEM((pairs, LANES, LANES), f32),
            pltpu.VMEM((Q + 8, inner), f32),
            pltpu.VMEM((Q + 8, 2 * LANES), f32),
            pltpu.VMEM((2 * pairs, Q, LANES), f32),
            pltpu.VMEM((pairs, Q, LANES), f32),
            pltpu.VMEM((LANES, Q), f32),
            pltpu.VMEM((Q, Q), f32),
            pltpu.VMEM((Q, Q), f32),
            pltpu.VMEM((Q, LANES), f32),
        ],
        compiler_params=pltpu.CompilerParams(vmem_limit_bytes=56 << 20),
        name="mixer_forward",
    )(lengths, x, gain, wg, wv, ws, wt, tapv, biasv, taps, biass, stepb, rate, skip)


def backward_mixer(lengths, dsc, rms, coef, gain, gate, vraw, pre, y, sraw, spre, stepin, states, tapv, taps, stepb, rate, skip):
    rows, inner = gate.shape
    chunks, pairs = rows // Q, inner // LANES

    def by_chunk(width):
        return pl.BlockSpec((Q, width), lambda i: (chunks - 1 - i, 0))

    def state_block(ahead):
        return pl.BlockSpec(
            (1, pairs, LANES, LANES), lambda i: (jnp.minimum(chunks - 1 - i + ahead, chunks - 1), 0, 0, 0)
        )

    out_shape = [
        jax.ShapeDtypeStruct((rows, inner), bf16),
        jax.ShapeDtypeStruct((rows, inner), bf16),
        jax.ShapeDtypeStruct((rows, 2 * LANES), bf16),
        jax.ShapeDtypeStruct((rows, LANES), bf16),
        jax.ShapeDtypeStruct((rows, 1), f32),
        jax.ShapeDtypeStruct((56, inner), f32),
        jax.ShapeDtypeStruct((40, 2 * LANES), f32),
        jax.ShapeDtypeStruct((16, LANES), f32),
    ]
    out_specs = [
        by_chunk(inner), by_chunk(inner), by_chunk(2 * LANES), by_chunk(LANES), by_chunk(1),
        whole((56, inner)), whole((40, 2 * LANES)), whole((16, LANES)),
    ]
    return pl.pallas_call(
        bwd_kernel,
        grid=(chunks,),
        out_shape=out_shape,
        in_specs=[
            pl.BlockSpec(memory_space=pltpu.SMEM), by_chunk(inner), by_chunk(1), by_chunk(1), whole(gain.shape),
            by_chunk(inner), by_chunk(inner), by_chunk(inner), by_chunk(inner), by_chunk(2 * LANES),
            by_chunk(2 * LANES), by_chunk(LANES), state_block(0), state_block(1),
        ] + [whole(v.shape) for v in (tapv, taps, stepb, rate, skip)],
        out_specs=out_specs,
        scratch_shapes=[
            pltpu.VMEM((pairs, LANES, LANES), f32),
            pltpu.VMEM((Q + 8, inner), f32),
            pltpu.VMEM((Q + 8, 2 * LANES), f32),
            pltpu.VMEM((2 * pairs, Q, LANES), f32),
            pltpu.VMEM((pairs, Q, LANES), f32),
            pltpu.VMEM((LANES, Q), f32),
            pltpu.VMEM((Q, Q), f32),
            pltpu.VMEM((Q, Q), f32),
            pltpu.VMEM((Q, Q), f32),
            pltpu.VMEM((Q, LANES), f32),
            pltpu.VMEM((Q, LANES), f32),
            pltpu.VMEM((Q, LANES), f32),
            pltpu.VMEM((Q, LANES), f32),
            pltpu.VMEM((Q, LANES), f32),
        ],
        compiler_params=pltpu.CompilerParams(vmem_limit_bytes=56 << 20),
        name="mixer_backward",
    )(lengths, dsc, rms, coef, gain, gate, vraw, pre, y, sraw, spre, stepin, states, states, tapv, taps, stepb, rate, skip)


def contract_rows(left, right):
    return lax.dot_general(left, right, (((0,), (0,)), ((), ())), preferred_element_type=f32)


def pad_heads(values):
    return jnp.pad(values, ((0, 0), (0, LANES - values.shape[1])))


def unfold(sums, index):
    return jnp.sum(sums[8 * index : 8 * index + 8], axis=0)


def per_device(
    tokens, cotangent, norm_gain, gate_proj, value_proj, state_proj, step_proj, conv_value, conv_value_bias,
    conv_state, conv_state_bias, step_bias, decay_log, skip_gain, gate_gain, out_proj, token_order, lengths,
):
    groups = lax.axis_size("dp")
    group = lax.axis_index("dp")
    slots = lax.axis_size("tensor")
    slot = lax.axis_index("tensor")
    rows, width = tokens.shape
    model = width * slots
    inner = gate_proj.shape[1]
    heads = step_bias.shape[0]
    run = 2 * rows // groups
    runs = rows // run

    source_run = token_order.reshape(groups, runs, run)[:, :, 0] // run
    source_group = source_run // runs
    from_here = source_group == group
    send_run = jnp.sum(jnp.where(from_here, source_run % runs, 0), axis=1)
    arrive_from = lax.dynamic_index_in_dim(source_group, group, 0, keepdims=False)
    every = jnp.arange(groups, dtype=jnp.int32)
    back_run = jnp.sum(
        jnp.where(arrive_from[None, :] == every[:, None], jnp.arange(runs, dtype=jnp.int32)[None, :], 0), axis=1
    )
    local_run = group * runs + jnp.arange(runs, dtype=jnp.int32)
    return_from = jnp.sum(
        jnp.where(source_run[None] == local_run[:, None, None], every[None, :, None], 0), axis=(1, 2)
    )

    def exchange(values, choose_send, choose_arrive):
        cut = values.reshape(runs, run, width)[choose_send]
        arrived = lax.all_to_all(cut, "dp", split_axis=0, concat_axis=0, tiled=True)
        return arrived[choose_arrive].reshape(rows, width)

    packed_tokens = exchange(tokens, send_run, arrive_from)
    packed_cotangent = exchange(cotangent, send_run, arrive_from)
    full_tokens = lax.all_gather(packed_tokens, "tensor", axis=1, tiled=True)
    full_cotangent = lax.all_gather(packed_cotangent, "tensor", axis=1, tiled=True)

    gain_full = norm_gain.astype(f32)
    tapv = conv_value.astype(f32)
    taps = conv_state.astype(f32)
    stepb = pad_heads(step_bias[None])
    rate = pad_heads(decay_log[None])
    skip = jnp.repeat(skip_gain, HEAD_DIM)[None]
    (normed, inv_rms, gate, vraw, pre, y, sraw, spre, stepin, states, squares) = forward_mixer(
        lengths, full_tokens, gain_full[None], gate_proj, value_proj, state_proj, pad_heads(step_proj), tapv,
        conv_value_bias.astype(f32)[None], taps, conv_state_bias.astype(f32)[None], stepb, rate, skip,
    )
    d_scaled = dot_nn(full_cotangent, out_proj)
    gain_wide = gate_gain.astype(f32)[None]
    gated = y * jax.nn.silu(gate)
    inner_dot = jnp.sum(d_scaled * gain_wide * gated, axis=1, keepdims=True)
    squares, inner_dot = lax.psum((squares, inner_dot), "tensor")
    inner_total = inner * slots
    inner_rms = lax.rsqrt(squares / inner_total + epsilon)
    scaled = (gated * inner_rms * gain_wide).astype(bf16)
    out_partial = dot_nt(scaled, out_proj).astype(bf16)
    out_share = lax.psum_scatter(out_partial, "tensor", scatter_dimension=1, tiled=True)
    output_packed = (packed_tokens.astype(f32) + out_share.astype(f32)).astype(bf16)
    out_grad = contract_rows(full_cotangent, scaled).astype(bf16)
    coef = inner_rms**3 * inner_dot / inner_total

    (d_gate, d_value, d_state, d_step, row_dot, sumv, sums, sumh) = backward_mixer(
        lengths, d_scaled, inner_rms, coef, gain_wide, gate, vraw, pre, y, sraw, spre, stepin, states, tapv, taps,
        stepb, rate, skip,
    )
    row_dot = lax.psum(row_dot, "tensor")
    back_partial = (
        dot_nt(d_gate, gate_proj) + dot_nt(d_value, value_proj) + dot_nt(d_state, state_proj)
        + dot_nt(d_step[:, :heads], step_proj)
    ).astype(bf16)
    back_share = lax.psum_scatter(back_partial, "tensor", scatter_dimension=1, tiled=True).astype(f32)
    gate_grad = contract_rows(normed, d_gate).astype(bf16)
    value_grad = contract_rows(normed, d_value).astype(bf16)
    state_grad = contract_rows(normed, d_state)
    step_grad = contract_rows(normed, d_step[:, :heads])
    unit_share = packed_tokens.astype(f32) * inv_rms
    gain_share = lax.dynamic_slice_in_dim(gain_full, slot * width, width, 0)
    norm_gain_back = jnp.sum(back_share * unit_share, axis=0)
    d_unit = back_share * gain_share
    input_back = packed_cotangent.astype(f32) + inv_rms * (d_unit - unit_share * (row_dot / model))
    layer_output = exchange(output_packed, back_run, return_from)
    tokens_grad = exchange(input_back.astype(bf16), back_run, return_from)

    def share(grad):
        return lax.psum_scatter(grad, "dp", scatter_dimension=0, tiled=True).astype(f32)

    out_grad_share, gate_share, value_share = share(out_grad), share(gate_grad), share(value_grad)
    step_share = share(step_grad)
    state_share = lax.psum_scatter(state_grad, ("dp", "tensor"), scatter_dimension=0, tiled=True).astype(f32)
    conv_state_sum, conv_state_bias_sum = lax.psum(
        (jnp.stack([unfold(sums, 4 - tap) for tap in range(4)]), unfold(sums, 0)), "tensor"
    )
    small = lax.psum(
        (
            norm_gain_back,
            jnp.stack([unfold(sumv, 6 - tap) for tap in range(4)]),
            unfold(sumv, 2),
            conv_state_sum,
            conv_state_bias_sum,
            unfold(sumh, 0)[:heads],
            unfold(sumh, 1)[:heads],
            jnp.sum(unfold(sumv, 1).reshape(heads, HEAD_DIM), axis=1),
            unfold(sumv, 0),
        ),
        "dp",
    )
    return (
        layer_output, tokens_grad, small[0], gate_share, value_share, state_share, step_share, small[1], small[2],
        small[3], small[4], small[5], small[6], small[7], small[8], out_grad_share,
    )


def solution(mesh):
    across = P(None, "tensor")
    both = P("dp", "tensor")
    heads = P("tensor")
    return jax.shard_map(
        per_device,
        mesh=mesh,
        in_specs=(
            both, both, P(), across, across, P(), across, across, heads, P(), P(), heads, heads, heads, heads, across,
            P(), P("dp", None),
        ),
        out_specs=(
            both, both, heads, both, both, P(("dp", "tensor"), None), both, across, heads, P(), P(), heads, heads, heads,
            heads, both,
        ),
        check_vma=False,
    )
```

```python
import jax
import jax.numpy as jnp
from jax import lax
from jax.experimental import pallas as pl
from jax.experimental.pallas import tpu as pltpu
from jax.sharding import PartitionSpec as P

f32 = jnp.float32
bf16 = jnp.bfloat16
Q = 256
LANES = 128
HEAD_DIM = 64
AHEAD = 2
IN_FLIGHT = 3
HEAD_VMEM = 64 << 20
highest = lax.Precision.HIGHEST
epsilon = 1e-05


def dot_nn(a, b, precision=None):
    return lax.dot_general(a, b, (((1,), (0,)), ((), ())), precision=precision, preferred_element_type=f32)


def dot_nt(a, b, precision=None):
    return lax.dot_general(a, b, (((1,), (1,)), ((), ())), precision=precision, preferred_element_type=f32)


def halves(values):
    high = values.astype(bf16)
    return jnp.concatenate([high, (values - high.astype(f32)).astype(bf16)], axis=1)


def dot_halves(a, values):
    both = dot_nn(a, halves(values))
    return both[:, :LANES] + both[:, LANES:]


def sigmoid(values):
    return 0.5 * jnp.tanh(0.5 * values) + 0.5


def fold_rows(values):
    return jnp.sum(values.reshape(-1, 8, values.shape[-1]), axis=0)


def segment_at(position, lengths_ref):
    total = lengths_ref[0, 0]
    seg = (position >= total).astype(jnp.int32)
    for index in range(1, lengths_ref.shape[1]):
        total = total + lengths_ref[0, index]
        seg = seg + (position >= total).astype(jnp.int32)
    return seg


def tap_mask(start, shift, rows, lengths_ref):
    position = start + lax.broadcasted_iota(jnp.int32, (rows, LANES), 0)
    same = (segment_at(position, lengths_ref) == segment_at(position - shift, lengths_ref)) & (position >= shift)
    return same.astype(f32)


def triangle(start, lengths_ref, transposed):
    first = lax.broadcasted_iota(jnp.int32, (Q, Q), 0)
    second = lax.broadcasted_iota(jnp.int32, (Q, Q), 1)
    same = segment_at(start + first, lengths_ref) == segment_at(start + second, lengths_ref)
    order = (second >= first) if transposed else (first >= second)
    return same & order


def head_columns(cum, step, cum_cols, step_cols):
    lane = lax.broadcasted_iota(jnp.int32, (Q, LANES), 1)
    for head in range(cum_cols.shape[0]):
        cum_cols[head] = jnp.broadcast_to(cum[:, head : head + 1], (Q, LANES))
    for pair in range(step_cols.shape[0]):
        even = jnp.broadcast_to(step[:, 2 * pair : 2 * pair + 1], (Q, LANES))
        odd = jnp.broadcast_to(step[:, 2 * pair + 1 : 2 * pair + 2], (Q, LANES))
        step_cols[pair] = jnp.where(lane < HEAD_DIM, even, odd)


def boundary(start, lengths_ref):
    position = start + lax.broadcasted_iota(jnp.int32, (Q, LANES), 0)
    seg = segment_at(position, lengths_ref)
    last = segment_at(jnp.full((1, LANES), start + Q - 1, jnp.int32), lengths_ref)
    before = segment_at(jnp.full((1, LANES), start - 1, jnp.int32), lengths_ref)
    before = jnp.where(start > 0, before, -1)
    return (seg == last), (seg == before), (last == before)


def softplus(values):
    return jnp.maximum(values, 0.0) + jnp.log1p(jnp.exp(-jnp.abs(values)))


def causal_taps(ext_ref, taps, bias, masks, columns):
    total = taps[3:4] * ext_ref[pl.ds(8, Q), columns]
    for shift in range(1, 4):
        total = total + taps[3 - shift : 4 - shift] * (ext_ref[pl.ds(8 - shift, Q), columns] * masks[shift - 1])
    return total + bias


def chunk_scalars(start, step_in, rate, lengths_ref, causal):
    step = softplus(step_in)
    log_decay = -step * jnp.exp(rate)
    cum = dot_nn(causal, log_decay, highest)
    return step, log_decay, cum


MESH = pl.DeviceIdType.MESH


def greet(groups, slots):
    group, slot = lax.axis_index("dp"), lax.axis_index("tensor")
    barrier = pltpu.get_barrier_semaphore()

    def along_dp(step, nothing):
        pl.semaphore_signal(barrier, inc=1, device_id=(lax.rem(group + step, groups), slot), device_id_type=MESH)
        return nothing

    lax.fori_loop(1, groups, along_dp, 0)
    for step in range(1, slots):
        pl.semaphore_signal(barrier, inc=1, device_id=(group, lax.rem(slot + step, slots)), device_id_type=MESH)
    pl.semaphore_wait(barrier, groups - 1 + slots - 1)


def head_kernel(
    send_run_ref, arrive_from_ref, lengths_ref, tokens, cotangent, wg_hbm, wv_hbm, ws_hbm, wt_hbm, wo_hbm,
    gain_ref, ggain_ref, tapv_ref, biasv_ref, taps_ref, biass_ref, stepb_ref, rate_ref, skip_ref,
    fulltok, fullcot, normed_out, dgate_out, dvalue_out, scaled_out, back_out, keep, out_part,
    dstate_ref, dstep_ref, inv_ref, dot_ref, sumv_ref, sums_ref, sumh_ref,
    wg, wv, ws, wt, wo, ptok, pcot, slots_buf, arr_tok, arr_cot, xbuf, nbuf, kbuf, gate_all, y_all,
    sraw_all, spre_all, stepin_all, states, d_carry, vext, dvext, sext, cum_cols, step_cols, cum_rows, neg_bias,
    scores, d_scores, d_entry, d_leave, acc_step, acc_cum, acc_dot, dsc, dgbuf, dvbuf, scbuf, bbuf, zbuf,
    sq_rows, ex_send, ex_recv, cols, masks, gathers,
    w_sem, in_sem, ts, tr, cs, cr, ags, agr, own_sem, x_sem, n_sem, keep_sem, o_sem, es, er,
):
    groups, slots = lax.axis_size("dp"), lax.axis_size("tensor")
    group, slot = lax.axis_index("dp"), lax.axis_index("tensor")
    runs, run, width = ptok.shape
    chunks = runs * run // Q
    per_chunk = Q // run
    pairs = d_carry.shape[0]
    last = slots - 1
    model = width * slots
    inner_total = wg.shape[1] * slots
    lane = lax.broadcasted_iota(jnp.int32, (Q, LANES), 1)
    first_half = lane < HEAD_DIM

    greet(groups, slots)
    weights = ((wg_hbm, wg), (wv_hbm, wv), (ws_hbm, ws), (wt_hbm, wt), (wo_hbm, wo))

    def weight_load(which):
        return pltpu.make_async_copy(weights[which][0], weights[which][1], w_sem.at[which])

    tok_in = pltpu.make_async_copy(tokens, ptok, in_sem.at[0])
    cot_in = pltpu.make_async_copy(cotangent, pcot, in_sem.at[1])
    tok_in.start()
    cot_in.start()
    for which in range(5):
        weight_load(which).start()

    def row_send(arrive, send_sem, recv_sem, step):
        other = lax.rem(group + step, groups)
        return pltpu.make_async_remote_copy(
            src_ref=slots_buf.at[other], dst_ref=arrive.at[group], send_sem=send_sem.at[other],
            recv_sem=recv_sem.at[group], device_id=(other, slot), device_id_type=MESH,
        )

    def send_rows(source, arrive, send_sem, recv_sem):
        def one(step, nothing):
            other = lax.rem(group + step, groups)
            slots_buf[other] = source[send_run_ref[other]]
            row_send(arrive, send_sem, recv_sem, step).start()
            return nothing

        lax.fori_loop(1, groups, one, 0)
        arrive[group] = source[send_run_ref[group]]

    def take_rows(packed, arrive, send_sem, recv_sem):
        def one(step, nothing):
            source = lax.rem(group + groups - step, groups)
            pltpu.make_async_remote_copy(
                src_ref=arrive.at[source], dst_ref=arrive.at[source], send_sem=send_sem.at[source],
                recv_sem=recv_sem.at[source], device_id=(group, slot), device_id_type=MESH,
            ).wait_recv()
            row_send(arrive, send_sem, recv_sem, step).wait_send()
            return nothing

        lax.fori_loop(1, groups, one, 0)
        for index in range(runs):
            packed[index] = arrive[arrive_from_ref[index]]

    def rows_of(packed, chunk):
        return packed.at[pl.ds(chunk * per_chunk, per_chunk)]

    def gather_push(kind, source, target, chunk, number, shard, to):
        return pltpu.make_async_remote_copy(
            src_ref=source, dst_ref=target.at[chunk, shard], send_sem=ags.at[kind, chunk, number],
            recv_sem=agr.at[kind, chunk, shard], device_id=(group, to), device_id_type=MESH,
        )

    gather_to = ((1, 2), (0, 2, 3), (3, 1, 0), (2, 1))

    def gather_direct(kind, packed, target, chunk, me):
        return [
            gather_push(kind, rows_of(packed, chunk), target, chunk, number, me, to)
            for number, to in enumerate(gather_to[me])
        ]

    def gather_forward(kind, target, chunk, me):
        shard, to = (3, 0) if me == 1 else (0, 3)
        return gather_push(kind, target.at[chunk, shard], target, chunk, 3, shard, to)

    def own_copy(kind, packed, target, chunk):
        return pltpu.make_async_copy(rows_of(packed, chunk), target.at[chunk, slot], own_sem.at[kind, chunk])

    def gather_start(kind, packed, target, chunk):
        own_copy(kind, packed, target, chunk).start()
        for me in range(slots):
            @pl.when(slot == me)
            def _(me=me):
                for copy in gather_direct(kind, packed, target, chunk, me):
                    copy.start()

    def gather_wait(kind, packed, target, chunk, hook=None):
        for me in range(slots):
            @pl.when(slot == me)
            def _(me=me):
                order = (3, 0, 2) if me == 1 else (0, 3, 1) if me == 2 else (1, 2, 3 - me)
                for position, shard in enumerate(order):
                    pltpu.make_async_remote_copy(
                        src_ref=target.at[chunk, shard], dst_ref=target.at[chunk, shard],
                        send_sem=ags.at[kind, chunk, 0], recv_sem=agr.at[kind, chunk, shard],
                        device_id=(group, slot), device_id_type=MESH,
                    ).wait_recv()
                    if position == 0 and me in (1, 2):
                        gather_forward(kind, target, chunk, me).start()
                    if position == 0 and hook is not None:
                        hook()
        own_copy(kind, packed, target, chunk).wait()

    def gather_drain(kind, packed, target):
        for chunk in range(chunks):
            for me in range(slots):
                @pl.when(slot == me)
                def _(me=me):
                    for copy in gather_direct(kind, packed, target, chunk, me):
                        copy.wait_send()
                    if me in (1, 2):
                        gather_forward(kind, target, chunk, me).wait_send()

    def keep_store(chunk, which):
        source = vext.at[pl.ds(8, Q)] if which == 0 else kbuf.at[1]
        return pltpu.make_async_copy(source, keep.at[chunk, which], keep_sem.at[which])

    def keep_load(chunk):
        return pltpu.make_async_copy(keep.at[chunk], kbuf, keep_sem.at[2])

    def normed_store(chunk):
        return pltpu.make_async_copy(nbuf, normed_out.at[chunk], n_sem)

    stores = ((dgbuf, dgate_out), (dvbuf, dvalue_out), (scbuf, scaled_out), (bbuf, back_out), (zbuf, out_part))

    def store(which, chunk):
        return pltpu.make_async_copy(stores[which][0], stores[which][1].at[chunk], o_sem.at[which])

    def x_load(source, chunk):
        return pltpu.make_async_copy(source.at[chunk], xbuf, x_sem)

    def ones_rows(values):
        return dot_nt(jnp.ones((8, LANES), f32), values, highest)

    def prepare(chunk, transposed):
        start = chunk * Q
        can_see = triangle(start, lengths_ref, transposed)
        neg_bias[...] = jnp.where(can_see, 0.0, -1e30)
        row = lax.broadcasted_iota(jnp.int32, (Q, Q), 0)
        col = lax.broadcasted_iota(jnp.int32, (Q, Q), 1)
        step_in = stepin_all[chunk]
        step, log_decay, cum = chunk_scalars(start, step_in, rate_ref[...], lengths_ref, (row >= col).astype(f32))
        cum_rows[...] = cum.T
        head_columns(cum, step, cum_cols, step_cols)
        return log_decay

    tok_in.wait()
    send_rows(ptok, arr_tok, ts, tr)
    states[0] = jnp.zeros_like(states[0])
    vext[pl.ds(0, 8)] = jnp.zeros((8, vext.shape[1]), f32)
    sext[pl.ds(0, 8)] = jnp.zeros((8, sext.shape[1]), f32)
    d_carry[...] = jnp.zeros_like(d_carry)
    dvext[pl.ds(Q, 8)] = jnp.zeros((8, dvext.shape[1]), f32)
    sumv_ref[...] = jnp.zeros_like(sumv_ref)
    sums_ref[...] = jnp.zeros_like(sums_ref)
    sumh_ref[...] = jnp.zeros_like(sumh_ref)
    place = lax.broadcasted_iota(jnp.int32, (2 * LANES, LANES), 1)
    source = lax.broadcasted_iota(jnp.int32, (2 * LANES, LANES), 0)
    source = (lax.rem(source, LANES) >= HEAD_DIM).astype(jnp.int32)
    for pair in range(pairs):
        gathers[pair] = (place == source + 2 * pair).astype(bf16)
    take_rows(ptok, arr_tok, ts, tr)
    gather_start(0, ptok, fulltok, 0)
    cot_in.wait()
    send_rows(pcot, arr_cot, cs, cr)
    for which in range(5):
        weight_load(which).wait()

    def forward_chunk(chunk, nothing):
        start = chunk * Q
        def second():
            @pl.when(chunk == 0)
            def _():
                gather_start(0, ptok, fulltok, 1)

        gather_wait(0, ptok, fulltok, chunk, second)
        x_load(fulltok, chunk).start()

        @pl.when(chunk + AHEAD < chunks)
        def _():
            gather_start(0, ptok, fulltok, chunk + AHEAD)

        @pl.when(chunk + AHEAD == chunks)
        def _():
            take_rows(pcot, arr_cot, cs, cr)

        @pl.when(chunk + AHEAD >= chunks)
        def _():
            gather_start(1, pcot, fullcot, 2 * chunks - 1 - AHEAD - chunk)

        @pl.when(chunk > 0)
        def _():
            normed_store(chunk - 1).wait()
            keep_store(chunk - 1, 0).wait()
            keep_store(chunk - 1, 1).wait()
            vext[pl.ds(0, 8)] = vext[pl.ds(Q, 8)]
            sext[pl.ds(0, 8)] = sext[pl.ds(Q, 8)]

        x_load(fulltok, chunk).wait()
        squares = jnp.zeros((Q, 1), f32)
        for shard in range(slots):
            wide = xbuf[shard].reshape(Q, width).astype(f32)
            squares = squares + jnp.sum(wide * wide, axis=1, keepdims=True)
        inv = lax.rsqrt(squares * (1.0 / model) + epsilon)
        inv_ref[pl.ds(start, Q)] = inv
        for shard in range(slots):
            wide = xbuf[shard].reshape(Q, width).astype(f32)
            columns = slice(shard * width, (shard + 1) * width)
            nbuf[:, columns] = (wide * inv * gain_ref[:, columns]).astype(bf16)
        normed_store(chunk).start()
        gate_all[chunk] = dot_nn(nbuf[...], wg[...])
        vext[pl.ds(8, Q)] = dot_nn(nbuf[...], wv[...])
        sext[pl.ds(8, Q)] = dot_nn(nbuf[...], ws[...])
        stepin_all[chunk] = dot_nn(nbuf[...], wt[...]) + stepb_ref[...]
        keep_store(chunk, 0).start()
        sraw_all[chunk] = sext[pl.ds(8, Q)]
        prepare(chunk, False)
        for shift in range(1, 4):
            masks[shift - 1] = tap_mask(start, shift, Q, lengths_ref)

        for half in range(2):
            columns = slice(half * LANES, (half + 1) * LANES)
            spre_all[chunk, :, columns] = causal_taps(
                sext, taps_ref[:, columns], biass_ref[:, columns], masks, columns
            )
        spre = spre_all[chunk]
        state_conv = spre * sigmoid(spre)
        entry = state_conv[:, :LANES]
        leave = state_conv[:, LANES:]
        scores[...] = dot_nt(leave, entry, highest)
        entry_t = entry.T.astype(bf16)
        leave_low = leave.astype(bf16)
        with_last, with_before, through = boundary(start, lengths_ref)
        to_last = with_last.astype(f32)
        from_before = with_before.astype(f32)
        passes = through.astype(f32)
        acc_dot[...] = jnp.zeros_like(acc_dot)

        def one_pair(pair, nothing):
            columns = pl.ds(pl.multiple_of(pair * LANES, LANES), LANES)
            pre = causal_taps(vext, tapv_ref[:, columns], biasv_ref[:, columns], masks, columns)
            kbuf[1, :, columns] = pre
            x = pre * sigmoid(pre)
            weighted = x * step_cols[pair]
            both = halves(weighted)
            results = []
            for half in range(2):
                head = 2 * pair + half
                c_col = cum_cols[head]
                c_row = cum_rows[pl.ds(head, 1), :]
                top = scores[:LANES, :LANES] * jnp.exp(c_col[:LANES] - c_row[:, :LANES] + neg_bias[:LANES, :LANES])
                low_left = scores[LANES:, :LANES] * jnp.exp(c_col[LANES:] - c_row[:, :LANES] + neg_bias[LANES:, :LANES])
                low_right = scores[LANES:, LANES:] * jnp.exp(
                    c_col[LANES:] - c_row[:, LANES:] + neg_bias[LANES:, LANES:]
                )
                upper = dot_nn(top.astype(bf16), both[:LANES])
                lower = dot_nn(jnp.concatenate([low_left, low_right], axis=1).astype(bf16), both)
                out = jnp.concatenate([upper, lower], axis=0)
                results.append(out[:, :LANES] + out[:, LANES:])
            inside = jnp.where(first_half, results[0], results[1])
            cum_pair = jnp.where(first_half, cum_cols[2 * pair], cum_cols[2 * pair + 1])
            cum_last = cum_pair[Q - 1 :]
            held = states[chunk, pair]
            carried = dot_halves(leave_low, held) * (jnp.exp(cum_pair) * from_before)
            y = inside + carried + skip_ref[:, columns] * x
            y_all[chunk, :, columns] = y
            to_end = jnp.exp(cum_last - cum_pair) * to_last
            states[chunk + 1, pair] = held * (jnp.exp(cum_last) * passes) + dot_halves(entry_t, to_end * weighted)
            gate = gate_all[chunk, :, columns]
            gated = y * (gate * sigmoid(gate))
            acc_dot[...] += gated * gated
            return nothing

        lax.fori_loop(0, pairs, one_pair, 0)
        keep_store(chunk, 1).start()
        sq_rows[chunk] = ones_rows(acc_dot[...])

        return nothing

    lax.fori_loop(0, chunks, forward_chunk, 0)
    normed_store(chunks - 1).wait()
    keep_store(chunks - 1, 0).wait()
    keep_store(chunks - 1, 1).wait()
    dsext = sext
    dsext[pl.ds(Q, 8)] = jnp.zeros((8, dsext.shape[1]), f32)

    def send_sums(chunk, step):
        return pltpu.make_async_remote_copy(
            src_ref=ex_send.at[chunk], dst_ref=ex_recv.at[chunk, slots - step], send_sem=es.at[chunk, step],
            recv_sem=er.at[chunk, slots - step], device_id=(group, lax.rem(slot + step, slots)), device_id_type=MESH,
        )

    def backward_chunk(index, nothing):
        chunk = chunks - 1 - index
        start = chunk * Q
        keep_load(chunk).start()
        gather_wait(1, pcot, fullcot, chunk)
        x_load(fullcot, chunk).start()

        @pl.when(chunk >= AHEAD)
        def _():
            gather_start(1, pcot, fullcot, chunk - AHEAD)

        x_load(fullcot, chunk).wait()
        for half in range(2):
            columns = slice(half * (dsc.shape[1] // 2), (half + 1) * (dsc.shape[1] // 2))
            value = dot_nn(xbuf[0].reshape(Q, width), wo[pl.ds(0, width), columns])
            for shard in range(1, slots):
                value = value + dot_nn(xbuf[shard].reshape(Q, width), wo[pl.ds(shard * width, width), columns])
            dsc[:, columns] = value
        acc_dot[...] = jnp.zeros_like(acc_dot)

        def product(pair, nothing):
            columns = pl.ds(pl.multiple_of(pair * LANES, LANES), LANES)
            gate = gate_all[chunk, :, columns]
            gated = y_all[chunk, :, columns] * (gate * sigmoid(gate))
            acc_dot[...] += dsc[:, columns] * ggain_ref[:, columns] * gated
            return nothing

        lax.fori_loop(0, pairs, product, 0)
        ex_send[chunk, pl.ds(0, 8)] = sq_rows[chunk]
        ex_send[chunk, pl.ds(8, 8)] = ones_rows(acc_dot[...])
        for step in range(1, slots):
            send_sums(chunk, step).start()

        @pl.when(index > 0)
        def _():
            dvext[pl.ds(Q, 8)] = dvext[pl.ds(0, 8)]
            dsext[pl.ds(Q, 8)] = dsext[pl.ds(0, 8)]
            for which in range(5):
                store(which, chunk + 1).wait()

        def later_mask(shift):
            position = start + lax.broadcasted_iota(jnp.int32, (Q, LANES), 0)
            same = segment_at(position, lengths_ref) == segment_at(position + shift, lengths_ref)
            return (same & (position + shift < chunks * Q)).astype(f32)

        log_decay = prepare(chunk, True)
        for shift in range(1, 4):
            masks[shift - 1] = later_mask(shift)
        step_in = stepin_all[chunk]
        spre = spre_all[chunk]
        spre_sig = sigmoid(spre)
        state_conv = spre * spre_sig
        entry = state_conv[:, :LANES]
        leave = state_conv[:, LANES:]
        scores[...] = dot_nt(entry, leave, highest)
        entry_low = entry.astype(bf16)
        leave_t = leave.T.astype(bf16)
        with_last, with_before, through = boundary(start, lengths_ref)
        to_last = with_last.astype(f32)
        from_before = with_before.astype(f32)
        passes = through.astype(f32)
        row_lane = lax.broadcasted_iota(jnp.int32, (Q, LANES), 0)
        for ref in (d_scores, d_entry, d_leave, acc_step, acc_cum, acc_dot):
            ref[...] = jnp.zeros_like(ref)

        sums = ex_send[chunk]
        for step in range(1, slots):
            send_sums(chunk, step).wait()
        for step in range(1, slots):
            sums = sums + ex_recv[chunk, step]
        rms_row = lax.rsqrt(sums[0:1] * (1.0 / inner_total) + epsilon)
        coef_row = rms_row * rms_row * rms_row * sums[8:9] * (1.0 / inner_total)
        cols[0] = jnp.broadcast_to(rms_row, (LANES, Q)).T
        cols[1] = jnp.broadcast_to(coef_row, (LANES, Q)).T
        keep_load(chunk).wait()

        def one_pair(pair, nothing):
            columns = pl.ds(pl.multiple_of(pair * LANES, LANES), LANES)
            rms = cols[0]
            pre = kbuf[1, :, columns]
            pre_sig = sigmoid(pre)
            x = pre * pre_sig
            step_pair = step_cols[pair]
            weighted = x * step_pair
            gate = gate_all[chunk, :, columns]
            gate_sig = sigmoid(gate)
            gate_silu = gate * gate_sig
            y = y_all[chunk, :, columns]
            gated = y * gate_silu
            d_scaled = dsc[:, columns]
            ggain = ggain_ref[:, columns]
            normalized = gated * rms
            scbuf[:, columns] = (normalized * ggain).astype(bf16)
            d_gated = rms * (d_scaled * ggain) - gated * cols[1]
            sumv_ref[pl.ds(0, 8), columns] += fold_rows(d_scaled * normalized)
            d_gate = (d_gated * y * (gate_sig + gate_silu * (1.0 - gate_sig))).astype(bf16)
            dgbuf[:, columns] = d_gate
            acc_dot[...] += d_gate.astype(f32) * gate
            d_y = d_gated * gate_silu
            skip = skip_ref[:, columns]
            sumv_ref[pl.ds(8, 8), columns] += fold_rows(d_y * x)
            y_scan = y - skip * x

            d_y_t = d_y.T.astype(bf16)
            d_y_both = halves(d_y)
            weighted_low = weighted.astype(bf16)
            results = []
            for half in range(2):
                head = 2 * pair + half
                own = jnp.where(first_half if half == 0 else ~first_half, weighted_low, jnp.zeros_like(weighted_low))
                d_m_top = dot_nn(own[:LANES], d_y_t)
                d_m_low = dot_nn(own[LANES:], d_y_t[:, LANES:])
                c_col = cum_cols[head]
                c_row = cum_rows[pl.ds(head, 1), :]
                l_top = jnp.exp(c_row - jnp.concatenate([c_col[:LANES]] * 2, axis=1) + neg_bias[:LANES])
                l_low = jnp.exp(c_row[:, LANES:] - c_col[LANES:] + neg_bias[LANES:, LANES:])
                d_scores[:LANES] += d_m_top * l_top
                d_scores[LANES:, LANES:] += d_m_low * l_low
                m_top = (scores[:LANES] * l_top).astype(bf16)
                m_low = (scores[LANES:, LANES:] * l_low).astype(bf16)
                upper = dot_nn(m_top, d_y_both)
                lower = dot_nn(m_low, d_y_both[LANES:])
                out = jnp.concatenate([upper, lower], axis=0)
                results.append(out[:, :LANES] + out[:, LANES:])
            d_weighted = jnp.where(first_half, results[0], results[1])
            cum_pair = jnp.where(first_half, cum_cols[2 * pair], cum_cols[2 * pair + 1])
            cum_last = cum_pair[Q - 1 :]
            to_end = jnp.exp(cum_last - cum_pair) * to_last
            from_start = jnp.exp(cum_pair) * from_before
            d_state = d_carry[pair]
            held = states[chunk, pair]
            d_weighted = d_weighted + dot_halves(entry_low, d_state) * to_end
            d_entry[...] += dot_nt((to_end * weighted).astype(bf16), d_state.astype(bf16))
            moved = from_start * d_y
            d_leave[...] += dot_nt(moved.astype(bf16), held.astype(bf16))
            state_dot = jnp.sum(states[chunk + 1, pair] * d_state, axis=0, keepdims=True)
            d_carry[pair] = d_state * (jnp.exp(cum_last) * passes) + dot_halves(leave_t, moved)

            to_step = d_weighted * x
            to_cum = d_y * y_scan - to_step * step_pair + jnp.where(row_lane == Q - 1, state_dot, 0.0)
            acc_step[...] += dot_nn(halves(to_step), gathers[pair])
            acc_cum[...] += dot_nn(halves(to_cum), gathers[pair])

            d_x = d_weighted * step_pair + skip * d_y
            d_pre = d_x * (pre_sig + x * (1.0 - pre_sig))
            dvext[pl.ds(0, Q), columns] = d_pre
            sumv_ref[pl.ds(16, 8), columns] += fold_rows(d_pre)
            vraw = kbuf[0, :, columns]
            total = tapv_ref[3:4, columns] * d_pre
            sumv_ref[pl.ds(24, 8), columns] += fold_rows(vraw * d_pre)
            for shift in range(1, 4):
                moved_back = dvext[pl.ds(shift, Q), columns] * masks[shift - 1]
                total = total + tapv_ref[3 - shift : 4 - shift, columns] * moved_back
                sumv_ref[pl.ds(24 + 8 * shift, 8), columns] += fold_rows(vraw * moved_back)
            d_value = total.astype(bf16)
            dvbuf[:, columns] = d_value
            acc_dot[...] += d_value.astype(f32) * vraw
            return nothing

        lax.fori_loop(0, pairs, one_pair, 0)
        for which in range(3):
            store(which, chunk).start()

        can_see = (neg_bias[...] == 0.0).astype(f32)
        d_log = dot_nn(can_see, acc_cum[...], highest)
        rate = jnp.exp(rate_ref[...])
        d_step_in = (acc_step[...] - d_log * rate) * sigmoid(step_in)
        d_step = d_step_in.astype(bf16)
        dstep_ref[pl.ds(start, Q)] = d_step
        step_raw = step_in - stepb_ref[...]
        acc_dot[...] += jnp.where(lane < 2 * pairs, d_step.astype(f32) * step_raw, 0.0)
        sumh_ref[pl.ds(0, 8)] += fold_rows(d_step_in)
        sumh_ref[pl.ds(8, 8)] += fold_rows(d_log * log_decay)

        d_scores_now = d_scores[...]
        d_b = d_entry[...] + dot_halves(d_scores_now.astype(bf16), leave)
        d_c = d_leave[...] + dot_halves(d_scores_now.T.astype(bf16), entry)
        for half, grad in enumerate((d_b, d_c)):
            columns = slice(half * LANES, (half + 1) * LANES)
            part = spre_sig[:, columns]
            d_pre = grad * (part + state_conv[:, columns] * (1.0 - part))
            dsext[pl.ds(0, Q), columns] = d_pre
            sums_ref[pl.ds(0, 8), columns] += fold_rows(d_pre)
            sraw = sraw_all[chunk, :, columns]
            total = taps_ref[3:4, columns] * d_pre
            sums_ref[pl.ds(8, 8), columns] += fold_rows(sraw * d_pre)
            for shift in range(1, 4):
                moved_back = dsext[pl.ds(shift, Q), columns] * masks[shift - 1]
                total = total + taps_ref[3 - shift : 4 - shift, columns] * moved_back
                sums_ref[pl.ds(8 + 8 * shift, 8), columns] += fold_rows(sraw * moved_back)
            d_state_raw = total.astype(bf16)
            dstate_ref[pl.ds(start, Q), columns] = d_state_raw
            acc_dot[...] += d_state_raw.astype(f32) * sraw
        dot_ref[chunk] = ones_rows(acc_dot[...])

        for shard in range(slots):
            here = pl.ds(shard * width, width)
            part = dot_nt(dgbuf[...], wg[here]) + dot_nt(dvbuf[...], wv[here])
            part = part + dot_nt(dstate_ref[pl.ds(start, Q)], ws[here]) + dot_nt(d_step, wt[here])
            bbuf[:, shard * width : (shard + 1) * width] = part.astype(bf16)
        store(3, chunk).start()
        for shard in range(slots):
            part = dot_nt(scbuf[...], wo[pl.ds(shard * width, width)])
            zbuf[:, shard * width : (shard + 1) * width] = part.astype(bf16)
        store(4, chunk).start()
        return nothing

    lax.fori_loop(0, chunks, backward_chunk, 0)
    for which in range(5):
        store(which, 0).wait()
    gather_drain(0, ptok, fulltok)
    gather_drain(1, pcot, fullcot)


def head(send_run, arrive_from, lengths, tokens, cotangent, wg, wv, ws, wt, wo, small):
    groups, slots = lax.axis_size("dp"), lax.axis_size("tensor")
    runs, run, width = tokens.shape
    rows = runs * run
    chunks, per_chunk = rows // Q, Q // run
    model, inner = wg.shape
    pairs = inner // LANES
    vmem, anywhere, smem = (pl.BlockSpec(memory_space=s) for s in (pltpu.VMEM, pl.ANY, pltpu.SMEM))
    dma = pltpu.SemaphoreType.DMA
    shape = jax.ShapeDtypeStruct
    return pl.pallas_call(
        head_kernel,
        out_shape=[
            shape((chunks, slots, per_chunk, run, width), bf16),
            shape((chunks, slots, per_chunk, run, width), bf16),
            shape((chunks, Q, model), bf16),
            shape((chunks, Q, inner), bf16),
            shape((chunks, Q, inner), bf16),
            shape((chunks, Q, inner), bf16),
            shape((chunks, Q, model), bf16),
            shape((chunks, 2, Q, inner), f32),
            shape((chunks, Q, model), bf16),
            shape((rows, 2 * LANES), bf16),
            shape((rows, LANES), bf16),
            shape((rows, 1), f32),
            shape((chunks, 8, Q), f32),
            shape((56, inner), f32),
            shape((40, 2 * LANES), f32),
            shape((16, LANES), f32),
        ],
        in_specs=[smem] * 3 + [anywhere] * 7 + [vmem] * len(small),
        out_specs=[anywhere] * 9 + [vmem] * 7,
        scratch_shapes=[
            pltpu.VMEM(wg.shape, bf16), pltpu.VMEM(wv.shape, bf16), pltpu.VMEM(ws.shape, bf16),
            pltpu.VMEM(wt.shape, bf16), pltpu.VMEM(wo.shape, bf16),
            pltpu.VMEM((runs, run, width), bf16),
            pltpu.VMEM((runs, run, width), bf16),
            pltpu.VMEM((groups, run, width), bf16),
            pltpu.VMEM((groups, run, width), bf16),
            pltpu.VMEM((groups, run, width), bf16),
            pltpu.VMEM((slots, per_chunk, run, width), bf16),
            pltpu.VMEM((Q, model), bf16),
            pltpu.VMEM((2, Q, inner), f32),
            pltpu.VMEM((chunks, Q, inner), f32),
            pltpu.VMEM((chunks, Q, inner), f32),
            pltpu.VMEM((chunks, Q, 2 * LANES), f32),
            pltpu.VMEM((chunks, Q, 2 * LANES), f32),
            pltpu.VMEM((chunks, Q, LANES), f32),
            pltpu.VMEM((chunks + 1, pairs, LANES, LANES), f32),
            pltpu.VMEM((pairs, LANES, LANES), f32),
            pltpu.VMEM((Q + 8, inner), f32),
            pltpu.VMEM((Q + 8, inner), f32),
            pltpu.VMEM((Q + 8, 2 * LANES), f32),
            pltpu.VMEM((2 * pairs, Q, LANES), f32),
            pltpu.VMEM((pairs, Q, LANES), f32),
            pltpu.VMEM((LANES, Q), f32),
            pltpu.VMEM((Q, Q), f32),
            pltpu.VMEM((Q, Q), f32),
            pltpu.VMEM((Q, Q), f32),
            pltpu.VMEM((Q, LANES), f32),
            pltpu.VMEM((Q, LANES), f32),
            pltpu.VMEM((Q, LANES), f32),
            pltpu.VMEM((Q, LANES), f32),
            pltpu.VMEM((Q, LANES), f32),
            pltpu.VMEM((Q, inner), f32),
            pltpu.VMEM((Q, inner), bf16),
            pltpu.VMEM((Q, inner), bf16),
            pltpu.VMEM((Q, inner), bf16),
            pltpu.VMEM((Q, model), bf16),
            pltpu.VMEM((Q, model), bf16),
            pltpu.VMEM((chunks, 8, Q), f32),
            pltpu.VMEM((chunks, 16, Q), f32),
            pltpu.VMEM((chunks, slots, 16, Q), f32),
            pltpu.VMEM((2, Q, LANES), f32),
            pltpu.VMEM((3, Q, LANES), f32),
            pltpu.VMEM((pairs, 2 * LANES, LANES), bf16),
            dma((5,)), dma((2,)), dma((groups,)), dma((groups,)), dma((groups,)), dma((groups,)),
            dma((2, chunks, 4)), dma((2, chunks, slots)), dma((2, chunks)), dma, dma, dma((3,)), dma((5,)),
            dma((chunks, slots)), dma((chunks, slots)),
        ],
        compiler_params=pltpu.CompilerParams(collective_id=2, has_side_effects=True, vmem_limit_bytes=HEAD_VMEM),
        name="head",
    )(send_run, arrive_from, lengths, tokens, cotangent, wg, wv, ws, wt, wo, *small)


def tail_kernel(
    back_run_ref, return_from_ref, out_part, back_part, normed, tokens, cotangent, scaled, d_gate, d_value,
    row_dot_ref, inv_ref, gain_ref, small_ref, small_z_ref,
    layer_ref, tgrad_ref, small_out, ngain_out, share0, share1, share2,
    z_recv, z_comb, z_own, z_mix, ptok, pcot, rd_recv, rd_col, row_buf, slots_buf, arrive, left, right, full,
    core_recv, chip_recv, total, sz_recv, small_all, small_recv, ngain_all, ngain_recv,
    load_sem, mix_sem, left_sem, right_sem, zs, zr, zc, rds, rdr, szs, szr, sms, smr, ngs, ngr, rs, rr, cs, cr, hs, hr,
):
    groups, slots = lax.axis_size("dp"), lax.axis_size("tensor")
    group, slot = lax.axis_index("dp"), lax.axis_index("tensor")
    jobs = z_recv.shape[0]
    pieces = jobs // 2
    runs, run, width = layer_ref.shape
    rows = runs * run
    piece_run = run // pieces
    chips = groups // 2
    core = lax.rem(group, 2)
    chip = group // 2
    grow = share0.shape[0]
    per_block = 256 // grow
    blocks = full.shape[1] // per_block
    inner = share0.shape[1]
    last = slots - 1

    greet(groups, slots)

    def z_small(source, target, send_sem, recv_sem, step):
        return pltpu.make_async_remote_copy(
            src_ref=source, dst_ref=target.at[slots - step], send_sem=send_sem.at[step],
            recv_sem=recv_sem.at[slots - step], device_id=(group, lax.rem(slot + step, slots)), device_id_type=MESH,
        )

    def send_dot(step):
        return z_small(row_dot_ref, rd_recv, rds, rdr, step)

    def send_state(step):
        return z_small(small_z_ref, sz_recv, szs, szr, step)

    for step in range(1, slots):
        send_state(step).start()
        send_dot(step).start()

    def piece_of(job, shard):
        source = out_part if job < pieces else back_part
        return source.at[:, pl.ds((job % pieces) * piece_run, piece_run), pl.ds(shard * width, width)]

    def landing(job, me, to):
        return z_recv.at[job, me if me < to else me - 1], zr.at[job, me if me < to else me - 1]

    def z_push(job, number, shard, to, source, target, sem):
        return pltpu.make_async_remote_copy(
            src_ref=source, dst_ref=target, send_sem=zs.at[job, number], recv_sem=sem, device_id=(group, to),
            device_id_type=MESH,
        )

    def direct(job, me):
        def push(number, to):
            return z_push(job, number, to, to, piece_of(job, to), *landing(job, me, to))

        def to_mix(number, shard, to):
            return z_push(job, number, shard, to, piece_of(job, shard), z_comb.at[job], zc.at[job])

        if me == 0:
            return [to_mix(0, 3, 1), push(1, 2), push(2, 1)]
        if me == last:
            return [to_mix(0, 0, 2), push(1, 1), push(2, 2)]
        return [push(0, 0), push(1, 2)] if me == 1 else [push(0, 3), push(1, 1)]

    def mixed(job, me):
        to = 3 if me == 1 else 0
        return z_push(job, 2, to, to, z_mix.at[job], *landing(job, me, to))

    def own_load(kind):
        source = back_part if kind else out_part
        return pltpu.make_async_copy(source.at[:, :, pl.ds(slot * width, width)], z_own.at[kind], load_sem.at[kind])

    def mix_load(job, me):
        return pltpu.make_async_copy(piece_of(job, 3 if me == 1 else 0), z_mix.at[job], mix_sem.at[job])

    def shard_load(which):
        source, target = ((tokens, ptok), (cotangent, pcot))[which]
        return pltpu.make_async_copy(source.at[:, slot], target, load_sem.at[2 + which])

    def push(job):
        for me in range(slots):
            @pl.when(slot == me)
            def _(me=me):
                for copy in direct(job, me):
                    copy.start()

    def combine(job):
        for me in (1, 2):
            @pl.when(slot == me)
            def _(me=me):
                mix_load(job, me).wait()
                z_push(job, 2, 0, 0, z_comb.at[job], z_comb.at[job], zc.at[job]).wait_recv()
                both = z_mix[job].astype(f32) + z_comb[job].astype(f32)
                z_mix[job] = both.astype(bf16)
                mixed(job, me).start()

    rights = (scaled, d_gate, d_value)
    shares = (share0, share1, share2)

    def right_load(which):
        return pltpu.make_async_copy(rights[which], right.at[which % 2], right_sem.at[which])

    def left_load(which, block, place):
        if which == 0:
            per_shard = width // 256
            columns = pl.ds(pl.multiple_of(lax.rem(block, per_shard) * 256, 256), 256)
            source = cotangent.at[:, block // per_shard, :, :, columns]
        else:
            source = normed.at[:, :, :, pl.ds(pl.multiple_of(block * 256, 256), 256)]
        return pltpu.make_async_copy(source, left.at[place], left_sem.at[place])

    def grad_blocks(which, begin, end):
        def one(block, nothing):
            place = lax.rem(block, 2)

            @pl.when(block + 1 < blocks)
            def _():
                left_load(which, block + 1, 1 - place).start()

            left_load(which, block, place).wait()
            value = lax.dot_general(
                left[place].reshape(rows, 256), right[which % 2], (((0,), (0,)), ((), ())), preferred_element_type=f32
            )
            full[which % 2, pl.ds(block * per_block, per_block)] = value.reshape(per_block, grow, -1).astype(bf16)
            return nothing

        lax.fori_loop(begin, end, one, 0)

    partner = group + 1 - 2 * core

    def core_send(which):
        theirs = full.at[which % 2].reshape(chips, 2, grow, inner).at[:, 1 - core]
        return pltpu.make_async_remote_copy(
            src_ref=theirs, dst_ref=core_recv.at[which], send_sem=cs.at[which], recv_sem=cr.at[which],
            device_id=(partner, slot), device_id_type=MESH,
        )

    def chip_send(which, step):
        other = lax.rem(chip + step, chips)
        return pltpu.make_async_remote_copy(
            src_ref=full.at[which % 2, 2 * other + core], dst_ref=chip_recv.at[which, chips - step],
            send_sem=hs.at[which, step], recv_sem=hr.at[which, chips - step], device_id=(2 * other + core, slot),
            device_id_type=MESH,
        )

    def chip_pushes(which):
        core_send(which).wait()

        def one(step, nothing):
            other = lax.rem(chip + step, chips)
            mine = 2 * other + core
            both = full[which % 2, mine].astype(f32) + core_recv[which, other].astype(f32)
            full[which % 2, mine] = both.astype(bf16)
            chip_send(which, step).start()
            return nothing

        lax.fori_loop(1, chips, one, 0)
        shares[which][...] = full[which % 2, group].astype(f32) + core_recv[which, chip].astype(f32)

    def chip_drain(which):
        def drain(step, nothing):
            chip_send(which, step).wait_send()
            return nothing

        lax.fori_loop(1, chips, drain, 0)

    def chip_total(which):
        def one(step, nothing):
            pltpu.make_async_remote_copy(
                src_ref=chip_recv.at[which, step], dst_ref=chip_recv.at[which, step], send_sem=hs.at[which, step],
                recv_sem=hr.at[which, step], device_id=(group, slot), device_id_type=MESH,
            ).wait_recv()
            shares[which][...] += chip_recv[which, step].astype(f32)
            return nothing

        lax.fori_loop(1, chips, one, 0)

    def dp_small(source, target, send_sem, recv_sem, step):
        return pltpu.make_async_remote_copy(
            src_ref=source, dst_ref=target.at[groups - step], send_sem=send_sem.at[step],
            recv_sem=recv_sem.at[groups - step], device_id=(lax.rem(group + step, groups), slot), device_id_type=MESH,
        )

    def dp_small_start(source, target, send_sem, recv_sem):
        def one(step, nothing):
            dp_small(source, target, send_sem, recv_sem, step).start()
            return nothing

        lax.fori_loop(1, groups, one, 0)

    def dp_small_finish(source, target, send_sem, recv_sem, result):
        result[...] = source[...]

        def one(step, nothing):
            pltpu.make_async_remote_copy(
                src_ref=target.at[step], dst_ref=target.at[step], send_sem=send_sem.at[step],
                recv_sem=recv_sem.at[step], device_id=(group, slot), device_id_type=MESH,
            ).wait_recv()
            result[...] += target[step]
            return nothing

        lax.fori_loop(1, groups, one, 0)

        def drain(step, nothing):
            dp_small(source, target, send_sem, recv_sem, step).wait_send()
            return nothing

        lax.fori_loop(1, groups, drain, 0)

    def row_send(job, step):
        other = lax.rem(group + step, groups)
        return pltpu.make_async_remote_copy(
            src_ref=slots_buf.at[job, other], dst_ref=arrive.at[job, group], send_sem=rs.at[job, other],
            recv_sem=rr.at[job, group], device_id=(other, slot), device_id_type=MESH,
        )

    def finish(job):
        kind, piece = job // pieces, job % pieces
        here = pl.ds(piece * piece_run, piece_run)
        tall = runs * piece_run
        for me in range(slots):
            @pl.when(slot == me)
            def _(me=me):
                acc = z_own[kind, :, here, :].astype(f32)
                for source in ((1, 2) if me in (0, 3) else tuple(s for s in range(slots) if s != me)):
                    place, sem = landing(job, source, me)
                    z_push(job, 0, 0, 0, place, place, sem).wait_recv()
                    acc = acc + place[...].astype(f32)
                total[...] = acc
        summed = total[...].reshape(tall, width)
        kept = ptok[:, :, here, :].reshape(tall, width).astype(f32)
        if kind == 0:
            result = kept + summed
        else:
            inv = inv_ref[:, here, :].reshape(tall, 1)
            unit = kept * inv
            ngain_all[...] += fold_rows(summed * unit)
            dot_cols = rd_col[:, here, :].reshape(tall, LANES)
            dot_cols = jnp.concatenate([dot_cols] * (width // LANES), axis=1)
            cot = pcot[:, :, here, :].reshape(tall, width).astype(f32)
            result = cot + inv * (summed * gain_ref[...] - unit * dot_cols)
        row_buf[...] = result.astype(bf16).reshape(runs, piece_run, width)

        def fill(step, nothing):
            other = lax.rem(group + step, groups)
            slots_buf[job, other] = row_buf[back_run_ref[other]]
            row_send(job, step).start()
            return nothing

        lax.fori_loop(1, groups, fill, 0)
        arrive[job, group] = row_buf[back_run_ref[group]]

    def rows_wait(kind):
        for job in range(kind * pieces, (kind + 1) * pieces):
            def one(step, nothing, job=job):
                source = lax.rem(group + groups - step, groups)
                pltpu.make_async_remote_copy(
                    src_ref=arrive.at[job, source], dst_ref=arrive.at[job, source], send_sem=rs.at[job, source],
                    recv_sem=rr.at[job, source], device_id=(group, slot), device_id_type=MESH,
                ).wait_recv()
                row_send(job, step).wait_send()
                return nothing

            lax.fori_loop(1, groups, one, 0)

    def rows_take(kind, target):
        for piece in range(pieces):
            for index in range(runs):
                target[index, pl.ds(piece * piece_run, piece_run)] = arrive[kind * pieces + piece, return_from_ref[index]]

    z_groups = []
    for job in range(jobs):
        group_steps = [(combine, job)]
        if job + IN_FLIGHT < jobs:
            group_steps.append((push, job + IN_FLIGHT))
        if job > 0:
            group_steps.append((finish, job - 1))
        z_groups.append(group_steps)
    z_groups.append([(finish, jobs - 1)])

    def z_work():
        if z_groups:
            for step, job in z_groups.pop(0):
                step(job)

    for job in range(min(IN_FLIGHT, jobs)):
        push(job)
    own_load(0).start()
    own_load(1).start()
    shard_load(0).start()
    shard_load(1).start()
    for me in (1, 2):
        @pl.when(slot == me)
        def _(me=me):
            for job in range(jobs):
                mix_load(job, me).start()
    right_load(0).start()
    left_load(0, 0, 0).start()
    right_load(1).start()
    ngain_all[...] = jnp.zeros_like(ngain_all)

    half = blocks // 2
    right_load(0).wait()
    grad_blocks(0, 0, half)
    small_z = small_z_ref[...]
    for step in range(1, slots):
        send_state(step).wait()
    for step in range(1, slots):
        small_z = small_z + sz_recv[step]
    small_all[:, pl.ds(0, inner)] = small_ref[...]
    small_all[:, pl.ds(inner, 2 * LANES)] = small_z
    dp_small_start(small_all, small_recv, sms, smr)
    grad_blocks(0, half, blocks)
    core_send(0).start()
    right_load(2).start()
    for kind in range(2):
        own_load(kind).wait()
        shard_load(kind).wait()
    left_load(1, 0, 0).start()
    z_work()
    right_load(1).wait()
    grad_blocks(1, 0, half)
    chip_pushes(0)
    grad_blocks(1, half, blocks)
    core_send(1).start()
    left_load(2, 0, 0).start()
    rd_total = row_dot_ref[...]
    for step in range(1, slots):
        send_dot(step).wait()
    for step in range(1, slots):
        rd_total = rd_total + rd_recv[step]
    rd_total = rd_total * (1.0 / (width * slots))
    for block in range(rows // 256):
        piece_row = jnp.broadcast_to(rd_total[0:1, block * 256 : (block + 1) * 256], (LANES, 256))
        count = 256 // run
        rd_col[pl.ds(block * count, count)] = piece_row.T.reshape(count, run, LANES)
    z_work()
    right_load(2).wait()
    chip_drain(0)
    grad_blocks(2, 0, half)
    chip_pushes(1)
    z_work()
    grad_blocks(2, half, blocks)
    core_send(2).start()
    z_work()
    chip_pushes(2)
    while z_groups:
        z_work()
    dp_small_start(ngain_all, ngain_recv, ngs, ngr)

    rows_wait(0)
    rows_wait(1)
    rows_take(0, layer_ref)
    rows_take(1, tgrad_ref)
    dp_small_finish(small_all, small_recv, sms, smr, small_out)
    for which in range(3):
        chip_total(which)
    chip_drain(1)
    chip_drain(2)
    dp_small_finish(ngain_all, ngain_recv, ngs, ngr, ngain_out)
    for me in range(slots):
        @pl.when(slot == me)
        def _(me=me):
            for job in range(jobs):
                for copy in direct(job, me):
                    copy.wait_send()
                if me in (1, 2):
                    mixed(job, me).wait_send()


def tail(back_run, return_from, out_part, back_part, normed, tokens, cotangent, scaled, d_gate, d_value, row_dot, inv,
         gain, small, small_z):
    groups, slots = lax.axis_size("dp"), lax.axis_size("tensor")
    runs, run, model = out_part.shape
    width = model // slots
    rows = runs * run
    inner = scaled.shape[1]
    pieces = min(4, run // 16)
    jobs = 2 * pieces
    piece_run = run // pieces
    grow = model // groups
    chips = groups // 2
    vmem, anywhere, smem = (pl.BlockSpec(memory_space=s) for s in (pltpu.VMEM, pl.ANY, pltpu.SMEM))
    dma = pltpu.SemaphoreType.DMA
    shape = jax.ShapeDtypeStruct
    by_chunk = tokens.shape[:1] + tokens.shape[2:]
    part = (runs, piece_run, width)
    return pl.pallas_call(
        tail_kernel,
        out_shape=[
            shape((runs, run, width), bf16), shape((runs, run, width), bf16), shape((8, inner + 2 * LANES), f32),
            shape((8, width), f32),
        ] + [shape((grow, inner), f32)] * 3,
        in_specs=[smem] * 2 + [anywhere] * 8 + [vmem] * 5,
        out_specs=[vmem] * 7,
        scratch_shapes=[
            pltpu.VMEM((jobs, slots - 1) + part, bf16),
            pltpu.VMEM((jobs,) + part, bf16),
            pltpu.VMEM((2, runs, run, width), bf16),
            pltpu.VMEM((jobs,) + part, bf16),
            pltpu.VMEM(by_chunk, bf16),
            pltpu.VMEM(by_chunk, bf16),
            pltpu.VMEM((slots, 8, rows), f32),
            pltpu.VMEM((runs, run, LANES), f32),
            pltpu.VMEM(part, bf16),
            pltpu.VMEM((jobs, groups, piece_run, width), bf16),
            pltpu.VMEM((jobs, groups, piece_run, width), bf16),
            pltpu.VMEM((2,) + by_chunk[:-1] + (256,), bf16),
            pltpu.VMEM((2, rows, inner), bf16),
            pltpu.VMEM((2, groups, grow, inner), bf16),
            pltpu.VMEM((3, chips, grow, inner), bf16),
            pltpu.VMEM((3, chips, grow, inner), bf16),
            pltpu.VMEM(part, f32),
            pltpu.VMEM((slots, 8, 2 * LANES), f32),
            pltpu.VMEM((8, inner + 2 * LANES), f32),
            pltpu.VMEM((groups, 8, inner + 2 * LANES), f32),
            pltpu.VMEM((8, width), f32),
            pltpu.VMEM((groups, 8, width), f32),
            dma((4,)), dma((jobs,)), dma((2,)), dma((3,)),
            dma((jobs, 3)), dma((jobs, slots - 1)), dma((jobs,)),
            dma((slots,)), dma((slots,)), dma((slots,)), dma((slots,)),
            dma((groups,)), dma((groups,)), dma((groups,)), dma((groups,)),
            dma((jobs, groups)), dma((jobs, groups)),
            dma((3,)), dma((3,)), dma((3, chips)), dma((3, chips)),
        ],
        compiler_params=pltpu.CompilerParams(collective_id=3, has_side_effects=True, vmem_limit_bytes=64 << 20),
        name="tail",
    )(back_run, return_from, out_part, back_part, normed, tokens, cotangent, scaled, d_gate, d_value, row_dot, inv, gain,
      small, small_z)


def contract_rows(left, right):
    return lax.dot_general(left, right, (((0,), (0,)), ((), ())), preferred_element_type=f32)


def pad_heads(values):
    return jnp.pad(values, ((0, 0), (0, LANES - values.shape[1])))


def unfold(sums, index):
    return jnp.sum(sums[8 * index : 8 * index + 8], axis=0)


def per_device(
    tokens, cotangent, norm_gain, gate_proj, value_proj, state_proj, step_proj, conv_value, conv_value_bias,
    conv_state, conv_state_bias, step_bias, decay_log, skip_gain, gate_gain, out_proj, token_order, lengths,
):
    groups = lax.axis_size("dp")
    group = lax.axis_index("dp")
    slots = lax.axis_size("tensor")
    slot = lax.axis_index("tensor")
    rows, width = tokens.shape
    model = width * slots
    inner = gate_proj.shape[1]
    heads = step_bias.shape[0]
    run = 2 * rows // groups
    runs = rows // run

    source_run = token_order.reshape(groups, runs, run)[:, :, 0] // run
    source_group = source_run // runs
    from_here = source_group == group
    send_run = jnp.sum(jnp.where(from_here, source_run % runs, 0), axis=1)
    arrive_from = lax.dynamic_index_in_dim(source_group, group, 0, keepdims=False)
    every = jnp.arange(groups, dtype=jnp.int32)
    back_run = jnp.sum(
        jnp.where(arrive_from[None, :] == every[:, None], jnp.arange(runs, dtype=jnp.int32)[None, :], 0), axis=1
    )
    local_run = group * runs + jnp.arange(runs, dtype=jnp.int32)
    return_from = jnp.sum(
        jnp.where(source_run[None] == local_run[:, None, None], every[None, :, None], 0), axis=(1, 2)
    )

    def cut(values):
        return values.reshape(runs, run, values.shape[1])

    gain_full = norm_gain.astype(f32)
    small = (
        gain_full[None], gate_gain.astype(f32)[None], conv_value.astype(f32), conv_value_bias.astype(f32)[None],
        conv_state.astype(f32), conv_state_bias.astype(f32)[None], pad_heads(step_bias[None]),
        pad_heads(decay_log[None]), jnp.repeat(skip_gain, HEAD_DIM)[None],
    )
    (full_tokens, full_cotangent, normed, d_gate, d_value, scaled, back_partial, _, out_partial, d_state, d_step,
     inv_rms, row_dot, sumv, sums, sumh) = head(
        send_run, arrive_from, lengths, cut(tokens), cut(cotangent), gate_proj, value_proj, state_proj,
        pad_heads(step_proj), out_proj, small,
    )
    row_dot = row_dot.transpose(1, 0, 2).reshape(8, rows)
    normed_cut = normed.reshape(full_tokens.shape[0], full_tokens.shape[2], run, model)
    normed, d_gate, d_value, scaled, back_partial, out_partial = (
        v.reshape(rows, v.shape[2]) for v in (normed, d_gate, d_value, scaled, back_partial, out_partial)
    )
    state_grad = contract_rows(normed, d_state)
    step_grad = contract_rows(normed, d_step[:, :heads])
    gain_share = lax.dynamic_slice_in_dim(gain_full, slot * width, width, 0)
    by_head = jnp.pad(sumh.reshape(2, 8, LANES).sum(1).reshape(1, 2 * LANES), ((0, 0), (0, inner - 2 * LANES)))
    small = jnp.concatenate([sumv.reshape(7, 8, inner).sum(1), by_head])
    small_z = jnp.pad(sums.reshape(5, 8, 2 * LANES).sum(1), ((0, 3), (0, 0)))
    layer_output, tokens_grad, small, norm_gain_rows, out_grad_share, gate_share, value_share = tail(
        back_run, return_from, cut(out_partial), cut(back_partial), normed_cut, full_tokens, full_cotangent, scaled,
        d_gate, d_value, row_dot, cut(inv_rms), gain_share[None], small, small_z,
    )
    state_sums = small[:, inner:]

    def share(grad):
        return lax.psum_scatter(grad, "dp", scatter_dimension=0, tiled=True)

    step_share = share(step_grad)
    state_share = lax.psum_scatter(state_grad, ("dp", "tensor"), scatter_dimension=0, tiled=True)
    return (
        layer_output.reshape(rows, width),
        tokens_grad.reshape(rows, width),
        jnp.sum(norm_gain_rows, axis=0),
        gate_share,
        value_share,
        state_share,
        step_share,
        small[6:2:-1, :inner],
        small[2, :inner],
        state_sums[4:0:-1],
        state_sums[0],
        small[7, :heads],
        small[7, LANES : LANES + heads],
        jnp.sum(small[1, :inner].reshape(heads, HEAD_DIM), axis=1),
        small[0, :inner],
        out_grad_share,
    )


def solution(mesh):
    across = P(None, "tensor")
    both = P("dp", "tensor")
    heads = P("tensor")
    return jax.shard_map(
        per_device,
        mesh=mesh,
        in_specs=(
            both, both, P(), across, across, P(), across, across, heads, P(), P(), heads, heads, heads, heads, across,
            P(), P("dp", None),
        ),
        out_specs=(
            both, both, heads, both, both, P(("dp", "tensor"), None), both, across, heads, P(), P(), heads, heads, heads,
            heads, both,
        ),
        check_vma=False,
    )
```

```python
import jax
import jax.numpy as jnp
from jax import lax
from jax.experimental import pallas as pl
from jax.experimental.pallas import tpu as pltpu
from jax.sharding import PartitionSpec as P

f32 = jnp.float32
bf16 = jnp.bfloat16
Q = 256
LANES = 128
HEAD_DIM = 64
AHEAD = 2
WINDOW = 2
EARLY = 5
HEAD_VMEM = 64 << 20
highest = lax.Precision.HIGHEST
epsilon = 1e-05


def dot_nn(a, b, precision=None):
    return lax.dot_general(a, b, (((1,), (0,)), ((), ())), precision=precision, preferred_element_type=f32)


def dot_nt(a, b, precision=None):
    return lax.dot_general(a, b, (((1,), (1,)), ((), ())), precision=precision, preferred_element_type=f32)


def halves(values):
    high = values.astype(bf16)
    return jnp.concatenate([high, (values - high.astype(f32)).astype(bf16)], axis=1)


def dot_halves(a, values):
    both = dot_nn(a, halves(values))
    return both[:, :LANES] + both[:, LANES:]


def sigmoid(values):
    return 0.5 * jnp.tanh(0.5 * values) + 0.5


def fold_rows(values):
    return jnp.sum(values.reshape(-1, 8, values.shape[-1]), axis=0)


def segment_at(position, lengths_ref):
    total = lengths_ref[0, 0]
    seg = (position >= total).astype(jnp.int32)
    for index in range(1, lengths_ref.shape[1]):
        total = total + lengths_ref[0, index]
        seg = seg + (position >= total).astype(jnp.int32)
    return seg


def tap_mask(start, shift, rows, lengths_ref):
    position = start + lax.broadcasted_iota(jnp.int32, (rows, LANES), 0)
    same = (segment_at(position, lengths_ref) == segment_at(position - shift, lengths_ref)) & (position >= shift)
    return same.astype(f32)


def triangle(start, lengths_ref, transposed):
    first = lax.broadcasted_iota(jnp.int32, (Q, Q), 0)
    second = lax.broadcasted_iota(jnp.int32, (Q, Q), 1)
    same = segment_at(start + first, lengths_ref) == segment_at(start + second, lengths_ref)
    order = (second >= first) if transposed else (first >= second)
    return same & order


def head_columns(cum, step, cum_cols, step_cols):
    lane = lax.broadcasted_iota(jnp.int32, (Q, LANES), 1)
    for head in range(cum_cols.shape[0]):
        cum_cols[head] = jnp.broadcast_to(cum[:, head : head + 1], (Q, LANES))
    for pair in range(step_cols.shape[0]):
        even = jnp.broadcast_to(step[:, 2 * pair : 2 * pair + 1], (Q, LANES))
        odd = jnp.broadcast_to(step[:, 2 * pair + 1 : 2 * pair + 2], (Q, LANES))
        step_cols[pair] = jnp.where(lane < HEAD_DIM, even, odd)


def boundary(start, lengths_ref):
    position = start + lax.broadcasted_iota(jnp.int32, (Q, LANES), 0)
    seg = segment_at(position, lengths_ref)
    last = segment_at(jnp.full((1, LANES), start + Q - 1, jnp.int32), lengths_ref)
    before = segment_at(jnp.full((1, LANES), start - 1, jnp.int32), lengths_ref)
    before = jnp.where(start > 0, before, -1)
    return (seg == last), (seg == before), (last == before)


def softplus(values):
    return jnp.maximum(values, 0.0) + jnp.log1p(jnp.exp(-jnp.abs(values)))


def causal_taps(ext_ref, taps, bias, masks, columns):
    total = taps[3:4] * ext_ref[pl.ds(8, Q), columns]
    for shift in range(1, 4):
        total = total + taps[3 - shift : 4 - shift] * (ext_ref[pl.ds(8 - shift, Q), columns] * masks[shift - 1])
    return total + bias


def chunk_scalars(start, step_in, rate, lengths_ref, causal):
    step = softplus(step_in)
    log_decay = -step * jnp.exp(rate)
    cum = dot_nn(causal, log_decay, highest)
    return step, log_decay, cum


MESH = pl.DeviceIdType.MESH


def greet(groups, slots):
    group, slot = lax.axis_index("dp"), lax.axis_index("tensor")
    barrier = pltpu.get_barrier_semaphore()

    def along_dp(step, nothing):
        pl.semaphore_signal(barrier, inc=1, device_id=(lax.rem(group + step, groups), slot), device_id_type=MESH)
        return nothing

    lax.fori_loop(1, groups, along_dp, 0)
    for step in range(1, slots):
        pl.semaphore_signal(barrier, inc=1, device_id=(group, lax.rem(slot + step, slots)), device_id_type=MESH)
    pl.semaphore_wait(barrier, groups - 1 + slots - 1)


def head_kernel(
    send_run_ref, arrive_from_ref, lengths_ref, tokens, cotangent, wg_hbm, wv_hbm, ws_hbm, wt_hbm, wo_hbm,
    gain_ref, ggain_ref, tapv_ref, biasv_ref, taps_ref, biass_ref, stepb_ref, rate_ref, skip_ref,
    fulltok, fullcot, normed_out, dgate_out, dvalue_out, scaled_out, back_out, keep, out_part,
    dsmall_ref, inv_ref, dot_ref, sumv_ref, sums_ref, sumh_ref,
    wg, wv, ws, wt, wo, ptok, pcot, slots_buf, arr_tok, arr_cot, xbuf, nbuf, kbuf, gate_all, y_all,
    sraw_all, spre_all, stepin_all, states, d_carry, vext, dvext, sext, cum_cols, step_cols, cum_rows, neg_bias,
    scores, d_scores, d_entry, d_leave, acc_step, acc_cum, acc_dot, dsc, dgbuf, dvbuf, scbuf, bbuf, zbuf,
    sq_rows, ex_send, ex_recv, cols, masks, gathers,
    w_sem, in_sem, ts, tr, cs, cr, ags, agr, own_sem, x_sem, n_sem, keep_sem, o_sem, es, er,
):
    groups, slots = lax.axis_size("dp"), lax.axis_size("tensor")
    group, slot = lax.axis_index("dp"), lax.axis_index("tensor")
    runs, run, width = ptok.shape
    chunks = runs * run // Q
    per_chunk = Q // run
    pairs = d_carry.shape[0]
    last = slots - 1
    model = width * slots
    inner_total = wg.shape[1] * slots
    lane = lax.broadcasted_iota(jnp.int32, (Q, LANES), 1)
    first_half = lane < HEAD_DIM

    greet(groups, slots)
    weights = ((wg_hbm, wg), (wv_hbm, wv), (ws_hbm, ws), (wt_hbm, wt), (wo_hbm, wo))

    def weight_load(which):
        return pltpu.make_async_copy(weights[which][0], weights[which][1], w_sem.at[which])

    tok_in = pltpu.make_async_copy(tokens, ptok, in_sem.at[0])
    cot_in = pltpu.make_async_copy(cotangent, pcot, in_sem.at[1])
    tok_in.start()
    cot_in.start()
    for which in range(5):
        weight_load(which).start()

    def row_send(arrive, send_sem, recv_sem, step):
        other = lax.rem(group + step, groups)
        return pltpu.make_async_remote_copy(
            src_ref=slots_buf.at[other], dst_ref=arrive.at[group], send_sem=send_sem.at[other],
            recv_sem=recv_sem.at[group], device_id=(other, slot), device_id_type=MESH,
        )

    def send_rows(source, arrive, send_sem, recv_sem):
        def one(step, nothing):
            other = lax.rem(group + step, groups)
            slots_buf[other] = source[send_run_ref[other]]
            row_send(arrive, send_sem, recv_sem, step).start()
            return nothing

        lax.fori_loop(1, groups, one, 0)
        arrive[group] = source[send_run_ref[group]]

    def take_rows(packed, arrive, send_sem, recv_sem):
        def one(step, nothing):
            source = lax.rem(group + groups - step, groups)
            pltpu.make_async_remote_copy(
                src_ref=arrive.at[source], dst_ref=arrive.at[source], send_sem=send_sem.at[source],
                recv_sem=recv_sem.at[source], device_id=(group, slot), device_id_type=MESH,
            ).wait_recv()
            row_send(arrive, send_sem, recv_sem, step).wait_send()
            return nothing

        lax.fori_loop(1, groups, one, 0)
        for index in range(runs):
            packed[index] = arrive[arrive_from_ref[index]]

    def rows_of(packed, chunk):
        return packed.at[pl.ds(chunk * per_chunk, per_chunk)]

    def gather_push(kind, source, target, chunk, number, shard, to):
        return pltpu.make_async_remote_copy(
            src_ref=source, dst_ref=target.at[chunk, shard], send_sem=ags.at[kind, chunk, number],
            recv_sem=agr.at[kind, chunk, shard], device_id=(group, to), device_id_type=MESH,
        )

    gather_to = ((1, 2), (0, 2, 3), (3, 1, 0), (2, 1))

    def gather_direct(kind, packed, target, chunk, me):
        return [
            gather_push(kind, rows_of(packed, chunk), target, chunk, number, me, to)
            for number, to in enumerate(gather_to[me])
        ]

    def gather_forward(kind, target, chunk, me):
        shard, to = (3, 0) if me == 1 else (0, 3)
        return gather_push(kind, target.at[chunk, shard], target, chunk, 3, shard, to)

    def own_copy(kind, packed, target, chunk):
        return pltpu.make_async_copy(rows_of(packed, chunk), target.at[chunk, slot], own_sem.at[kind, chunk])

    def gather_start(kind, packed, target, chunk):
        own_copy(kind, packed, target, chunk).start()
        for me in range(slots):
            @pl.when(slot == me)
            def _(me=me):
                for copy in gather_direct(kind, packed, target, chunk, me):
                    copy.start()

    def gather_wait(kind, packed, target, chunk, hook=None):
        for me in range(slots):
            @pl.when(slot == me)
            def _(me=me):
                order = (3, 0, 2) if me == 1 else (0, 3, 1) if me == 2 else (1, 2, 3 - me)
                for position, shard in enumerate(order):
                    pltpu.make_async_remote_copy(
                        src_ref=target.at[chunk, shard], dst_ref=target.at[chunk, shard],
                        send_sem=ags.at[kind, chunk, 0], recv_sem=agr.at[kind, chunk, shard],
                        device_id=(group, slot), device_id_type=MESH,
                    ).wait_recv()
                    if position == 0 and me in (1, 2):
                        gather_forward(kind, target, chunk, me).start()
                    if position == 0 and hook is not None:
                        hook()
        own_copy(kind, packed, target, chunk).wait()

    def gather_drain(kind, packed, target):
        for chunk in range(chunks):
            for me in range(slots):
                @pl.when(slot == me)
                def _(me=me):
                    for copy in gather_direct(kind, packed, target, chunk, me):
                        copy.wait_send()
                    if me in (1, 2):
                        gather_forward(kind, target, chunk, me).wait_send()

    def keep_store(chunk, which):
        source = vext.at[pl.ds(8, Q)] if which == 0 else kbuf.at[1]
        return pltpu.make_async_copy(source, keep.at[chunk, which], keep_sem.at[which])

    def keep_load(chunk):
        return pltpu.make_async_copy(keep.at[chunk], kbuf, keep_sem.at[2])

    def normed_store(chunk):
        return pltpu.make_async_copy(nbuf, normed_out.at[chunk], n_sem)

    stores = ((dgbuf, dgate_out), (dvbuf, dvalue_out), (scbuf, scaled_out), (bbuf, back_out), (zbuf, out_part))

    def store(which, chunk):
        return pltpu.make_async_copy(stores[which][0], stores[which][1].at[chunk], o_sem.at[which])

    def x_load(source, chunk):
        return pltpu.make_async_copy(source.at[chunk], xbuf, x_sem)

    def ones_rows(values):
        return dot_nt(jnp.ones((8, LANES), f32), values, highest)

    def prepare(chunk, transposed):
        start = chunk * Q
        can_see = triangle(start, lengths_ref, transposed)
        neg_bias[...] = jnp.where(can_see, 0.0, -1e30)
        row = lax.broadcasted_iota(jnp.int32, (Q, Q), 0)
        col = lax.broadcasted_iota(jnp.int32, (Q, Q), 1)
        step_in = stepin_all[chunk]
        step, log_decay, cum = chunk_scalars(start, step_in, rate_ref[...], lengths_ref, (row >= col).astype(f32))
        cum_rows[...] = cum.T
        head_columns(cum, step, cum_cols, step_cols)
        return log_decay

    tok_in.wait()
    send_rows(ptok, arr_tok, ts, tr)
    states[0] = jnp.zeros_like(states[0])
    vext[pl.ds(0, 8)] = jnp.zeros((8, vext.shape[1]), f32)
    sext[pl.ds(0, 8)] = jnp.zeros((8, sext.shape[1]), f32)
    d_carry[...] = jnp.zeros_like(d_carry)
    dvext[pl.ds(Q, 8)] = jnp.zeros((8, dvext.shape[1]), f32)
    sumv_ref[...] = jnp.zeros_like(sumv_ref)
    sums_ref[...] = jnp.zeros_like(sums_ref)
    sumh_ref[...] = jnp.zeros_like(sumh_ref)
    place = lax.broadcasted_iota(jnp.int32, (2 * LANES, LANES), 1)
    source = lax.broadcasted_iota(jnp.int32, (2 * LANES, LANES), 0)
    source = (lax.rem(source, LANES) >= HEAD_DIM).astype(jnp.int32)
    for pair in range(pairs):
        gathers[pair] = (place == source + 2 * pair).astype(bf16)
    take_rows(ptok, arr_tok, ts, tr)
    gather_start(0, ptok, fulltok, 0)
    cot_in.wait()
    send_rows(pcot, arr_cot, cs, cr)
    for which in range(5):
        weight_load(which).wait()

    def forward_chunk(chunk, nothing):
        start = chunk * Q
        def second():
            @pl.when(chunk == 0)
            def _():
                gather_start(0, ptok, fulltok, 1)

        gather_wait(0, ptok, fulltok, chunk, second)
        x_load(fulltok, chunk).start()

        @pl.when(chunk + AHEAD < chunks)
        def _():
            gather_start(0, ptok, fulltok, chunk + AHEAD)

        @pl.when(chunk + AHEAD == chunks)
        def _():
            take_rows(pcot, arr_cot, cs, cr)

        @pl.when(chunk + AHEAD >= chunks)
        def _():
            gather_start(1, pcot, fullcot, 2 * chunks - 1 - AHEAD - chunk)

        @pl.when(chunk > 0)
        def _():
            normed_store(chunk - 1).wait()
            keep_store(chunk - 1, 0).wait()
            keep_store(chunk - 1, 1).wait()
            vext[pl.ds(0, 8)] = vext[pl.ds(Q, 8)]
            sext[pl.ds(0, 8)] = sext[pl.ds(Q, 8)]

        x_load(fulltok, chunk).wait()
        squares = jnp.zeros((Q, 1), f32)
        for shard in range(slots):
            wide = xbuf[shard].reshape(Q, width).astype(f32)
            squares = squares + jnp.sum(wide * wide, axis=1, keepdims=True)
        inv = lax.rsqrt(squares * (1.0 / model) + epsilon)
        inv_ref[pl.ds(start, Q)] = inv
        for shard in range(slots):
            wide = xbuf[shard].reshape(Q, width).astype(f32)
            columns = slice(shard * width, (shard + 1) * width)
            nbuf[:, columns] = (wide * inv * gain_ref[:, columns]).astype(bf16)
        normed_store(chunk).start()
        gate_all[chunk] = dot_nn(nbuf[...], wg[...])
        vext[pl.ds(8, Q)] = dot_nn(nbuf[...], wv[...])
        sext[pl.ds(8, Q)] = dot_nn(nbuf[...], ws[...])
        stepin_all[chunk] = dot_nn(nbuf[...], wt[...]) + stepb_ref[...]
        keep_store(chunk, 0).start()
        sraw_all[chunk] = sext[pl.ds(8, Q)]
        prepare(chunk, False)
        for shift in range(1, 4):
            masks[shift - 1] = tap_mask(start, shift, Q, lengths_ref)

        for half in range(2):
            columns = slice(half * LANES, (half + 1) * LANES)
            spre_all[chunk, :, columns] = causal_taps(
                sext, taps_ref[:, columns], biass_ref[:, columns], masks, columns
            )
        spre = spre_all[chunk]
        state_conv = spre * sigmoid(spre)
        entry = state_conv[:, :LANES]
        leave = state_conv[:, LANES:]
        scores[...] = dot_nt(leave, entry, highest)
        entry_t = entry.T.astype(bf16)
        leave_low = leave.astype(bf16)
        with_last, with_before, through = boundary(start, lengths_ref)
        to_last = with_last.astype(f32)
        from_before = with_before.astype(f32)
        passes = through.astype(f32)
        acc_dot[...] = jnp.zeros_like(acc_dot)

        def one_pair(pair, nothing):
            columns = pl.ds(pl.multiple_of(pair * LANES, LANES), LANES)
            pre = causal_taps(vext, tapv_ref[:, columns], biasv_ref[:, columns], masks, columns)
            kbuf[1, :, columns] = pre
            x = pre * sigmoid(pre)
            weighted = x * step_cols[pair]
            both = halves(weighted)
            results = []
            for half in range(2):
                head = 2 * pair + half
                c_col = cum_cols[head]
                c_row = cum_rows[pl.ds(head, 1), :]
                top = scores[:LANES, :LANES] * jnp.exp(c_col[:LANES] - c_row[:, :LANES] + neg_bias[:LANES, :LANES])
                low_left = scores[LANES:, :LANES] * jnp.exp(c_col[LANES:] - c_row[:, :LANES] + neg_bias[LANES:, :LANES])
                low_right = scores[LANES:, LANES:] * jnp.exp(
                    c_col[LANES:] - c_row[:, LANES:] + neg_bias[LANES:, LANES:]
                )
                upper = dot_nn(top.astype(bf16), both[:LANES])
                lower = dot_nn(jnp.concatenate([low_left, low_right], axis=1).astype(bf16), both)
                out = jnp.concatenate([upper, lower], axis=0)
                results.append(out[:, :LANES] + out[:, LANES:])
            inside = jnp.where(first_half, results[0], results[1])
            cum_pair = jnp.where(first_half, cum_cols[2 * pair], cum_cols[2 * pair + 1])
            cum_last = cum_pair[Q - 1 :]
            held = states[chunk, pair]
            carried = dot_halves(leave_low, held) * (jnp.exp(cum_pair) * from_before)
            y = inside + carried + skip_ref[:, columns] * x
            y_all[chunk, :, columns] = y
            to_end = jnp.exp(cum_last - cum_pair) * to_last
            states[chunk + 1, pair] = held * (jnp.exp(cum_last) * passes) + dot_halves(entry_t, to_end * weighted)
            gate = gate_all[chunk, :, columns]
            gated = y * (gate * sigmoid(gate))
            acc_dot[...] += gated * gated
            return nothing

        lax.fori_loop(0, pairs, one_pair, 0)
        keep_store(chunk, 1).start()
        sq_rows[chunk] = ones_rows(acc_dot[...])

        return nothing

    lax.fori_loop(0, chunks, forward_chunk, 0)
    normed_store(chunks - 1).wait()
    keep_store(chunks - 1, 0).wait()
    keep_store(chunks - 1, 1).wait()
    dsext = sext
    dsext[pl.ds(Q, 8)] = jnp.zeros((8, dsext.shape[1]), f32)

    def send_sums(chunk, step):
        return pltpu.make_async_remote_copy(
            src_ref=ex_send.at[chunk], dst_ref=ex_recv.at[chunk, slots - step], send_sem=es.at[chunk, step],
            recv_sem=er.at[chunk, slots - step], device_id=(group, lax.rem(slot + step, slots)), device_id_type=MESH,
        )

    def backward_chunk(index, nothing):
        chunk = chunks - 1 - index
        start = chunk * Q
        keep_load(chunk).start()
        gather_wait(1, pcot, fullcot, chunk)
        x_load(fullcot, chunk).start()

        @pl.when(chunk >= AHEAD)
        def _():
            gather_start(1, pcot, fullcot, chunk - AHEAD)

        x_load(fullcot, chunk).wait()
        for half in range(2):
            columns = slice(half * (dsc.shape[1] // 2), (half + 1) * (dsc.shape[1] // 2))
            value = dot_nn(xbuf[0].reshape(Q, width), wo[pl.ds(0, width), columns])
            for shard in range(1, slots):
                value = value + dot_nn(xbuf[shard].reshape(Q, width), wo[pl.ds(shard * width, width), columns])
            dsc[:, columns] = value
        acc_dot[...] = jnp.zeros_like(acc_dot)

        def product(pair, nothing):
            columns = pl.ds(pl.multiple_of(pair * LANES, LANES), LANES)
            gate = gate_all[chunk, :, columns]
            gated = y_all[chunk, :, columns] * (gate * sigmoid(gate))
            acc_dot[...] += dsc[:, columns] * ggain_ref[:, columns] * gated
            return nothing

        lax.fori_loop(0, pairs, product, 0)
        ex_send[chunk, pl.ds(0, 8)] = sq_rows[chunk]
        ex_send[chunk, pl.ds(8, 8)] = ones_rows(acc_dot[...])
        for step in range(1, slots):
            send_sums(chunk, step).start()

        @pl.when(index > 0)
        def _():
            dvext[pl.ds(Q, 8)] = dvext[pl.ds(0, 8)]
            dsext[pl.ds(Q, 8)] = dsext[pl.ds(0, 8)]
            for which in range(5):
                store(which, chunk + 1).wait()

        def later_mask(shift):
            position = start + lax.broadcasted_iota(jnp.int32, (Q, LANES), 0)
            same = segment_at(position, lengths_ref) == segment_at(position + shift, lengths_ref)
            return (same & (position + shift < chunks * Q)).astype(f32)

        log_decay = prepare(chunk, True)
        for shift in range(1, 4):
            masks[shift - 1] = later_mask(shift)
        step_in = stepin_all[chunk]
        spre = spre_all[chunk]
        spre_sig = sigmoid(spre)
        state_conv = spre * spre_sig
        entry = state_conv[:, :LANES]
        leave = state_conv[:, LANES:]
        scores[...] = dot_nt(entry, leave, highest)
        entry_low = entry.astype(bf16)
        leave_t = leave.T.astype(bf16)
        with_last, with_before, through = boundary(start, lengths_ref)
        to_last = with_last.astype(f32)
        from_before = with_before.astype(f32)
        passes = through.astype(f32)
        row_lane = lax.broadcasted_iota(jnp.int32, (Q, LANES), 0)
        for ref in (d_scores, d_entry, d_leave, acc_step, acc_cum, acc_dot):
            ref[...] = jnp.zeros_like(ref)

        sums = ex_send[chunk]
        for step in range(1, slots):
            send_sums(chunk, step).wait()
        for step in range(1, slots):
            sums = sums + ex_recv[chunk, step]
        rms_row = lax.rsqrt(sums[0:1] * (1.0 / inner_total) + epsilon)
        coef_row = rms_row * rms_row * rms_row * sums[8:9] * (1.0 / inner_total)
        cols[0] = jnp.broadcast_to(rms_row, (LANES, Q)).T
        cols[1] = jnp.broadcast_to(coef_row, (LANES, Q)).T
        keep_load(chunk).wait()

        def one_pair(pair, nothing):
            columns = pl.ds(pl.multiple_of(pair * LANES, LANES), LANES)
            rms = cols[0]
            pre = kbuf[1, :, columns]
            pre_sig = sigmoid(pre)
            x = pre * pre_sig
            step_pair = step_cols[pair]
            weighted = x * step_pair
            gate = gate_all[chunk, :, columns]
            gate_sig = sigmoid(gate)
            gate_silu = gate * gate_sig
            y = y_all[chunk, :, columns]
            gated = y * gate_silu
            d_scaled = dsc[:, columns]
            ggain = ggain_ref[:, columns]
            normalized = gated * rms
            scbuf[:, columns] = (normalized * ggain).astype(bf16)
            d_gated = rms * (d_scaled * ggain) - gated * cols[1]
            sumv_ref[pl.ds(0, 8), columns] += fold_rows(d_scaled * normalized)
            d_gate = (d_gated * y * (gate_sig + gate_silu * (1.0 - gate_sig))).astype(bf16)
            dgbuf[:, columns] = d_gate
            acc_dot[...] += d_gate.astype(f32) * gate
            d_y = d_gated * gate_silu
            skip = skip_ref[:, columns]
            sumv_ref[pl.ds(8, 8), columns] += fold_rows(d_y * x)
            y_scan = y - skip * x

            d_y_t = d_y.T.astype(bf16)
            d_y_both = halves(d_y)
            weighted_low = weighted.astype(bf16)
            results = []
            for half in range(2):
                head = 2 * pair + half
                own = jnp.where(first_half if half == 0 else ~first_half, weighted_low, jnp.zeros_like(weighted_low))
                d_m_top = dot_nn(own[:LANES], d_y_t)
                d_m_low = dot_nn(own[LANES:], d_y_t[:, LANES:])
                c_col = cum_cols[head]
                c_row = cum_rows[pl.ds(head, 1), :]
                l_top = jnp.exp(c_row - jnp.concatenate([c_col[:LANES]] * 2, axis=1) + neg_bias[:LANES])
                l_low = jnp.exp(c_row[:, LANES:] - c_col[LANES:] + neg_bias[LANES:, LANES:])
                d_scores[:LANES] += d_m_top * l_top
                d_scores[LANES:, LANES:] += d_m_low * l_low
                m_top = (scores[:LANES] * l_top).astype(bf16)
                m_low = (scores[LANES:, LANES:] * l_low).astype(bf16)
                upper = dot_nn(m_top, d_y_both)
                lower = dot_nn(m_low, d_y_both[LANES:])
                out = jnp.concatenate([upper, lower], axis=0)
                results.append(out[:, :LANES] + out[:, LANES:])
            d_weighted = jnp.where(first_half, results[0], results[1])
            cum_pair = jnp.where(first_half, cum_cols[2 * pair], cum_cols[2 * pair + 1])
            cum_last = cum_pair[Q - 1 :]
            to_end = jnp.exp(cum_last - cum_pair) * to_last
            from_start = jnp.exp(cum_pair) * from_before
            d_state = d_carry[pair]
            held = states[chunk, pair]
            d_weighted = d_weighted + dot_halves(entry_low, d_state) * to_end
            d_entry[...] += dot_nt((to_end * weighted).astype(bf16), d_state.astype(bf16))
            moved = from_start * d_y
            d_leave[...] += dot_nt(moved.astype(bf16), held.astype(bf16))
            state_dot = jnp.sum(states[chunk + 1, pair] * d_state, axis=0, keepdims=True)
            d_carry[pair] = d_state * (jnp.exp(cum_last) * passes) + dot_halves(leave_t, moved)

            to_step = d_weighted * x
            to_cum = d_y * y_scan - to_step * step_pair + jnp.where(row_lane == Q - 1, state_dot, 0.0)
            acc_step[...] += dot_nn(halves(to_step), gathers[pair])
            acc_cum[...] += dot_nn(halves(to_cum), gathers[pair])

            d_x = d_weighted * step_pair + skip * d_y
            d_pre = d_x * (pre_sig + x * (1.0 - pre_sig))
            dvext[pl.ds(0, Q), columns] = d_pre
            sumv_ref[pl.ds(16, 8), columns] += fold_rows(d_pre)
            vraw = kbuf[0, :, columns]
            total = tapv_ref[3:4, columns] * d_pre
            sumv_ref[pl.ds(24, 8), columns] += fold_rows(vraw * d_pre)
            for shift in range(1, 4):
                moved_back = dvext[pl.ds(shift, Q), columns] * masks[shift - 1]
                total = total + tapv_ref[3 - shift : 4 - shift, columns] * moved_back
                sumv_ref[pl.ds(24 + 8 * shift, 8), columns] += fold_rows(vraw * moved_back)
            d_value = total.astype(bf16)
            dvbuf[:, columns] = d_value
            acc_dot[...] += d_value.astype(f32) * vraw
            return nothing

        lax.fori_loop(0, pairs, one_pair, 0)
        for which in range(3):
            store(which, chunk).start()

        can_see = (neg_bias[...] == 0.0).astype(f32)
        d_log = dot_nn(can_see, acc_cum[...], highest)
        rate = jnp.exp(rate_ref[...])
        d_step_in = (acc_step[...] - d_log * rate) * sigmoid(step_in)
        d_step = d_step_in.astype(bf16)
        dsmall_ref[pl.ds(start, Q), 2 * LANES :] = d_step
        step_raw = step_in - stepb_ref[...]
        acc_dot[...] += jnp.where(lane < 2 * pairs, d_step.astype(f32) * step_raw, 0.0)
        sumh_ref[pl.ds(0, 8)] += fold_rows(d_step_in)
        sumh_ref[pl.ds(8, 8)] += fold_rows(d_log * log_decay)

        d_scores_now = d_scores[...]
        d_b = d_entry[...] + dot_halves(d_scores_now.astype(bf16), leave)
        d_c = d_leave[...] + dot_halves(d_scores_now.T.astype(bf16), entry)
        for half, grad in enumerate((d_b, d_c)):
            columns = slice(half * LANES, (half + 1) * LANES)
            part = spre_sig[:, columns]
            d_pre = grad * (part + state_conv[:, columns] * (1.0 - part))
            dsext[pl.ds(0, Q), columns] = d_pre
            sums_ref[pl.ds(0, 8), columns] += fold_rows(d_pre)
            sraw = sraw_all[chunk, :, columns]
            total = taps_ref[3:4, columns] * d_pre
            sums_ref[pl.ds(8, 8), columns] += fold_rows(sraw * d_pre)
            for shift in range(1, 4):
                moved_back = dsext[pl.ds(shift, Q), columns] * masks[shift - 1]
                total = total + taps_ref[3 - shift : 4 - shift, columns] * moved_back
                sums_ref[pl.ds(8 + 8 * shift, 8), columns] += fold_rows(sraw * moved_back)
            d_state_raw = total.astype(bf16)
            dsmall_ref[pl.ds(start, Q), columns] = d_state_raw
            acc_dot[...] += d_state_raw.astype(f32) * sraw
        dot_ref[chunk] = ones_rows(acc_dot[...])

        for shard in range(slots):
            here = pl.ds(shard * width, width)
            part = dot_nt(dgbuf[...], wg[here]) + dot_nt(dvbuf[...], wv[here])
            part = part + dot_nt(dsmall_ref[pl.ds(start, Q), : 2 * LANES], ws[here]) + dot_nt(d_step, wt[here])
            bbuf[:, shard * width : (shard + 1) * width] = part.astype(bf16)
        store(3, chunk).start()
        for shard in range(slots):
            part = dot_nt(scbuf[...], wo[pl.ds(shard * width, width)])
            zbuf[:, shard * width : (shard + 1) * width] = part.astype(bf16)
        store(4, chunk).start()
        return nothing

    lax.fori_loop(0, chunks, backward_chunk, 0)
    for which in range(5):
        store(which, 0).wait()
    gather_drain(0, ptok, fulltok)
    gather_drain(1, pcot, fullcot)


def head(send_run, arrive_from, lengths, tokens, cotangent, wg, wv, ws, wt, wo, small):
    groups, slots = lax.axis_size("dp"), lax.axis_size("tensor")
    runs, run, width = tokens.shape
    rows = runs * run
    chunks, per_chunk = rows // Q, Q // run
    model, inner = wg.shape
    pairs = inner // LANES
    vmem, anywhere, smem = (pl.BlockSpec(memory_space=s) for s in (pltpu.VMEM, pl.ANY, pltpu.SMEM))
    dma = pltpu.SemaphoreType.DMA
    shape = jax.ShapeDtypeStruct
    return pl.pallas_call(
        head_kernel,
        out_shape=[
            shape((chunks, slots, per_chunk, run, width), bf16),
            shape((chunks, slots, per_chunk, run, width), bf16),
            shape((chunks, Q, model), bf16),
            shape((chunks, Q, inner), bf16),
            shape((chunks, Q, inner), bf16),
            shape((chunks, Q, inner), bf16),
            shape((chunks, Q, model), bf16),
            shape((chunks, 2, Q, inner), f32),
            shape((chunks, Q, model), bf16),
            shape((rows, 3 * LANES), bf16),
            shape((rows, 1), f32),
            shape((chunks, 8, Q), f32),
            shape((56, inner), f32),
            shape((40, 2 * LANES), f32),
            shape((16, LANES), f32),
        ],
        in_specs=[smem] * 3 + [anywhere] * 7 + [vmem] * len(small),
        out_specs=[anywhere] * 9 + [vmem] * 6,
        scratch_shapes=[
            pltpu.VMEM(wg.shape, bf16), pltpu.VMEM(wv.shape, bf16), pltpu.VMEM(ws.shape, bf16),
            pltpu.VMEM(wt.shape, bf16), pltpu.VMEM(wo.shape, bf16),
            pltpu.VMEM((runs, run, width), bf16),
            pltpu.VMEM((runs, run, width), bf16),
            pltpu.VMEM((groups, run, width), bf16),
            pltpu.VMEM((groups, run, width), bf16),
            pltpu.VMEM((groups, run, width), bf16),
            pltpu.VMEM((slots, per_chunk, run, width), bf16),
            pltpu.VMEM((Q, model), bf16),
            pltpu.VMEM((2, Q, inner), f32),
            pltpu.VMEM((chunks, Q, inner), f32),
            pltpu.VMEM((chunks, Q, inner), f32),
            pltpu.VMEM((chunks, Q, 2 * LANES), f32),
            pltpu.VMEM((chunks, Q, 2 * LANES), f32),
            pltpu.VMEM((chunks, Q, LANES), f32),
            pltpu.VMEM((chunks + 1, pairs, LANES, LANES), f32),
            pltpu.VMEM((pairs, LANES, LANES), f32),
            pltpu.VMEM((Q + 8, inner), f32),
            pltpu.VMEM((Q + 8, inner), f32),
            pltpu.VMEM((Q + 8, 2 * LANES), f32),
            pltpu.VMEM((2 * pairs, Q, LANES), f32),
            pltpu.VMEM((pairs, Q, LANES), f32),
            pltpu.VMEM((LANES, Q), f32),
            pltpu.VMEM((Q, Q), f32),
            pltpu.VMEM((Q, Q), f32),
            pltpu.VMEM((Q, Q), f32),
            pltpu.VMEM((Q, LANES), f32),
            pltpu.VMEM((Q, LANES), f32),
            pltpu.VMEM((Q, LANES), f32),
            pltpu.VMEM((Q, LANES), f32),
            pltpu.VMEM((Q, LANES), f32),
            pltpu.VMEM((Q, inner), f32),
            pltpu.VMEM((Q, inner), bf16),
            pltpu.VMEM((Q, inner), bf16),
            pltpu.VMEM((Q, inner), bf16),
            pltpu.VMEM((Q, model), bf16),
            pltpu.VMEM((Q, model), bf16),
            pltpu.VMEM((chunks, 8, Q), f32),
            pltpu.VMEM((chunks, 16, Q), f32),
            pltpu.VMEM((chunks, slots, 16, Q), f32),
            pltpu.VMEM((2, Q, LANES), f32),
            pltpu.VMEM((3, Q, LANES), f32),
            pltpu.VMEM((pairs, 2 * LANES, LANES), bf16),
            dma((5,)), dma((2,)), dma((groups,)), dma((groups,)), dma((groups,)), dma((groups,)),
            dma((2, chunks, 4)), dma((2, chunks, slots)), dma((2, chunks)), dma, dma, dma((3,)), dma((5,)),
            dma((chunks, slots)), dma((chunks, slots)),
        ],
        compiler_params=pltpu.CompilerParams(collective_id=2, has_side_effects=True, vmem_limit_bytes=HEAD_VMEM),
        name="head",
    )(send_run, arrive_from, lengths, tokens, cotangent, wg, wv, ws, wt, wo, *small)


def tail_kernel(
    back_run_ref, return_from_ref, out_part, back_part, normed, tokens, cotangent, scaled, d_gate, d_value,
    row_dot_ref, inv_ref, gain_ref, small_ref, small_z_ref, dsmall_ref,
    layer_ref, tgrad_ref, small_out, ngain_out, share0, share1, share2, state_out, step_out,
    z_recv, z_comb, z_own, z_mix, ptok, pcot, rd_recv, rd_col, row_buf, slots_buf, arrive, left, right, full,
    core_recv, chip_recv, total, sz_recv, small_all, small_recv, ngain_all, ngain_recv,
    thin, thin_core, thin_chip, thin_own, thin_z,
    load_sem, mix_sem, left_sem, right_sem, zs, zr, zc, rds, rdr, szs, szr, sms, smr, ngs, ngr, rs, rr, cs, cr, hs, hr, tcs, ths, thr, tzs, tzr,
):
    groups, slots = lax.axis_size("dp"), lax.axis_size("tensor")
    group, slot = lax.axis_index("dp"), lax.axis_index("tensor")
    jobs = z_recv.shape[0]
    pieces = jobs // 2
    runs, run, width = layer_ref.shape
    rows = runs * run
    piece_run = run // pieces
    chips = groups // 2
    core = lax.rem(group, 2)
    chip = group // 2
    grow = share0.shape[0]
    per_block = 256 // grow
    blocks = full.shape[1] // per_block
    inner = share0.shape[1]
    last = slots - 1

    greet(groups, slots)

    def z_small(source, target, send_sem, recv_sem, step):
        return pltpu.make_async_remote_copy(
            src_ref=source, dst_ref=target.at[slots - step], send_sem=send_sem.at[step],
            recv_sem=recv_sem.at[slots - step], device_id=(group, lax.rem(slot + step, slots)), device_id_type=MESH,
        )

    def send_dot(step):
        return z_small(row_dot_ref, rd_recv, rds, rdr, step)

    def send_state(step):
        return z_small(small_z_ref, sz_recv, szs, szr, step)

    for step in range(1, slots):
        send_state(step).start()
        send_dot(step).start()

    def piece_of(job, shard):
        source = out_part if job < pieces else back_part
        return source.at[:, pl.ds((job % pieces) * piece_run, piece_run), pl.ds(shard * width, width)]

    def landing(job, me, to):
        return z_recv.at[job, me if me < to else me - 1], zr.at[job, me if me < to else me - 1]

    def z_push(job, number, shard, to, source, target, sem):
        return pltpu.make_async_remote_copy(
            src_ref=source, dst_ref=target, send_sem=zs.at[job, number], recv_sem=sem, device_id=(group, to),
            device_id_type=MESH,
        )

    def direct(job, me, early):
        def push(number, to):
            return z_push(job, number, to, to, piece_of(job, to), *landing(job, me, to))

        def to_mix(number, shard, to):
            return z_push(job, number, shard, to, piece_of(job, shard), z_comb.at[job], zc.at[job])

        if me == 0:
            return [to_mix(0, 3, 1)] if early else [push(1, 2), push(2, 1)]
        if me == last:
            return [to_mix(0, 0, 2)] if early else [push(1, 1), push(2, 2)]
        if early:
            return []
        return [push(0, 0), push(1, 2)] if me == 1 else [push(0, 3), push(1, 1)]

    def mixed(job, me):
        to = 3 if me == 1 else 0
        return z_push(job, 2, to, to, z_mix.at[job], *landing(job, me, to))

    def own_load(kind):
        source = back_part if kind else out_part
        return pltpu.make_async_copy(source.at[:, :, pl.ds(slot * width, width)], z_own.at[kind], load_sem.at[kind])

    def mix_load(job, me):
        return pltpu.make_async_copy(piece_of(job, 3 if me == 1 else 0), z_mix.at[job], mix_sem.at[job])

    def shard_load(which):
        source, target = ((tokens, ptok), (cotangent, pcot))[which]
        return pltpu.make_async_copy(source.at[:, slot], target, load_sem.at[2 + which])

    def push(job, early):
        for me in (0, last) if early else range(slots):
            @pl.when(slot == me)
            def _(me=me):
                for copy in direct(job, me, early):
                    copy.start()

    def combine(job):
        for me in (1, 2):
            @pl.when(slot == me)
            def _(me=me):
                mix_load(job, me).wait()
                z_push(job, 2, 0, 0, z_comb.at[job], z_comb.at[job], zc.at[job]).wait_recv()
                both = z_mix[job].astype(f32) + z_comb[job].astype(f32)
                z_mix[job] = both.astype(bf16)
                mixed(job, me).start()

    rights = (scaled, d_gate, d_value)
    shares = (share0, share1, share2)

    def right_load(which):
        return pltpu.make_async_copy(rights[which], right.at[which % 2], right_sem.at[which])

    def left_load(which, block, place):
        if which == 0:
            per_shard = width // 256
            columns = pl.ds(pl.multiple_of(lax.rem(block, per_shard) * 256, 256), 256)
            source = cotangent.at[:, block // per_shard, :, :, columns]
        else:
            source = normed.at[:, :, :, pl.ds(pl.multiple_of(block * 256, 256), 256)]
        return pltpu.make_async_copy(source, left.at[place], left_sem.at[place])

    def grad_blocks(which, begin, end):
        def one(block, nothing):
            place = lax.rem(block, 2)

            @pl.when(block + 1 < blocks)
            def _():
                left_load(which, block + 1, 1 - place).start()

            left_load(which, block, place).wait()
            value = lax.dot_general(
                left[place].reshape(rows, 256), right[which % 2], (((0,), (0,)), ((), ())), preferred_element_type=f32
            )
            full[which % 2, pl.ds(block * per_block, per_block)] = value.reshape(per_block, grow, -1).astype(bf16)
            if which == 1:
                value = lax.dot_general(
                    left[place].reshape(rows, 256), dsmall_ref[...], (((0,), (0,)), ((), ())), preferred_element_type=f32
                )
                thin[pl.ds(block * per_block, per_block)] = value.reshape(per_block, grow, -1)
            return nothing

        lax.fori_loop(begin, end, one, 0)

    partner = group + 1 - 2 * core

    def core_send(which):
        theirs = full.at[which % 2].reshape(chips, 2, grow, inner).at[:, 1 - core]
        return pltpu.make_async_remote_copy(
            src_ref=theirs, dst_ref=core_recv.at[which], send_sem=cs.at[which], recv_sem=cr.at[which],
            device_id=(partner, slot), device_id_type=MESH,
        )

    def chip_send(which, step):
        other = lax.rem(chip + step, chips)
        return pltpu.make_async_remote_copy(
            src_ref=full.at[which % 2, 2 * other + core], dst_ref=chip_recv.at[which, chips - step],
            send_sem=hs.at[which, step], recv_sem=hr.at[which, chips - step], device_id=(2 * other + core, slot),
            device_id_type=MESH,
        )

    def chip_pushes(which):
        core_send(which).wait()

        def one(step, nothing):
            other = lax.rem(chip + step, chips)
            mine = 2 * other + core
            both = full[which % 2, mine].astype(f32) + core_recv[which, other].astype(f32)
            full[which % 2, mine] = both.astype(bf16)
            chip_send(which, step).start()
            return nothing

        lax.fori_loop(1, chips, one, 0)
        shares[which][...] = full[which % 2, group].astype(f32) + core_recv[which, chip].astype(f32)

    def chip_drain(which):
        def drain(step, nothing):
            chip_send(which, step).wait_send()
            return nothing

        lax.fori_loop(1, chips, drain, 0)

    def chip_total(which):
        def one(step, nothing):
            pltpu.make_async_remote_copy(
                src_ref=chip_recv.at[which, step], dst_ref=chip_recv.at[which, step], send_sem=hs.at[which, step],
                recv_sem=hr.at[which, step], device_id=(group, slot), device_id_type=MESH,
            ).wait_recv()
            shares[which][...] += chip_recv[which, step].astype(f32)
            return nothing

        lax.fori_loop(1, chips, one, 0)

    def thin_core_send():
        theirs = thin.reshape(chips, 2, grow, thin.shape[2]).at[:, 1 - core]
        return pltpu.make_async_remote_copy(
            src_ref=theirs, dst_ref=thin_core, send_sem=tcs.at[0], recv_sem=tcs.at[1], device_id=(partner, slot),
            device_id_type=MESH,
        )

    def thin_chip_send(step):
        other = lax.rem(chip + step, chips)
        return pltpu.make_async_remote_copy(
            src_ref=thin.at[2 * other + core], dst_ref=thin_chip.at[chips - step], send_sem=ths.at[step],
            recv_sem=thr.at[chips - step], device_id=(2 * other + core, slot), device_id_type=MESH,
        )

    def thin_pushes():
        thin_core_send().wait()

        def one(step, nothing):
            other = lax.rem(chip + step, chips)
            thin[2 * other + core] = thin[2 * other + core] + thin_core[other]
            thin_chip_send(step).start()
            return nothing

        lax.fori_loop(1, chips, one, 0)
        thin_own[...] = thin[group] + thin_core[chip]

    def thin_z_send(step):
        other = lax.rem(slot + step, slots)
        part = state_out.shape[0]
        return pltpu.make_async_remote_copy(
            src_ref=thin_own.at[pl.ds(other * part, part), pl.ds(0, 2 * LANES)], dst_ref=thin_z.at[slots - step],
            send_sem=tzs.at[step], recv_sem=tzr.at[slots - step], device_id=(group, other), device_id_type=MESH,
        )

    def thin_total():
        def one(step, nothing):
            pltpu.make_async_remote_copy(
                src_ref=thin_chip.at[step], dst_ref=thin_chip.at[step], send_sem=ths.at[step], recv_sem=thr.at[step],
                device_id=(group, slot), device_id_type=MESH,
            ).wait_recv()
            thin_own[...] += thin_chip[step]
            return nothing

        lax.fori_loop(1, chips, one, 0)
        for step in range(1, slots):
            thin_z_send(step).start()
        step_out[...] = thin_own[:, 2 * LANES :]

    def thin_finish():
        part = state_out.shape[0]
        acc = thin_own[pl.ds(slot * part, part), : 2 * LANES]
        for step in range(1, slots):
            thin_z_send(step).wait()
        for step in range(1, slots):
            acc = acc + thin_z[step]
        state_out[...] = acc

        def drain(step, nothing):
            thin_chip_send(step).wait_send()
            return nothing

        lax.fori_loop(1, chips, drain, 0)

    def dp_small(source, target, send_sem, recv_sem, step):
        return pltpu.make_async_remote_copy(
            src_ref=source, dst_ref=target.at[groups - step], send_sem=send_sem.at[step],
            recv_sem=recv_sem.at[groups - step], device_id=(lax.rem(group + step, groups), slot), device_id_type=MESH,
        )

    def dp_small_start(source, target, send_sem, recv_sem):
        def one(step, nothing):
            dp_small(source, target, send_sem, recv_sem, step).start()
            return nothing

        lax.fori_loop(1, groups, one, 0)

    def dp_small_finish(source, target, send_sem, recv_sem, result):
        result[...] = source[...]

        def one(step, nothing):
            pltpu.make_async_remote_copy(
                src_ref=target.at[step], dst_ref=target.at[step], send_sem=send_sem.at[step],
                recv_sem=recv_sem.at[step], device_id=(group, slot), device_id_type=MESH,
            ).wait_recv()
            result[...] += target[step]
            return nothing

        lax.fori_loop(1, groups, one, 0)

        def drain(step, nothing):
            dp_small(source, target, send_sem, recv_sem, step).wait_send()
            return nothing

        lax.fori_loop(1, groups, drain, 0)

    def row_send(job, step):
        other = lax.rem(group + step, groups)
        return pltpu.make_async_remote_copy(
            src_ref=slots_buf.at[job % pieces, other], dst_ref=arrive.at[job, group], send_sem=rs.at[job, other],
            recv_sem=rr.at[job, group], device_id=(other, slot), device_id_type=MESH,
        )

    def rows_drain(job):
        def one(step, nothing):
            row_send(job, step).wait_send()
            return nothing

        lax.fori_loop(1, groups, one, 0)

    def finish(job):
        kind, piece = job // pieces, job % pieces
        here = pl.ds(piece * piece_run, piece_run)
        tall = runs * piece_run
        for me in range(slots):
            @pl.when(slot == me)
            def _(me=me):
                acc = z_own[kind, :, here, :].astype(f32)
                for source in ((1, 2) if me in (0, 3) else tuple(s for s in range(slots) if s != me)):
                    place, sem = landing(job, source, me)
                    z_push(job, 0, 0, 0, place, place, sem).wait_recv()
                    acc = acc + place[...].astype(f32)
                total[...] = acc
        summed = total[...].reshape(tall, width)
        kept = ptok[:, :, here, :].reshape(tall, width).astype(f32)
        if kind == 0:
            result = kept + summed
        else:
            inv = inv_ref[:, here, :].reshape(tall, 1)
            unit = kept * inv
            ngain_all[...] += fold_rows(summed * unit)
            dot_cols = rd_col[:, here, :].reshape(tall, LANES)
            dot_cols = jnp.concatenate([dot_cols] * (width // LANES), axis=1)
            cot = pcot[:, :, here, :].reshape(tall, width).astype(f32)
            result = cot + inv * (summed * gain_ref[...] - unit * dot_cols)
        row_buf[...] = result.astype(bf16).reshape(runs, piece_run, width)

        def fill(step, nothing):
            other = lax.rem(group + step, groups)
            slots_buf[job % pieces, other] = row_buf[back_run_ref[other]]
            row_send(job, step).start()
            return nothing

        if kind == 1:
            rows_drain(job - pieces)
        lax.fori_loop(1, groups, fill, 0)
        arrive[job, group] = row_buf[back_run_ref[group]]

    def rows_wait(kind):
        for job in range(kind * pieces, (kind + 1) * pieces):
            def one(step, nothing, job=job):
                source = lax.rem(group + groups - step, groups)
                pltpu.make_async_remote_copy(
                    src_ref=arrive.at[job, source], dst_ref=arrive.at[job, source], send_sem=rs.at[job, source],
                    recv_sem=rr.at[job, source], device_id=(group, slot), device_id_type=MESH,
                ).wait_recv()
                return nothing

            lax.fori_loop(1, groups, one, 0)

    def rows_take(kind, target):
        for piece in range(pieces):
            for index in range(runs):
                target[index, pl.ds(piece * piece_run, piece_run)] = arrive[kind * pieces + piece, return_from_ref[index]]

    def let_in(job):
        if job < jobs:
            push(job, False)
            combine(job)

    def step_of(job):
        if job + EARLY < jobs:
            push(job + EARLY, True)
        let_in(job + WINDOW)
        finish(job)

    for job in range(min(EARLY, jobs)):
        push(job, True)
    own_load(0).start()
    own_load(1).start()
    shard_load(0).start()
    shard_load(1).start()
    for me in (1, 2):
        @pl.when(slot == me)
        def _(me=me):
            for job in range(jobs):
                mix_load(job, me).start()
    right_load(0).start()
    left_load(0, 0, 0).start()
    right_load(1).start()
    ngain_all[...] = jnp.zeros_like(ngain_all)

    half = blocks // 2
    right_load(0).wait()
    grad_blocks(0, 0, half)
    small_z = small_z_ref[...]
    for step in range(1, slots):
        send_state(step).wait()
    for step in range(1, slots):
        small_z = small_z + sz_recv[step]
    small_all[:, pl.ds(0, inner)] = small_ref[...]
    small_all[:, pl.ds(inner, 2 * LANES)] = small_z
    dp_small_start(small_all, small_recv, sms, smr)
    grad_blocks(0, half, blocks)
    core_send(0).start()
    right_load(2).start()
    for kind in range(2):
        own_load(kind).wait()
        shard_load(kind).wait()
    left_load(1, 0, 0).start()
    push(0, False)
    right_load(1).wait()
    grad_blocks(1, 0, half)
    chip_pushes(0)
    grad_blocks(1, half, blocks)
    core_send(1).start()
    thin_core_send().start()
    left_load(2, 0, 0).start()
    rd_total = row_dot_ref[...]
    for step in range(1, slots):
        send_dot(step).wait()
    for step in range(1, slots):
        rd_total = rd_total + rd_recv[step]
    rd_total = rd_total * (1.0 / (width * slots))
    for block in range(rows // 256):
        piece_row = jnp.broadcast_to(rd_total[0:1, block * 256 : (block + 1) * 256], (LANES, 256))
        count = 256 // run
        rd_col[pl.ds(block * count, count)] = piece_row.T.reshape(count, run, LANES)
    combine(0)
    right_load(2).wait()
    chip_drain(0)
    let_in(1)
    grad_blocks(2, 0, half)
    chip_pushes(1)
    thin_pushes()
    grad_blocks(2, half, blocks)
    core_send(2).start()
    for job in range(2, WINDOW):
        let_in(job)
    for job in range(jobs):
        if job == 1:
            chip_pushes(2)
        step_of(job)
        if job == jobs // 2:
            thin_total()
    dp_small_start(ngain_all, ngain_recv, ngs, ngr)

    rows_wait(0)
    rows_wait(1)
    for job in range(pieces, jobs):
        rows_drain(job)
    rows_take(0, layer_ref)
    rows_take(1, tgrad_ref)
    dp_small_finish(small_all, small_recv, sms, smr, small_out)
    for which in range(3):
        chip_total(which)
    thin_finish()
    chip_drain(1)
    chip_drain(2)
    dp_small_finish(ngain_all, ngain_recv, ngs, ngr, ngain_out)
    for me in range(slots):
        @pl.when(slot == me)
        def _(me=me):
            for job in range(jobs):
                for copy in direct(job, me, True) + direct(job, me, False):
                    copy.wait_send()
                if me in (1, 2):
                    mixed(job, me).wait_send()


def tail(back_run, return_from, out_part, back_part, normed, tokens, cotangent, scaled, d_gate, d_value, row_dot, inv,
         gain, small, small_z, d_small):
    groups, slots = lax.axis_size("dp"), lax.axis_size("tensor")
    runs, run, model = out_part.shape
    width = model // slots
    rows = runs * run
    inner = scaled.shape[1]
    pieces = min(4, run // 16)
    jobs = 2 * pieces
    piece_run = run // pieces
    grow = model // groups
    chips = groups // 2
    vmem, anywhere, smem = (pl.BlockSpec(memory_space=s) for s in (pltpu.VMEM, pl.ANY, pltpu.SMEM))
    dma = pltpu.SemaphoreType.DMA
    shape = jax.ShapeDtypeStruct
    by_chunk = tokens.shape[:1] + tokens.shape[2:]
    part = (runs, piece_run, width)
    return pl.pallas_call(
        tail_kernel,
        out_shape=[
            shape((runs, run, width), bf16), shape((runs, run, width), bf16), shape((8, inner + 2 * LANES), f32),
            shape((8, width), f32),
        ] + [shape((grow, inner), f32)] * 3 + [shape((grow // slots, 2 * LANES), f32), shape((grow, LANES), f32)],
        in_specs=[smem] * 2 + [anywhere] * 8 + [vmem] * 6,
        out_specs=[vmem] * 9,
        scratch_shapes=[
            pltpu.VMEM((jobs, slots - 1) + part, bf16),
            pltpu.VMEM((jobs,) + part, bf16),
            pltpu.VMEM((2, runs, run, width), bf16),
            pltpu.VMEM((jobs,) + part, bf16),
            pltpu.VMEM(by_chunk, bf16),
            pltpu.VMEM(by_chunk, bf16),
            pltpu.VMEM((slots, 8, rows), f32),
            pltpu.VMEM((runs, run, LANES), f32),
            pltpu.VMEM(part, bf16),
            pltpu.VMEM((pieces, groups, piece_run, width), bf16),
            pltpu.VMEM((jobs, groups, piece_run, width), bf16),
            pltpu.VMEM((2,) + by_chunk[:-1] + (256,), bf16),
            pltpu.VMEM((2, rows, inner), bf16),
            pltpu.VMEM((2, groups, grow, inner), bf16),
            pltpu.VMEM((3, chips, grow, inner), bf16),
            pltpu.VMEM((3, chips, grow, inner), bf16),
            pltpu.VMEM(part, f32),
            pltpu.VMEM((slots, 8, 2 * LANES), f32),
            pltpu.VMEM((8, inner + 2 * LANES), f32),
            pltpu.VMEM((groups, 8, inner + 2 * LANES), f32),
            pltpu.VMEM((8, width), f32),
            pltpu.VMEM((groups, 8, width), f32),
            pltpu.VMEM((groups, grow, 3 * LANES), f32),
            pltpu.VMEM((chips, grow, 3 * LANES), f32),
            pltpu.VMEM((chips, grow, 3 * LANES), f32),
            pltpu.VMEM((grow, 3 * LANES), f32),
            pltpu.VMEM((slots, grow // slots, 2 * LANES), f32),
            dma((4,)), dma((jobs,)), dma((2,)), dma((3,)),
            dma((jobs, 3)), dma((jobs, slots - 1)), dma((jobs,)),
            dma((slots,)), dma((slots,)), dma((slots,)), dma((slots,)),
            dma((groups,)), dma((groups,)), dma((groups,)), dma((groups,)),
            dma((jobs, groups)), dma((jobs, groups)),
            dma((3,)), dma((3,)), dma((3, chips)), dma((3, chips)),
            dma((2,)), dma((chips,)), dma((chips,)), dma((slots,)), dma((slots,)),
        ],
        compiler_params=pltpu.CompilerParams(collective_id=3, has_side_effects=True, vmem_limit_bytes=64 << 20),
        name="tail",
    )(back_run, return_from, out_part, back_part, normed, tokens, cotangent, scaled, d_gate, d_value, row_dot, inv, gain,
      small, small_z, d_small)


def pad_heads(values):
    return jnp.pad(values, ((0, 0), (0, LANES - values.shape[1])))


def per_device(
    tokens, cotangent, norm_gain, gate_proj, value_proj, state_proj, step_proj, conv_value, conv_value_bias,
    conv_state, conv_state_bias, step_bias, decay_log, skip_gain, gate_gain, out_proj, token_order, lengths,
):
    groups = lax.axis_size("dp")
    group = lax.axis_index("dp")
    slots = lax.axis_size("tensor")
    slot = lax.axis_index("tensor")
    rows, width = tokens.shape
    model = width * slots
    inner = gate_proj.shape[1]
    heads = step_bias.shape[0]
    run = 2 * rows // groups
    runs = rows // run

    source_run = token_order.reshape(groups, runs, run)[:, :, 0] // run
    source_group = source_run // runs
    from_here = source_group == group
    send_run = jnp.sum(jnp.where(from_here, source_run % runs, 0), axis=1)
    arrive_from = lax.dynamic_index_in_dim(source_group, group, 0, keepdims=False)
    every = jnp.arange(groups, dtype=jnp.int32)
    back_run = jnp.sum(
        jnp.where(arrive_from[None, :] == every[:, None], jnp.arange(runs, dtype=jnp.int32)[None, :], 0), axis=1
    )
    local_run = group * runs + jnp.arange(runs, dtype=jnp.int32)
    return_from = jnp.sum(
        jnp.where(source_run[None] == local_run[:, None, None], every[None, :, None], 0), axis=(1, 2)
    )

    def cut(values):
        return values.reshape(runs, run, values.shape[1])

    gain_full = norm_gain.astype(f32)
    small = (
        gain_full[None], gate_gain.astype(f32)[None], conv_value.astype(f32), conv_value_bias.astype(f32)[None],
        conv_state.astype(f32), conv_state_bias.astype(f32)[None], pad_heads(step_bias[None]),
        pad_heads(decay_log[None]), jnp.repeat(skip_gain, HEAD_DIM)[None],
    )
    (full_tokens, full_cotangent, normed, d_gate, d_value, scaled, back_partial, _, out_partial, d_small,
     inv_rms, row_dot, sumv, sums, sumh) = head(
        send_run, arrive_from, lengths, cut(tokens), cut(cotangent), gate_proj, value_proj, state_proj,
        pad_heads(step_proj), out_proj, small,
    )
    row_dot = row_dot.transpose(1, 0, 2).reshape(8, rows)
    normed_cut = normed.reshape(full_tokens.shape[0], full_tokens.shape[2], run, model)
    d_gate, d_value, scaled, back_partial, out_partial = (
        v.reshape(rows, v.shape[2]) for v in (d_gate, d_value, scaled, back_partial, out_partial)
    )
    gain_share = lax.dynamic_slice_in_dim(gain_full, slot * width, width, 0)
    by_head = jnp.pad(sumh.reshape(2, 8, LANES).sum(1).reshape(1, 2 * LANES), ((0, 0), (0, inner - 2 * LANES)))
    small = jnp.concatenate([sumv.reshape(7, 8, inner).sum(1), by_head])
    small_z = jnp.pad(sums.reshape(5, 8, 2 * LANES).sum(1), ((0, 3), (0, 0)))
    layer_output, tokens_grad, small, norm_gain_rows, out_grad_share, gate_share, value_share, state_share, step_share = tail(
        back_run, return_from, cut(out_partial), cut(back_partial), normed_cut, full_tokens, full_cotangent, scaled,
        d_gate, d_value, row_dot, cut(inv_rms), gain_share[None], small, small_z, d_small,
    )
    state_sums = small[:, inner:]
    return (
        layer_output.reshape(rows, width),
        tokens_grad.reshape(rows, width),
        jnp.sum(norm_gain_rows, axis=0),
        gate_share,
        value_share,
        state_share,
        step_share[:, :heads],
        small[6:2:-1, :inner],
        small[2, :inner],
        state_sums[4:0:-1],
        state_sums[0],
        small[7, :heads],
        small[7, LANES : LANES + heads],
        jnp.sum(small[1, :inner].reshape(heads, HEAD_DIM), axis=1),
        small[0, :inner],
        out_grad_share,
    )


def solution(mesh):
    across = P(None, "tensor")
    both = P("dp", "tensor")
    heads = P("tensor")
    return jax.shard_map(
        per_device,
        mesh=mesh,
        in_specs=(
            both, both, P(), across, across, P(), across, across, heads, P(), P(), heads, heads, heads, heads, across,
            P(), P("dp", None),
        ),
        out_specs=(
            both, both, heads, both, both, P(("dp", "tensor"), None), both, across, heads, P(), P(), heads, heads, heads,
            heads, both,
        ),
        check_vma=False,
    )
```

```python
import jax
import jax.numpy as jnp
from jax import lax
from jax.experimental import pallas as pl
from jax.experimental.pallas import tpu as pltpu
from jax.sharding import PartitionSpec as P

f32 = jnp.float32
bf16 = jnp.bfloat16
Q = 256
LANES = 128
HEAD_DIM = 64
WINDOW = 2
EARLY = 5
HEAD_VMEM = 64 << 20
highest = lax.Precision.HIGHEST
epsilon = 1e-05


def dot_nn(a, b, precision=None):
    return lax.dot_general(a, b, (((1,), (0,)), ((), ())), precision=precision, preferred_element_type=f32)


def dot_nt(a, b, precision=None):
    return lax.dot_general(a, b, (((1,), (1,)), ((), ())), precision=precision, preferred_element_type=f32)


def halves(values):
    high = values.astype(bf16)
    return jnp.concatenate([high, (values - high.astype(f32)).astype(bf16)], axis=1)


def dot_halves(a, values):
    both = dot_nn(a, halves(values))
    return both[:, :LANES] + both[:, LANES:]


def sigmoid(values):
    return 0.5 * jnp.tanh(0.5 * values) + 0.5


def fold_rows(values):
    return jnp.sum(values.reshape(-1, 8, values.shape[-1]), axis=0)


def segment_at(position, lengths_ref):
    total = lengths_ref[0, 0]
    seg = (position >= total).astype(jnp.int32)
    for index in range(1, lengths_ref.shape[1]):
        total = total + lengths_ref[0, index]
        seg = seg + (position >= total).astype(jnp.int32)
    return seg


def tap_mask(start, shift, rows, lengths_ref):
    position = start + lax.broadcasted_iota(jnp.int32, (rows, LANES), 0)
    same = (segment_at(position, lengths_ref) == segment_at(position - shift, lengths_ref)) & (position >= shift)
    return same.astype(f32)


def triangle(start, lengths_ref, transposed):
    first = lax.broadcasted_iota(jnp.int32, (Q, Q), 0)
    second = lax.broadcasted_iota(jnp.int32, (Q, Q), 1)
    same = segment_at(start + first, lengths_ref) == segment_at(start + second, lengths_ref)
    order = (second >= first) if transposed else (first >= second)
    return same & order


def head_columns(cum, step, cum_cols, step_cols):
    lane = lax.broadcasted_iota(jnp.int32, (Q, LANES), 1)
    for head in range(cum_cols.shape[0]):
        cum_cols[head] = jnp.broadcast_to(cum[:, head : head + 1], (Q, LANES))
    for pair in range(step_cols.shape[0]):
        even = jnp.broadcast_to(step[:, 2 * pair : 2 * pair + 1], (Q, LANES))
        odd = jnp.broadcast_to(step[:, 2 * pair + 1 : 2 * pair + 2], (Q, LANES))
        step_cols[pair] = jnp.where(lane < HEAD_DIM, even, odd)


def boundary(start, lengths_ref):
    position = start + lax.broadcasted_iota(jnp.int32, (Q, LANES), 0)
    seg = segment_at(position, lengths_ref)
    last = segment_at(jnp.full((1, LANES), start + Q - 1, jnp.int32), lengths_ref)
    before = segment_at(jnp.full((1, LANES), start - 1, jnp.int32), lengths_ref)
    before = jnp.where(start > 0, before, -1)
    return (seg == last), (seg == before), (last == before)


def softplus(values):
    return jnp.maximum(values, 0.0) + jnp.log1p(jnp.exp(-jnp.abs(values)))


def causal_taps(ext_ref, taps, bias, masks, columns):
    total = taps[3:4] * ext_ref[pl.ds(8, Q), columns]
    for shift in range(1, 4):
        total = total + taps[3 - shift : 4 - shift] * (ext_ref[pl.ds(8 - shift, Q), columns] * masks[shift - 1])
    return total + bias


def chunk_scalars(start, step_in, rate, lengths_ref, causal):
    step = softplus(step_in)
    log_decay = -step * jnp.exp(rate)
    cum = dot_nn(causal, log_decay, highest)
    return step, log_decay, cum


MESH = pl.DeviceIdType.MESH


def greet(groups, slots):
    group, slot = lax.axis_index("dp"), lax.axis_index("tensor")
    barrier = pltpu.get_barrier_semaphore()

    def along_dp(step, nothing):
        pl.semaphore_signal(barrier, inc=1, device_id=(lax.rem(group + step, groups), slot), device_id_type=MESH)
        return nothing

    lax.fori_loop(1, groups, along_dp, 0)
    for step in range(1, slots):
        pl.semaphore_signal(barrier, inc=1, device_id=(group, lax.rem(slot + step, slots)), device_id_type=MESH)
    pl.semaphore_wait(barrier, groups - 1 + slots - 1)


def head_kernel(
    send_run_ref, arrive_from_ref, lengths_ref, tokens, cotangent, wg_hbm, wv_hbm, ws_hbm, wt_hbm, wo_hbm,
    gain_ref, ggain_ref, tapv_ref, biasv_ref, taps_ref, biass_ref, stepb_ref, rate_ref, skip_ref,
    fulltok, fullcot, normed_out, dgate_out, dvalue_out, scaled_out, back_out, keep, out_part,
    dsmall_ref, inv_ref, dot_ref, sumv_ref, sums_ref, sumh_ref,
    wg, wv, ws, wt, wo, ptok, pcot, slots_buf, arr_tok, arr_cot, xbuf, nbuf, kbuf, gate_all, y_all,
    sraw_all, spre_all, stepin_all, states, d_carry, vext, dvext, sext, cum_cols, step_cols, cum_rows, neg_bias,
    scores, d_scores, d_entry, d_leave, acc_step, acc_cum, acc_dot, acc_prod, dsc, dgbuf, dvbuf, scbuf, bbuf, zbuf,
    sq_rows, ex_send, ex_recv, cols, masks, gathers,
    w_sem, in_sem, ts, tr, cs, cr, ags, agr, own_sem, x_sem, n_sem, keep_sem, o_sem, es, er,
):
    groups, slots = lax.axis_size("dp"), lax.axis_size("tensor")
    group, slot = lax.axis_index("dp"), lax.axis_index("tensor")
    runs, run, width = ptok.shape
    chunks = runs * run // Q
    per_chunk = Q // run
    pairs = d_carry.shape[0]
    last = slots - 1
    model = width * slots
    inner_total = wg.shape[1] * slots
    lane = lax.broadcasted_iota(jnp.int32, (Q, LANES), 1)
    first_half = lane < HEAD_DIM

    greet(groups, slots)
    weights = ((wg_hbm, wg), (wv_hbm, wv), (ws_hbm, ws), (wt_hbm, wt), (wo_hbm, wo))

    def weight_load(which):
        return pltpu.make_async_copy(weights[which][0], weights[which][1], w_sem.at[which])

    tok_in = pltpu.make_async_copy(tokens, ptok, in_sem.at[0])
    cot_in = pltpu.make_async_copy(cotangent, pcot, in_sem.at[1])
    tok_in.start()
    cot_in.start()
    for which in range(5):
        weight_load(which).start()

    def row_send(arrive, send_sem, recv_sem, step):
        other = lax.rem(group + step, groups)
        return pltpu.make_async_remote_copy(
            src_ref=slots_buf.at[other], dst_ref=arrive.at[group], send_sem=send_sem.at[other],
            recv_sem=recv_sem.at[group], device_id=(other, slot), device_id_type=MESH,
        )

    def send_rows(source, arrive, send_sem, recv_sem):
        def one(step, nothing):
            other = lax.rem(group + step, groups)
            slots_buf[other] = source[send_run_ref[other]]
            row_send(arrive, send_sem, recv_sem, step).start()
            return nothing

        lax.fori_loop(1, groups, one, 0)
        arrive[group] = source[send_run_ref[group]]

    def take_rows(packed, arrive, send_sem, recv_sem):
        def one(step, nothing):
            source = lax.rem(group + groups - step, groups)
            pltpu.make_async_remote_copy(
                src_ref=arrive.at[source], dst_ref=arrive.at[source], send_sem=send_sem.at[source],
                recv_sem=recv_sem.at[source], device_id=(group, slot), device_id_type=MESH,
            ).wait_recv()
            row_send(arrive, send_sem, recv_sem, step).wait_send()
            return nothing

        lax.fori_loop(1, groups, one, 0)
        for index in range(runs):
            packed[index] = arrive[arrive_from_ref[index]]

    def rows_of(packed, chunk):
        return packed.at[pl.ds(chunk * per_chunk, per_chunk)]

    def gather_push(kind, source, target, chunk, number, shard, to):
        return pltpu.make_async_remote_copy(
            src_ref=source, dst_ref=target.at[chunk, shard], send_sem=ags.at[kind, chunk, number],
            recv_sem=agr.at[kind, chunk, shard], device_id=(group, to), device_id_type=MESH,
        )

    far_to = ((2,), (), (), (1,))
    near_to = ((1,), (0, 2, 3), (3, 1, 0), (2,))

    def gather_direct(kind, packed, target, chunk, me, far):
        first = 0 if far else len(far_to[me])
        return [
            gather_push(kind, rows_of(packed, chunk), target, chunk, first + number, me, to)
            for number, to in enumerate(far_to[me] if far else near_to[me])
        ]

    def gather_forward(kind, target, chunk, me):
        shard, to = (3, 0) if me == 1 else (0, 3)
        return gather_push(kind, target.at[chunk, shard], target, chunk, 3, shard, to)

    def own_copy(kind, packed, target, chunk):
        return pltpu.make_async_copy(rows_of(packed, chunk), target.at[chunk, slot], own_sem.at[kind, chunk])

    def gather_far(kind, packed, target, chunk):
        for me in (0, 3):
            @pl.when(slot == me)
            def _(me=me):
                for copy in gather_direct(kind, packed, target, chunk, me, True):
                    copy.start()

    def gather_near(kind, packed, target, chunk):
        own_copy(kind, packed, target, chunk).start()
        for me in range(slots):
            @pl.when(slot == me)
            def _(me=me):
                for copy in gather_direct(kind, packed, target, chunk, me, False):
                    copy.start()

    def gather_arrived(kind, target, chunk, shard):
        pltpu.make_async_remote_copy(
            src_ref=target.at[chunk, shard], dst_ref=target.at[chunk, shard], send_sem=ags.at[kind, chunk, 0],
            recv_sem=agr.at[kind, chunk, shard], device_id=(group, slot), device_id_type=MESH,
        ).wait_recv()

    def gather_pass(kind, target, chunk):
        for me in (1, 2):
            @pl.when(slot == me)
            def _(me=me):
                gather_arrived(kind, target, chunk, 3 if me == 1 else 0)
                gather_forward(kind, target, chunk, me).start()

    def gather_wait(kind, packed, target, chunk):
        for me in range(slots):
            @pl.when(slot == me)
            def _(me=me):
                for shard in (1, 2) if me in (0, 3) else (0, 2) if me == 1 else (3, 1):
                    gather_arrived(kind, target, chunk, shard)
                if me in (0, 3):
                    gather_arrived(kind, target, chunk, 3 - me)
        own_copy(kind, packed, target, chunk).wait()

    def gather_drain(kind, packed, target):
        for chunk in range(chunks):
            for me in range(slots):
                @pl.when(slot == me)
                def _(me=me):
                    for copy in gather_direct(kind, packed, target, chunk, me, True):
                        copy.wait_send()
                    for copy in gather_direct(kind, packed, target, chunk, me, False):
                        copy.wait_send()
                    if me in (1, 2):
                        gather_forward(kind, target, chunk, me).wait_send()

    def keep_store(chunk, which):
        source = vext.at[pl.ds(8, Q)] if which == 0 else kbuf.at[1]
        return pltpu.make_async_copy(source, keep.at[chunk, which], keep_sem.at[which])

    def keep_load(chunk):
        return pltpu.make_async_copy(keep.at[chunk], kbuf, keep_sem.at[2])

    def normed_store(chunk):
        return pltpu.make_async_copy(nbuf, normed_out.at[chunk], n_sem)

    stores = ((dgbuf, dgate_out), (dvbuf, dvalue_out), (scbuf, scaled_out), (bbuf, back_out), (zbuf, out_part))

    def store(which, chunk):
        return pltpu.make_async_copy(stores[which][0], stores[which][1].at[chunk], o_sem.at[which])

    def x_load(source, chunk):
        return pltpu.make_async_copy(source.at[chunk], xbuf, x_sem)

    def ones_rows(values):
        return dot_nt(jnp.ones((8, LANES), f32), values, highest)

    def prepare(chunk, transposed):
        start = chunk * Q
        can_see = triangle(start, lengths_ref, transposed)
        neg_bias[...] = jnp.where(can_see, 0.0, -1e30)
        row = lax.broadcasted_iota(jnp.int32, (Q, Q), 0)
        col = lax.broadcasted_iota(jnp.int32, (Q, Q), 1)
        step_in = stepin_all[chunk]
        step, log_decay, cum = chunk_scalars(start, step_in, rate_ref[...], lengths_ref, (row >= col).astype(f32))
        cum_rows[...] = cum.T
        head_columns(cum, step, cum_cols, step_cols)
        return log_decay

    tok_in.wait()
    send_rows(ptok, arr_tok, ts, tr)
    states[0] = jnp.zeros_like(states[0])
    vext[pl.ds(0, 8)] = jnp.zeros((8, vext.shape[1]), f32)
    sext[pl.ds(0, 8)] = jnp.zeros((8, sext.shape[1]), f32)
    d_carry[...] = jnp.zeros_like(d_carry)
    dvext[pl.ds(Q, 8)] = jnp.zeros((8, dvext.shape[1]), f32)
    sumv_ref[...] = jnp.zeros_like(sumv_ref)
    sums_ref[...] = jnp.zeros_like(sums_ref)
    sumh_ref[...] = jnp.zeros_like(sumh_ref)
    place = lax.broadcasted_iota(jnp.int32, (2 * LANES, LANES), 1)
    source = lax.broadcasted_iota(jnp.int32, (2 * LANES, LANES), 0)
    source = (lax.rem(source, LANES) >= HEAD_DIM).astype(jnp.int32)
    for pair in range(pairs):
        gathers[pair] = (place == source + 2 * pair).astype(bf16)
    take_rows(ptok, arr_tok, ts, tr)
    gather_far(0, ptok, fulltok, 0)
    gather_near(0, ptok, fulltok, 0)
    gather_far(0, ptok, fulltok, 1)
    cot_in.wait()
    send_rows(pcot, arr_cot, cs, cr)
    for which in range(5):
        weight_load(which).wait()

    def forward_chunk(chunk, nothing):
        start = chunk * Q
        @pl.when(chunk == 0)
        def _():
            gather_pass(0, fulltok, 0)
            gather_near(0, ptok, fulltok, 1)
            gather_far(0, ptok, fulltok, 2)

        gather_wait(0, ptok, fulltok, chunk)
        x_load(fulltok, chunk).start()

        @pl.when(chunk + 2 < chunks)
        def _():
            gather_near(0, ptok, fulltok, chunk + 2)

        @pl.when(chunk + 3 < chunks)
        def _():
            gather_far(0, ptok, fulltok, chunk + 3)

        @pl.when(chunk + 3 == chunks)
        def _():
            take_rows(pcot, arr_cot, cs, cr)

        @pl.when(chunk + 3 >= chunks)
        def _():
            gather_far(1, pcot, fullcot, 2 * chunks - 4 - chunk)

        @pl.when(chunk + 2 >= chunks)
        def _():
            gather_near(1, pcot, fullcot, 2 * chunks - 3 - chunk)

        @pl.when(chunk > 0)
        def _():
            normed_store(chunk - 1).wait()
            keep_store(chunk - 1, 0).wait()
            keep_store(chunk - 1, 1).wait()
            vext[pl.ds(0, 8)] = vext[pl.ds(Q, 8)]
            sext[pl.ds(0, 8)] = sext[pl.ds(Q, 8)]

        x_load(fulltok, chunk).wait()
        squares = jnp.zeros((Q, 1), f32)
        for shard in range(slots):
            wide = xbuf[shard].reshape(Q, width).astype(f32)
            squares = squares + jnp.sum(wide * wide, axis=1, keepdims=True)
        inv = lax.rsqrt(squares * (1.0 / model) + epsilon)
        inv_ref[pl.ds(start, Q)] = inv
        for shard in range(slots):
            wide = xbuf[shard].reshape(Q, width).astype(f32)
            columns = slice(shard * width, (shard + 1) * width)
            nbuf[:, columns] = (wide * inv * gain_ref[:, columns]).astype(bf16)
        normed_store(chunk).start()
        gate_all[chunk] = dot_nn(nbuf[...], wg[...])
        vext[pl.ds(8, Q)] = dot_nn(nbuf[...], wv[...])
        sext[pl.ds(8, Q)] = dot_nn(nbuf[...], ws[...])
        stepin_all[chunk] = dot_nn(nbuf[...], wt[...]) + stepb_ref[...]
        keep_store(chunk, 0).start()
        sraw_all[chunk] = sext[pl.ds(8, Q)]
        prepare(chunk, False)
        for shift in range(1, 4):
            masks[shift - 1] = tap_mask(start, shift, Q, lengths_ref)

        for half in range(2):
            columns = slice(half * LANES, (half + 1) * LANES)
            spre_all[chunk, :, columns] = causal_taps(
                sext, taps_ref[:, columns], biass_ref[:, columns], masks, columns
            )
        spre = spre_all[chunk]
        state_conv = spre * sigmoid(spre)
        entry = state_conv[:, :LANES]
        leave = state_conv[:, LANES:]
        scores[...] = dot_nt(leave, entry, highest)
        entry_t = entry.T.astype(bf16)
        leave_low = leave.astype(bf16)
        @pl.when(chunk + 1 < chunks)
        def _():
            gather_pass(0, fulltok, chunk + 1)

        @pl.when(chunk + 1 == chunks)
        def _():
            gather_pass(1, fullcot, chunk)

        with_last, with_before, through = boundary(start, lengths_ref)
        to_last = with_last.astype(f32)
        from_before = with_before.astype(f32)
        passes = through.astype(f32)
        acc_dot[...] = jnp.zeros_like(acc_dot)

        def one_pair(pair, nothing):
            columns = pl.ds(pl.multiple_of(pair * LANES, LANES), LANES)
            pre = causal_taps(vext, tapv_ref[:, columns], biasv_ref[:, columns], masks, columns)
            kbuf[1, :, columns] = pre
            x = pre * sigmoid(pre)
            weighted = x * step_cols[pair]
            both = halves(weighted)
            results = []
            for half in range(2):
                head = 2 * pair + half
                c_col = cum_cols[head]
                c_row = cum_rows[pl.ds(head, 1), :]
                top = scores[:LANES, :LANES] * jnp.exp(c_col[:LANES] - c_row[:, :LANES] + neg_bias[:LANES, :LANES])
                low_left = scores[LANES:, :LANES] * jnp.exp(c_col[LANES:] - c_row[:, :LANES] + neg_bias[LANES:, :LANES])
                low_right = scores[LANES:, LANES:] * jnp.exp(
                    c_col[LANES:] - c_row[:, LANES:] + neg_bias[LANES:, LANES:]
                )
                upper = dot_nn(top.astype(bf16), both[:LANES])
                lower = dot_nn(jnp.concatenate([low_left, low_right], axis=1).astype(bf16), both)
                out = jnp.concatenate([upper, lower], axis=0)
                results.append(out[:, :LANES] + out[:, LANES:])
            inside = jnp.where(first_half, results[0], results[1])
            cum_pair = jnp.where(first_half, cum_cols[2 * pair], cum_cols[2 * pair + 1])
            cum_last = cum_pair[Q - 1 :]
            held = states[chunk, pair]
            carried = dot_halves(leave_low, held) * (jnp.exp(cum_pair) * from_before)
            y = inside + carried + skip_ref[:, columns] * x
            y_all[chunk, :, columns] = y
            to_end = jnp.exp(cum_last - cum_pair) * to_last
            states[chunk + 1, pair] = held * (jnp.exp(cum_last) * passes) + dot_halves(entry_t, to_end * weighted)
            gate = gate_all[chunk, :, columns]
            gated = y * (gate * sigmoid(gate))
            acc_dot[...] += gated * gated
            return nothing

        lax.fori_loop(0, pairs, one_pair, 0)
        keep_store(chunk, 1).start()
        sq_rows[chunk] = ones_rows(acc_dot[...])

        return nothing

    lax.fori_loop(0, chunks, forward_chunk, 0)
    normed_store(chunks - 1).wait()
    keep_store(chunks - 1, 0).wait()
    keep_store(chunks - 1, 1).wait()
    dsext = sext
    dsext[pl.ds(Q, 8)] = jnp.zeros((8, dsext.shape[1]), f32)

    def send_sums(chunk, step):
        return pltpu.make_async_remote_copy(
            src_ref=ex_send.at[chunk], dst_ref=ex_recv.at[chunk, slots - step], send_sem=es.at[chunk, step],
            recv_sem=er.at[chunk, slots - step], device_id=(group, lax.rem(slot + step, slots)), device_id_type=MESH,
        )

    def products(chunk):
        gather_wait(1, pcot, fullcot, chunk)
        x_load(fullcot, chunk).start()

        @pl.when(chunk >= 2)
        def _():
            gather_near(1, pcot, fullcot, chunk - 2)

        @pl.when(chunk >= 3)
        def _():
            gather_far(1, pcot, fullcot, chunk - 3)

        x_load(fullcot, chunk).wait()
        for half in range(2):
            columns = slice(half * (dsc.shape[1] // 2), (half + 1) * (dsc.shape[1] // 2))
            value = dot_nn(xbuf[0].reshape(Q, width), wo[pl.ds(0, width), columns])
            for shard in range(1, slots):
                value = value + dot_nn(xbuf[shard].reshape(Q, width), wo[pl.ds(shard * width, width), columns])
            dsc[:, columns] = value
        acc_prod[...] = jnp.zeros_like(acc_prod)

        def product(pair, nothing):
            columns = pl.ds(pl.multiple_of(pair * LANES, LANES), LANES)
            gate = gate_all[chunk, :, columns]
            gated = y_all[chunk, :, columns] * (gate * sigmoid(gate))
            acc_prod[...] += dsc[:, columns] * ggain_ref[:, columns] * gated
            return nothing

        lax.fori_loop(0, pairs, product, 0)
        ex_send[chunk, pl.ds(0, 8)] = sq_rows[chunk]
        ex_send[chunk, pl.ds(8, 8)] = ones_rows(acc_prod[...])
        for step in range(1, slots):
            send_sums(chunk, step).start()

    def backward_chunk(index, nothing):
        chunk = chunks - 1 - index
        start = chunk * Q
        keep_load(chunk).start()
        @pl.when(index > 0)
        def _():
            dvext[pl.ds(Q, 8)] = dvext[pl.ds(0, 8)]
            dsext[pl.ds(Q, 8)] = dsext[pl.ds(0, 8)]
            for which in range(5):
                store(which, chunk + 1).wait()

        def later_mask(shift):
            position = start + lax.broadcasted_iota(jnp.int32, (Q, LANES), 0)
            same = segment_at(position, lengths_ref) == segment_at(position + shift, lengths_ref)
            return (same & (position + shift < chunks * Q)).astype(f32)

        log_decay = prepare(chunk, True)
        for shift in range(1, 4):
            masks[shift - 1] = later_mask(shift)
        step_in = stepin_all[chunk]
        spre = spre_all[chunk]
        spre_sig = sigmoid(spre)
        state_conv = spre * spre_sig
        entry = state_conv[:, :LANES]
        leave = state_conv[:, LANES:]
        scores[...] = dot_nt(entry, leave, highest)
        entry_low = entry.astype(bf16)
        leave_t = leave.T.astype(bf16)
        @pl.when(chunk > 0)
        def _():
            gather_pass(1, fullcot, chunk - 1)

        with_last, with_before, through = boundary(start, lengths_ref)
        to_last = with_last.astype(f32)
        from_before = with_before.astype(f32)
        passes = through.astype(f32)
        row_lane = lax.broadcasted_iota(jnp.int32, (Q, LANES), 0)
        for ref in (d_scores, d_entry, d_leave, acc_step, acc_cum, acc_dot):
            ref[...] = jnp.zeros_like(ref)

        sums = ex_send[chunk]
        for step in range(1, slots):
            send_sums(chunk, step).wait()
        for step in range(1, slots):
            sums = sums + ex_recv[chunk, step]
        rms_row = lax.rsqrt(sums[0:1] * (1.0 / inner_total) + epsilon)
        coef_row = rms_row * rms_row * rms_row * sums[8:9] * (1.0 / inner_total)
        cols[0] = jnp.broadcast_to(rms_row, (LANES, Q)).T
        cols[1] = jnp.broadcast_to(coef_row, (LANES, Q)).T
        keep_load(chunk).wait()

        def one_pair(pair, nothing):
            columns = pl.ds(pl.multiple_of(pair * LANES, LANES), LANES)
            rms = cols[0]
            pre = kbuf[1, :, columns]
            pre_sig = sigmoid(pre)
            x = pre * pre_sig
            step_pair = step_cols[pair]
            weighted = x * step_pair
            gate = gate_all[chunk, :, columns]
            gate_sig = sigmoid(gate)
            gate_silu = gate * gate_sig
            y = y_all[chunk, :, columns]
            gated = y * gate_silu
            d_scaled = dsc[:, columns]
            ggain = ggain_ref[:, columns]
            normalized = gated * rms
            scbuf[:, columns] = (normalized * ggain).astype(bf16)
            d_gated = rms * (d_scaled * ggain) - gated * cols[1]
            sumv_ref[pl.ds(0, 8), columns] += fold_rows(d_scaled * normalized)
            d_gate = (d_gated * y * (gate_sig + gate_silu * (1.0 - gate_sig))).astype(bf16)
            dgbuf[:, columns] = d_gate
            acc_dot[...] += d_gate.astype(f32) * gate
            d_y = d_gated * gate_silu
            skip = skip_ref[:, columns]
            sumv_ref[pl.ds(8, 8), columns] += fold_rows(d_y * x)
            y_scan = y - skip * x

            d_y_t = d_y.T.astype(bf16)
            d_y_both = halves(d_y)
            weighted_low = weighted.astype(bf16)
            results = []
            for half in range(2):
                head = 2 * pair + half
                own = jnp.where(first_half if half == 0 else ~first_half, weighted_low, jnp.zeros_like(weighted_low))
                d_m_top = dot_nn(own[:LANES], d_y_t)
                d_m_low = dot_nn(own[LANES:], d_y_t[:, LANES:])
                c_col = cum_cols[head]
                c_row = cum_rows[pl.ds(head, 1), :]
                l_top = jnp.exp(c_row - jnp.concatenate([c_col[:LANES]] * 2, axis=1) + neg_bias[:LANES])
                l_low = jnp.exp(c_row[:, LANES:] - c_col[LANES:] + neg_bias[LANES:, LANES:])
                d_scores[:LANES] += d_m_top * l_top
                d_scores[LANES:, LANES:] += d_m_low * l_low
                m_top = (scores[:LANES] * l_top).astype(bf16)
                m_low = (scores[LANES:, LANES:] * l_low).astype(bf16)
                upper = dot_nn(m_top, d_y_both)
                lower = dot_nn(m_low, d_y_both[LANES:])
                out = jnp.concatenate([upper, lower], axis=0)
                results.append(out[:, :LANES] + out[:, LANES:])
            d_weighted = jnp.where(first_half, results[0], results[1])
            cum_pair = jnp.where(first_half, cum_cols[2 * pair], cum_cols[2 * pair + 1])
            cum_last = cum_pair[Q - 1 :]
            to_end = jnp.exp(cum_last - cum_pair) * to_last
            from_start = jnp.exp(cum_pair) * from_before
            d_state = d_carry[pair]
            held = states[chunk, pair]
            d_weighted = d_weighted + dot_halves(entry_low, d_state) * to_end
            d_entry[...] += dot_nt((to_end * weighted).astype(bf16), d_state.astype(bf16))
            moved = from_start * d_y
            d_leave[...] += dot_nt(moved.astype(bf16), held.astype(bf16))
            state_dot = jnp.sum(states[chunk + 1, pair] * d_state, axis=0, keepdims=True)
            d_carry[pair] = d_state * (jnp.exp(cum_last) * passes) + dot_halves(leave_t, moved)

            to_step = d_weighted * x
            to_cum = d_y * y_scan - to_step * step_pair + jnp.where(row_lane == Q - 1, state_dot, 0.0)
            acc_step[...] += dot_nn(halves(to_step), gathers[pair])
            acc_cum[...] += dot_nn(halves(to_cum), gathers[pair])

            d_x = d_weighted * step_pair + skip * d_y
            d_pre = d_x * (pre_sig + x * (1.0 - pre_sig))
            dvext[pl.ds(0, Q), columns] = d_pre
            sumv_ref[pl.ds(16, 8), columns] += fold_rows(d_pre)
            vraw = kbuf[0, :, columns]
            total = tapv_ref[3:4, columns] * d_pre
            sumv_ref[pl.ds(24, 8), columns] += fold_rows(vraw * d_pre)
            for shift in range(1, 4):
                moved_back = dvext[pl.ds(shift, Q), columns] * masks[shift - 1]
                total = total + tapv_ref[3 - shift : 4 - shift, columns] * moved_back
                sumv_ref[pl.ds(24 + 8 * shift, 8), columns] += fold_rows(vraw * moved_back)
            d_value = total.astype(bf16)
            dvbuf[:, columns] = d_value
            acc_dot[...] += d_value.astype(f32) * vraw
            return nothing

        lax.fori_loop(0, pairs, one_pair, 0)
        for which in range(3):
            store(which, chunk).start()

        @pl.when(chunk > 0)
        def _():
            products(chunk - 1)


        can_see = (neg_bias[...] == 0.0).astype(f32)
        d_log = dot_nn(can_see, acc_cum[...], highest)
        rate = jnp.exp(rate_ref[...])
        d_step_in = (acc_step[...] - d_log * rate) * sigmoid(step_in)
        d_step = d_step_in.astype(bf16)
        dsmall_ref[pl.ds(start, Q), 2 * LANES :] = d_step
        step_raw = step_in - stepb_ref[...]
        acc_dot[...] += jnp.where(lane < 2 * pairs, d_step.astype(f32) * step_raw, 0.0)
        sumh_ref[pl.ds(0, 8)] += fold_rows(d_step_in)
        sumh_ref[pl.ds(8, 8)] += fold_rows(d_log * log_decay)

        d_scores_now = d_scores[...]
        d_b = d_entry[...] + dot_halves(d_scores_now.astype(bf16), leave)
        d_c = d_leave[...] + dot_halves(d_scores_now.T.astype(bf16), entry)
        for half, grad in enumerate((d_b, d_c)):
            columns = slice(half * LANES, (half + 1) * LANES)
            part = spre_sig[:, columns]
            d_pre = grad * (part + state_conv[:, columns] * (1.0 - part))
            dsext[pl.ds(0, Q), columns] = d_pre
            sums_ref[pl.ds(0, 8), columns] += fold_rows(d_pre)
            sraw = sraw_all[chunk, :, columns]
            total = taps_ref[3:4, columns] * d_pre
            sums_ref[pl.ds(8, 8), columns] += fold_rows(sraw * d_pre)
            for shift in range(1, 4):
                moved_back = dsext[pl.ds(shift, Q), columns] * masks[shift - 1]
                total = total + taps_ref[3 - shift : 4 - shift, columns] * moved_back
                sums_ref[pl.ds(8 + 8 * shift, 8), columns] += fold_rows(sraw * moved_back)
            d_state_raw = total.astype(bf16)
            dsmall_ref[pl.ds(start, Q), columns] = d_state_raw
            acc_dot[...] += d_state_raw.astype(f32) * sraw
        dot_ref[chunk] = ones_rows(acc_dot[...])

        for shard in range(slots):
            here = pl.ds(shard * width, width)
            part = dot_nt(dgbuf[...], wg[here]) + dot_nt(dvbuf[...], wv[here])
            part = part + dot_nt(dsmall_ref[pl.ds(start, Q), : 2 * LANES], ws[here]) + dot_nt(d_step, wt[here])
            bbuf[:, shard * width : (shard + 1) * width] = part.astype(bf16)
        store(3, chunk).start()
        for shard in range(slots):
            part = dot_nt(scbuf[...], wo[pl.ds(shard * width, width)])
            zbuf[:, shard * width : (shard + 1) * width] = part.astype(bf16)
        store(4, chunk).start()
        return nothing

    products(chunks - 1)
    lax.fori_loop(0, chunks, backward_chunk, 0)
    for which in range(5):
        store(which, 0).wait()
    gather_drain(0, ptok, fulltok)
    gather_drain(1, pcot, fullcot)


def head(send_run, arrive_from, lengths, tokens, cotangent, wg, wv, ws, wt, wo, small):
    groups, slots = lax.axis_size("dp"), lax.axis_size("tensor")
    runs, run, width = tokens.shape
    rows = runs * run
    chunks, per_chunk = rows // Q, Q // run
    model, inner = wg.shape
    pairs = inner // LANES
    vmem, anywhere, smem = (pl.BlockSpec(memory_space=s) for s in (pltpu.VMEM, pl.ANY, pltpu.SMEM))
    dma = pltpu.SemaphoreType.DMA
    shape = jax.ShapeDtypeStruct
    return pl.pallas_call(
        head_kernel,
        out_shape=[
            shape((chunks, slots, per_chunk, run, width), bf16),
            shape((chunks, slots, per_chunk, run, width), bf16),
            shape((chunks, Q, model), bf16),
            shape((chunks, Q, inner), bf16),
            shape((chunks, Q, inner), bf16),
            shape((chunks, Q, inner), bf16),
            shape((chunks, Q, model), bf16),
            shape((chunks, 2, Q, inner), f32),
            shape((chunks, Q, model), bf16),
            shape((rows, 3 * LANES), bf16),
            shape((rows, 1), f32),
            shape((chunks, 8, Q), f32),
            shape((56, inner), f32),
            shape((40, 2 * LANES), f32),
            shape((16, LANES), f32),
        ],
        in_specs=[smem] * 3 + [anywhere] * 7 + [vmem] * len(small),
        out_specs=[anywhere] * 9 + [vmem] * 6,
        scratch_shapes=[
            pltpu.VMEM(wg.shape, bf16), pltpu.VMEM(wv.shape, bf16), pltpu.VMEM(ws.shape, bf16),
            pltpu.VMEM(wt.shape, bf16), pltpu.VMEM(wo.shape, bf16),
            pltpu.VMEM((runs, run, width), bf16),
            pltpu.VMEM((runs, run, width), bf16),
            pltpu.VMEM((groups, run, width), bf16),
            pltpu.VMEM((groups, run, width), bf16),
            pltpu.VMEM((groups, run, width), bf16),
            pltpu.VMEM((slots, per_chunk, run, width), bf16),
            pltpu.VMEM((Q, model), bf16),
            pltpu.VMEM((2, Q, inner), f32),
            pltpu.VMEM((chunks, Q, inner), f32),
            pltpu.VMEM((chunks, Q, inner), f32),
            pltpu.VMEM((chunks, Q, 2 * LANES), f32),
            pltpu.VMEM((chunks, Q, 2 * LANES), f32),
            pltpu.VMEM((chunks, Q, LANES), f32),
            pltpu.VMEM((chunks + 1, pairs, LANES, LANES), f32),
            pltpu.VMEM((pairs, LANES, LANES), f32),
            pltpu.VMEM((Q + 8, inner), f32),
            pltpu.VMEM((Q + 8, inner), f32),
            pltpu.VMEM((Q + 8, 2 * LANES), f32),
            pltpu.VMEM((2 * pairs, Q, LANES), f32),
            pltpu.VMEM((pairs, Q, LANES), f32),
            pltpu.VMEM((LANES, Q), f32),
            pltpu.VMEM((Q, Q), f32),
            pltpu.VMEM((Q, Q), f32),
            pltpu.VMEM((Q, Q), f32),
            pltpu.VMEM((Q, LANES), f32),
            pltpu.VMEM((Q, LANES), f32),
            pltpu.VMEM((Q, LANES), f32),
            pltpu.VMEM((Q, LANES), f32),
            pltpu.VMEM((Q, LANES), f32),
            pltpu.VMEM((Q, LANES), f32),
            pltpu.VMEM((Q, inner), f32),
            pltpu.VMEM((Q, inner), bf16),
            pltpu.VMEM((Q, inner), bf16),
            pltpu.VMEM((Q, inner), bf16),
            pltpu.VMEM((Q, model), bf16),
            pltpu.VMEM((Q, model), bf16),
            pltpu.VMEM((chunks, 8, Q), f32),
            pltpu.VMEM((chunks, 16, Q), f32),
            pltpu.VMEM((chunks, slots, 16, Q), f32),
            pltpu.VMEM((2, Q, LANES), f32),
            pltpu.VMEM((3, Q, LANES), f32),
            pltpu.VMEM((pairs, 2 * LANES, LANES), bf16),
            dma((5,)), dma((2,)), dma((groups,)), dma((groups,)), dma((groups,)), dma((groups,)),
            dma((2, chunks, 4)), dma((2, chunks, slots)), dma((2, chunks)), dma, dma, dma((3,)), dma((5,)),
            dma((chunks, slots)), dma((chunks, slots)),
        ],
        compiler_params=pltpu.CompilerParams(collective_id=2, has_side_effects=True, vmem_limit_bytes=HEAD_VMEM),
        name="head",
    )(send_run, arrive_from, lengths, tokens, cotangent, wg, wv, ws, wt, wo, *small)


def tail_kernel(
    back_run_ref, return_from_ref, out_part, back_part, normed, tokens, cotangent, scaled, d_gate, d_value,
    row_dot_ref, inv_ref, gain_ref, small_ref, small_z_ref, dsmall_ref,
    layer_ref, tgrad_ref, small_out, ngain_out, share0, share1, share2, state_out, step_out,
    z_recv, z_comb, z_own, z_mix, ptok, pcot, rd_recv, rd_col, row_buf, slots_buf, arrive, left, right, full,
    core_recv, chip_recv, total, sz_recv, small_all, small_recv, ngain_all, ngain_recv,
    thin, thin_core, thin_chip, thin_own, thin_z,
    load_sem, mix_sem, left_sem, right_sem, zs, zr, zc, rds, rdr, szs, szr, sms, smr, ngs, ngr, rs, rr, cs, cr, hs, hr, tcs, ths, thr, tzs, tzr,
):
    groups, slots = lax.axis_size("dp"), lax.axis_size("tensor")
    group, slot = lax.axis_index("dp"), lax.axis_index("tensor")
    jobs = z_recv.shape[0]
    pieces = jobs // 2
    runs, run, width = layer_ref.shape
    rows = runs * run
    piece_run = run // pieces
    chips = groups // 2
    core = lax.rem(group, 2)
    chip = group // 2
    grow = share0.shape[0]
    per_block = 256 // grow
    blocks = full.shape[1] // per_block
    inner = share0.shape[1]
    last = slots - 1

    greet(groups, slots)

    def z_small(source, target, send_sem, recv_sem, step):
        return pltpu.make_async_remote_copy(
            src_ref=source, dst_ref=target.at[slots - step], send_sem=send_sem.at[step],
            recv_sem=recv_sem.at[slots - step], device_id=(group, lax.rem(slot + step, slots)), device_id_type=MESH,
        )

    def send_dot(step):
        return z_small(row_dot_ref, rd_recv, rds, rdr, step)

    def send_state(step):
        return z_small(small_z_ref, sz_recv, szs, szr, step)

    for step in range(1, slots):
        send_state(step).start()
        send_dot(step).start()

    def piece_of(job, shard):
        source = out_part if job < pieces else back_part
        return source.at[:, pl.ds((job % pieces) * piece_run, piece_run), pl.ds(shard * width, width)]

    def landing(job, me, to):
        return z_recv.at[job, me if me < to else me - 1], zr.at[job, me if me < to else me - 1]

    def z_push(job, number, shard, to, source, target, sem):
        return pltpu.make_async_remote_copy(
            src_ref=source, dst_ref=target, send_sem=zs.at[job, number], recv_sem=sem, device_id=(group, to),
            device_id_type=MESH,
        )

    def direct(job, me, early):
        def push(number, to):
            return z_push(job, number, to, to, piece_of(job, to), *landing(job, me, to))

        def to_mix(number, shard, to):
            return z_push(job, number, shard, to, piece_of(job, shard), z_comb.at[job], zc.at[job])

        if me == 0:
            return [to_mix(0, 3, 1)] if early else [push(1, 2), push(2, 1)]
        if me == last:
            return [to_mix(0, 0, 2)] if early else [push(1, 1), push(2, 2)]
        if early:
            return []
        return [push(0, 0), push(1, 2)] if me == 1 else [push(0, 3), push(1, 1)]

    def mixed(job, me):
        to = 3 if me == 1 else 0
        return z_push(job, 2, to, to, z_mix.at[job], *landing(job, me, to))

    def own_load(kind):
        source = back_part if kind else out_part
        return pltpu.make_async_copy(source.at[:, :, pl.ds(slot * width, width)], z_own.at[kind], load_sem.at[kind])

    def mix_load(job, me):
        return pltpu.make_async_copy(piece_of(job, 3 if me == 1 else 0), z_mix.at[job], mix_sem.at[job])

    def shard_load(which):
        source, target = ((tokens, ptok), (cotangent, pcot))[which]
        return pltpu.make_async_copy(source.at[:, slot], target, load_sem.at[2 + which])

    def push(job, early):
        for me in (0, last) if early else range(slots):
            @pl.when(slot == me)
            def _(me=me):
                for copy in direct(job, me, early):
                    copy.start()

    def combine(job):
        for me in (1, 2):
            @pl.when(slot == me)
            def _(me=me):
                mix_load(job, me).wait()
                z_push(job, 2, 0, 0, z_comb.at[job], z_comb.at[job], zc.at[job]).wait_recv()
                both = z_mix[job].astype(f32) + z_comb[job].astype(f32)
                z_mix[job] = both.astype(bf16)
                mixed(job, me).start()

    rights = (scaled, d_gate, d_value)
    shares = (share0, share1, share2)

    def right_load(which):
        return pltpu.make_async_copy(rights[which], right.at[which % 2], right_sem.at[which])

    def left_load(which, block, place):
        if which == 0:
            per_shard = width // 256
            columns = pl.ds(pl.multiple_of(lax.rem(block, per_shard) * 256, 256), 256)
            source = cotangent.at[:, block // per_shard, :, :, columns]
        else:
            source = normed.at[:, :, :, pl.ds(pl.multiple_of(block * 256, 256), 256)]
        return pltpu.make_async_copy(source, left.at[place], left_sem.at[place])

    def grad_blocks(which, begin, end):
        def one(block, nothing):
            place = lax.rem(block, 2)

            @pl.when(block + 1 < blocks)
            def _():
                left_load(which, block + 1, 1 - place).start()

            left_load(which, block, place).wait()
            value = lax.dot_general(
                left[place].reshape(rows, 256), right[which % 2], (((0,), (0,)), ((), ())), preferred_element_type=f32
            )
            full[which % 2, pl.ds(block * per_block, per_block)] = value.reshape(per_block, grow, -1).astype(bf16)
            if which == 1:
                value = lax.dot_general(
                    left[place].reshape(rows, 256), dsmall_ref[...], (((0,), (0,)), ((), ())), preferred_element_type=f32
                )
                thin[pl.ds(block * per_block, per_block)] = value.reshape(per_block, grow, -1)
            return nothing

        lax.fori_loop(begin, end, one, 0)

    partner = group + 1 - 2 * core

    def core_send(which):
        theirs = full.at[which % 2].reshape(chips, 2, grow, inner).at[:, 1 - core]
        return pltpu.make_async_remote_copy(
            src_ref=theirs, dst_ref=core_recv.at[which], send_sem=cs.at[which], recv_sem=cr.at[which],
            device_id=(partner, slot), device_id_type=MESH,
        )

    def chip_send(which, step):
        other = lax.rem(chip + step, chips)
        return pltpu.make_async_remote_copy(
            src_ref=full.at[which % 2, 2 * other + core], dst_ref=chip_recv.at[which, chips - step],
            send_sem=hs.at[which, step], recv_sem=hr.at[which, chips - step], device_id=(2 * other + core, slot),
            device_id_type=MESH,
        )

    def chip_pushes(which):
        core_send(which).wait()

        def one(step, nothing):
            other = lax.rem(chip + step, chips)
            mine = 2 * other + core
            both = full[which % 2, mine].astype(f32) + core_recv[which, other].astype(f32)
            full[which % 2, mine] = both.astype(bf16)
            chip_send(which, step).start()
            return nothing

        lax.fori_loop(1, chips, one, 0)
        shares[which][...] = full[which % 2, group].astype(f32) + core_recv[which, chip].astype(f32)

    def chip_drain(which):
        def drain(step, nothing):
            chip_send(which, step).wait_send()
            return nothing

        lax.fori_loop(1, chips, drain, 0)

    def chip_total(which):
        def one(step, nothing):
            pltpu.make_async_remote_copy(
                src_ref=chip_recv.at[which, step], dst_ref=chip_recv.at[which, step], send_sem=hs.at[which, step],
                recv_sem=hr.at[which, step], device_id=(group, slot), device_id_type=MESH,
            ).wait_recv()
            shares[which][...] += chip_recv[which, step].astype(f32)
            return nothing

        lax.fori_loop(1, chips, one, 0)

    def thin_core_send():
        theirs = thin.reshape(chips, 2, grow, thin.shape[2]).at[:, 1 - core]
        return pltpu.make_async_remote_copy(
            src_ref=theirs, dst_ref=thin_core, send_sem=tcs.at[0], recv_sem=tcs.at[1], device_id=(partner, slot),
            device_id_type=MESH,
        )

    def thin_chip_send(step):
        other = lax.rem(chip + step, chips)
        return pltpu.make_async_remote_copy(
            src_ref=thin.at[2 * other + core], dst_ref=thin_chip.at[chips - step], send_sem=ths.at[step],
            recv_sem=thr.at[chips - step], device_id=(2 * other + core, slot), device_id_type=MESH,
        )

    def thin_pushes():
        thin_core_send().wait()

        def one(step, nothing):
            other = lax.rem(chip + step, chips)
            thin[2 * other + core] = thin[2 * other + core] + thin_core[other]
            thin_chip_send(step).start()
            return nothing

        lax.fori_loop(1, chips, one, 0)
        thin_own[...] = thin[group] + thin_core[chip]

    def thin_z_send(step):
        other = lax.rem(slot + step, slots)
        part = state_out.shape[0]
        return pltpu.make_async_remote_copy(
            src_ref=thin_own.at[pl.ds(other * part, part), pl.ds(0, 2 * LANES)], dst_ref=thin_z.at[slots - step],
            send_sem=tzs.at[step], recv_sem=tzr.at[slots - step], device_id=(group, other), device_id_type=MESH,
        )

    def thin_total():
        def one(step, nothing):
            pltpu.make_async_remote_copy(
                src_ref=thin_chip.at[step], dst_ref=thin_chip.at[step], send_sem=ths.at[step], recv_sem=thr.at[step],
                device_id=(group, slot), device_id_type=MESH,
            ).wait_recv()
            thin_own[...] += thin_chip[step]
            return nothing

        lax.fori_loop(1, chips, one, 0)
        for step in range(1, slots):
            thin_z_send(step).start()
        step_out[...] = thin_own[:, 2 * LANES :]

    def thin_finish():
        part = state_out.shape[0]
        acc = thin_own[pl.ds(slot * part, part), : 2 * LANES]
        for step in range(1, slots):
            thin_z_send(step).wait()
        for step in range(1, slots):
            acc = acc + thin_z[step]
        state_out[...] = acc

        def drain(step, nothing):
            thin_chip_send(step).wait_send()
            return nothing

        lax.fori_loop(1, chips, drain, 0)

    def dp_small(source, target, send_sem, recv_sem, step):
        return pltpu.make_async_remote_copy(
            src_ref=source, dst_ref=target.at[groups - step], send_sem=send_sem.at[step],
            recv_sem=recv_sem.at[groups - step], device_id=(lax.rem(group + step, groups), slot), device_id_type=MESH,
        )

    def dp_small_start(source, target, send_sem, recv_sem):
        def one(step, nothing):
            dp_small(source, target, send_sem, recv_sem, step).start()
            return nothing

        lax.fori_loop(1, groups, one, 0)

    def dp_small_finish(source, target, send_sem, recv_sem, result):
        result[...] = source[...]

        def one(step, nothing):
            pltpu.make_async_remote_copy(
                src_ref=target.at[step], dst_ref=target.at[step], send_sem=send_sem.at[step],
                recv_sem=recv_sem.at[step], device_id=(group, slot), device_id_type=MESH,
            ).wait_recv()
            result[...] += target[step]
            return nothing

        lax.fori_loop(1, groups, one, 0)

        def drain(step, nothing):
            dp_small(source, target, send_sem, recv_sem, step).wait_send()
            return nothing

        lax.fori_loop(1, groups, drain, 0)

    def row_send(job, step):
        other = lax.rem(group + step, groups)
        return pltpu.make_async_remote_copy(
            src_ref=slots_buf.at[job % pieces, other], dst_ref=arrive.at[job, group], send_sem=rs.at[job, other],
            recv_sem=rr.at[job, group], device_id=(other, slot), device_id_type=MESH,
        )

    def rows_drain(job):
        def one(step, nothing):
            row_send(job, step).wait_send()
            return nothing

        lax.fori_loop(1, groups, one, 0)

    def finish(job):
        kind, piece = job // pieces, job % pieces
        here = pl.ds(piece * piece_run, piece_run)
        tall = runs * piece_run
        for me in range(slots):
            @pl.when(slot == me)
            def _(me=me):
                acc = z_own[kind, :, here, :].astype(f32)
                for source in ((1, 2) if me in (0, 3) else tuple(s for s in range(slots) if s != me)):
                    place, sem = landing(job, source, me)
                    z_push(job, 0, 0, 0, place, place, sem).wait_recv()
                    acc = acc + place[...].astype(f32)
                total[...] = acc
        summed = total[...].reshape(tall, width)
        kept = ptok[:, :, here, :].reshape(tall, width).astype(f32)
        if kind == 0:
            result = kept + summed
        else:
            inv = inv_ref[:, here, :].reshape(tall, 1)
            unit = kept * inv
            ngain_all[...] += fold_rows(summed * unit)
            dot_cols = rd_col[:, here, :].reshape(tall, LANES)
            dot_cols = jnp.concatenate([dot_cols] * (width // LANES), axis=1)
            cot = pcot[:, :, here, :].reshape(tall, width).astype(f32)
            result = cot + inv * (summed * gain_ref[...] - unit * dot_cols)
        row_buf[...] = result.astype(bf16).reshape(runs, piece_run, width)

        def fill(step, nothing):
            other = lax.rem(group + step, groups)
            slots_buf[job % pieces, other] = row_buf[back_run_ref[other]]
            row_send(job, step).start()
            return nothing

        if kind == 1:
            rows_drain(job - pieces)
        lax.fori_loop(1, groups, fill, 0)
        arrive[job, group] = row_buf[back_run_ref[group]]

    def rows_wait(kind):
        for job in range(kind * pieces, (kind + 1) * pieces):
            def one(step, nothing, job=job):
                source = lax.rem(group + groups - step, groups)
                pltpu.make_async_remote_copy(
                    src_ref=arrive.at[job, source], dst_ref=arrive.at[job, source], send_sem=rs.at[job, source],
                    recv_sem=rr.at[job, source], device_id=(group, slot), device_id_type=MESH,
                ).wait_recv()
                return nothing

            lax.fori_loop(1, groups, one, 0)

    def rows_take(kind, target):
        for piece in range(pieces):
            for index in range(runs):
                target[index, pl.ds(piece * piece_run, piece_run)] = arrive[kind * pieces + piece, return_from_ref[index]]

    def let_in(job):
        if job < jobs:
            push(job, False)
            combine(job)

    def step_of(job):
        if job + EARLY < jobs:
            push(job + EARLY, True)
        let_in(job + WINDOW)
        finish(job)

    for job in range(min(EARLY, jobs)):
        push(job, True)
    own_load(0).start()
    own_load(1).start()
    shard_load(0).start()
    shard_load(1).start()
    for me in (1, 2):
        @pl.when(slot == me)
        def _(me=me):
            for job in range(jobs):
                mix_load(job, me).start()
    right_load(0).start()
    left_load(0, 0, 0).start()
    right_load(1).start()
    ngain_all[...] = jnp.zeros_like(ngain_all)

    half = blocks // 2
    right_load(0).wait()
    grad_blocks(0, 0, half)
    small_z = small_z_ref[...]
    for step in range(1, slots):
        send_state(step).wait()
    for step in range(1, slots):
        small_z = small_z + sz_recv[step]
    small_all[:, pl.ds(0, inner)] = small_ref[...]
    small_all[:, pl.ds(inner, 2 * LANES)] = small_z
    dp_small_start(small_all, small_recv, sms, smr)
    grad_blocks(0, half, blocks)
    core_send(0).start()
    right_load(2).start()
    for kind in range(2):
        own_load(kind).wait()
        shard_load(kind).wait()
    left_load(1, 0, 0).start()
    push(0, False)
    right_load(1).wait()
    grad_blocks(1, 0, half)
    chip_pushes(0)
    grad_blocks(1, half, blocks)
    core_send(1).start()
    thin_core_send().start()
    left_load(2, 0, 0).start()
    rd_total = row_dot_ref[...]
    for step in range(1, slots):
        send_dot(step).wait()
    for step in range(1, slots):
        rd_total = rd_total + rd_recv[step]
    rd_total = rd_total * (1.0 / (width * slots))
    for block in range(rows // 256):
        piece_row = jnp.broadcast_to(rd_total[0:1, block * 256 : (block + 1) * 256], (LANES, 256))
        count = 256 // run
        rd_col[pl.ds(block * count, count)] = piece_row.T.reshape(count, run, LANES)
    combine(0)
    right_load(2).wait()
    chip_drain(0)
    let_in(1)
    grad_blocks(2, 0, half)
    chip_pushes(1)
    thin_pushes()
    grad_blocks(2, half, blocks)
    core_send(2).start()
    for job in range(2, WINDOW):
        let_in(job)
    for job in range(jobs):
        if job == 1:
            chip_pushes(2)
        step_of(job)
        if job == jobs // 2:
            thin_total()
    dp_small_start(ngain_all, ngain_recv, ngs, ngr)

    rows_wait(0)
    rows_wait(1)
    for job in range(pieces, jobs):
        rows_drain(job)
    rows_take(0, layer_ref)
    rows_take(1, tgrad_ref)
    dp_small_finish(small_all, small_recv, sms, smr, small_out)
    for which in range(3):
        chip_total(which)
    thin_finish()
    chip_drain(1)
    chip_drain(2)
    dp_small_finish(ngain_all, ngain_recv, ngs, ngr, ngain_out)
    for me in range(slots):
        @pl.when(slot == me)
        def _(me=me):
            for job in range(jobs):
                for copy in direct(job, me, True) + direct(job, me, False):
                    copy.wait_send()
                if me in (1, 2):
                    mixed(job, me).wait_send()


def tail(back_run, return_from, out_part, back_part, normed, tokens, cotangent, scaled, d_gate, d_value, row_dot, inv,
         gain, small, small_z, d_small):
    groups, slots = lax.axis_size("dp"), lax.axis_size("tensor")
    runs, run, model = out_part.shape
    width = model // slots
    rows = runs * run
    inner = scaled.shape[1]
    pieces = min(4, run // 16)
    jobs = 2 * pieces
    piece_run = run // pieces
    grow = model // groups
    chips = groups // 2
    vmem, anywhere, smem = (pl.BlockSpec(memory_space=s) for s in (pltpu.VMEM, pl.ANY, pltpu.SMEM))
    dma = pltpu.SemaphoreType.DMA
    shape = jax.ShapeDtypeStruct
    by_chunk = tokens.shape[:1] + tokens.shape[2:]
    part = (runs, piece_run, width)
    return pl.pallas_call(
        tail_kernel,
        out_shape=[
            shape((runs, run, width), bf16), shape((runs, run, width), bf16), shape((8, inner + 2 * LANES), f32),
            shape((8, width), f32),
        ] + [shape((grow, inner), f32)] * 3 + [shape((grow // slots, 2 * LANES), f32), shape((grow, LANES), f32)],
        in_specs=[smem] * 2 + [anywhere] * 8 + [vmem] * 6,
        out_specs=[vmem] * 9,
        scratch_shapes=[
            pltpu.VMEM((jobs, slots - 1) + part, bf16),
            pltpu.VMEM((jobs,) + part, bf16),
            pltpu.VMEM((2, runs, run, width), bf16),
            pltpu.VMEM((jobs,) + part, bf16),
            pltpu.VMEM(by_chunk, bf16),
            pltpu.VMEM(by_chunk, bf16),
            pltpu.VMEM((slots, 8, rows), f32),
            pltpu.VMEM((runs, run, LANES), f32),
            pltpu.VMEM(part, bf16),
            pltpu.VMEM((pieces, groups, piece_run, width), bf16),
            pltpu.VMEM((jobs, groups, piece_run, width), bf16),
            pltpu.VMEM((2,) + by_chunk[:-1] + (256,), bf16),
            pltpu.VMEM((2, rows, inner), bf16),
            pltpu.VMEM((2, groups, grow, inner), bf16),
            pltpu.VMEM((3, chips, grow, inner), bf16),
            pltpu.VMEM((3, chips, grow, inner), bf16),
            pltpu.VMEM(part, f32),
            pltpu.VMEM((slots, 8, 2 * LANES), f32),
            pltpu.VMEM((8, inner + 2 * LANES), f32),
            pltpu.VMEM((groups, 8, inner + 2 * LANES), f32),
            pltpu.VMEM((8, width), f32),
            pltpu.VMEM((groups, 8, width), f32),
            pltpu.VMEM((groups, grow, 3 * LANES), f32),
            pltpu.VMEM((chips, grow, 3 * LANES), f32),
            pltpu.VMEM((chips, grow, 3 * LANES), f32),
            pltpu.VMEM((grow, 3 * LANES), f32),
            pltpu.VMEM((slots, grow // slots, 2 * LANES), f32),
            dma((4,)), dma((jobs,)), dma((2,)), dma((3,)),
            dma((jobs, 3)), dma((jobs, slots - 1)), dma((jobs,)),
            dma((slots,)), dma((slots,)), dma((slots,)), dma((slots,)),
            dma((groups,)), dma((groups,)), dma((groups,)), dma((groups,)),
            dma((jobs, groups)), dma((jobs, groups)),
            dma((3,)), dma((3,)), dma((3, chips)), dma((3, chips)),
            dma((2,)), dma((chips,)), dma((chips,)), dma((slots,)), dma((slots,)),
        ],
        compiler_params=pltpu.CompilerParams(collective_id=3, has_side_effects=True, vmem_limit_bytes=64 << 20),
        name="tail",
    )(back_run, return_from, out_part, back_part, normed, tokens, cotangent, scaled, d_gate, d_value, row_dot, inv, gain,
      small, small_z, d_small)


def pad_heads(values):
    return jnp.pad(values, ((0, 0), (0, LANES - values.shape[1])))


def per_device(
    tokens, cotangent, norm_gain, gate_proj, value_proj, state_proj, step_proj, conv_value, conv_value_bias,
    conv_state, conv_state_bias, step_bias, decay_log, skip_gain, gate_gain, out_proj, token_order, lengths,
):
    groups = lax.axis_size("dp")
    group = lax.axis_index("dp")
    slots = lax.axis_size("tensor")
    slot = lax.axis_index("tensor")
    rows, width = tokens.shape
    model = width * slots
    inner = gate_proj.shape[1]
    heads = step_bias.shape[0]
    run = 2 * rows // groups
    runs = rows // run

    source_run = token_order.reshape(groups, runs, run)[:, :, 0] // run
    source_group = source_run // runs
    from_here = source_group == group
    send_run = jnp.sum(jnp.where(from_here, source_run % runs, 0), axis=1)
    arrive_from = lax.dynamic_index_in_dim(source_group, group, 0, keepdims=False)
    every = jnp.arange(groups, dtype=jnp.int32)
    back_run = jnp.sum(
        jnp.where(arrive_from[None, :] == every[:, None], jnp.arange(runs, dtype=jnp.int32)[None, :], 0), axis=1
    )
    local_run = group * runs + jnp.arange(runs, dtype=jnp.int32)
    return_from = jnp.sum(
        jnp.where(source_run[None] == local_run[:, None, None], every[None, :, None], 0), axis=(1, 2)
    )

    def cut(values):
        return values.reshape(runs, run, values.shape[1])

    gain_full = norm_gain.astype(f32)
    small = (
        gain_full[None], gate_gain.astype(f32)[None], conv_value.astype(f32), conv_value_bias.astype(f32)[None],
        conv_state.astype(f32), conv_state_bias.astype(f32)[None], pad_heads(step_bias[None]),
        pad_heads(decay_log[None]), jnp.repeat(skip_gain, HEAD_DIM)[None],
    )
    (full_tokens, full_cotangent, normed, d_gate, d_value, scaled, back_partial, _, out_partial, d_small,
     inv_rms, row_dot, sumv, sums, sumh) = head(
        send_run, arrive_from, lengths, cut(tokens), cut(cotangent), gate_proj, value_proj, state_proj,
        pad_heads(step_proj), out_proj, small,
    )
    row_dot = row_dot.transpose(1, 0, 2).reshape(8, rows)
    normed_cut = normed.reshape(full_tokens.shape[0], full_tokens.shape[2], run, model)
    d_gate, d_value, scaled, back_partial, out_partial = (
        v.reshape(rows, v.shape[2]) for v in (d_gate, d_value, scaled, back_partial, out_partial)
    )
    gain_share = lax.dynamic_slice_in_dim(gain_full, slot * width, width, 0)
    by_head = jnp.pad(sumh.reshape(2, 8, LANES).sum(1).reshape(1, 2 * LANES), ((0, 0), (0, inner - 2 * LANES)))
    small = jnp.concatenate([sumv.reshape(7, 8, inner).sum(1), by_head])
    small_z = jnp.pad(sums.reshape(5, 8, 2 * LANES).sum(1), ((0, 3), (0, 0)))
    layer_output, tokens_grad, small, norm_gain_rows, out_grad_share, gate_share, value_share, state_share, step_share = tail(
        back_run, return_from, cut(out_partial), cut(back_partial), normed_cut, full_tokens, full_cotangent, scaled,
        d_gate, d_value, row_dot, cut(inv_rms), gain_share[None], small, small_z, d_small,
    )
    state_sums = small[:, inner:]
    return (
        layer_output.reshape(rows, width),
        tokens_grad.reshape(rows, width),
        jnp.sum(norm_gain_rows, axis=0),
        gate_share,
        value_share,
        state_share,
        step_share[:, :heads],
        small[6:2:-1, :inner],
        small[2, :inner],
        state_sums[4:0:-1],
        state_sums[0],
        small[7, :heads],
        small[7, LANES : LANES + heads],
        jnp.sum(small[1, :inner].reshape(heads, HEAD_DIM), axis=1),
        small[0, :inner],
        out_grad_share,
    )


def solution(mesh):
    across = P(None, "tensor")
    both = P("dp", "tensor")
    heads = P("tensor")
    return jax.shard_map(
        per_device,
        mesh=mesh,
        in_specs=(
            both, both, P(), across, across, P(), across, across, heads, P(), P(), heads, heads, heads, heads, across,
            P(), P("dp", None),
        ),
        out_specs=(
            both, both, heads, both, both, P(("dp", "tensor"), None), both, across, heads, P(), P(), heads, heads, heads,
            heads, both,
        ),
        check_vma=False,
    )
```

```python
import jax
import jax.numpy as jnp
from jax import lax
from jax.experimental import pallas as pl
from jax.experimental.pallas import tpu as pltpu
from jax.sharding import PartitionSpec as P

f32 = jnp.float32
bf16 = jnp.bfloat16
Q = 256
LANES = 128
HEAD_DIM = 64
WINDOW = 2
EARLY = 5
HEAD_VMEM = 64 << 20
highest = lax.Precision.HIGHEST
epsilon = 1e-05


def dot_nn(a, b, precision=None):
    return lax.dot_general(a, b, (((1,), (0,)), ((), ())), precision=precision, preferred_element_type=f32)


def dot_nt(a, b, precision=None):
    return lax.dot_general(a, b, (((1,), (1,)), ((), ())), precision=precision, preferred_element_type=f32)


def halves(values):
    high = values.astype(bf16)
    return jnp.concatenate([high, (values - high.astype(f32)).astype(bf16)], axis=1)


def dot_halves(a, values):
    both = dot_nn(a, halves(values))
    return both[:, :LANES] + both[:, LANES:]


def sigmoid(values):
    return 0.5 * jnp.tanh(0.5 * values) + 0.5


def fold_rows(values):
    return jnp.sum(values.reshape(-1, 8, values.shape[-1]), axis=0)


def segment_at(position, lengths_ref):
    total = lengths_ref[0, 0]
    seg = (position >= total).astype(jnp.int32)
    for index in range(1, lengths_ref.shape[1]):
        total = total + lengths_ref[0, index]
        seg = seg + (position >= total).astype(jnp.int32)
    return seg


def tap_mask(start, shift, rows, lengths_ref):
    position = start + lax.broadcasted_iota(jnp.int32, (rows, LANES), 0)
    same = (segment_at(position, lengths_ref) == segment_at(position - shift, lengths_ref)) & (position >= shift)
    return same.astype(f32)


def triangle(start, lengths_ref, transposed):
    first = lax.broadcasted_iota(jnp.int32, (Q, Q), 0)
    second = lax.broadcasted_iota(jnp.int32, (Q, Q), 1)
    same = segment_at(start + first, lengths_ref) == segment_at(start + second, lengths_ref)
    order = (second >= first) if transposed else (first >= second)
    return same & order


def head_columns(cum, step, cum_cols, step_cols):
    lane = lax.broadcasted_iota(jnp.int32, (Q, LANES), 1)
    for head in range(cum_cols.shape[0]):
        cum_cols[head] = jnp.broadcast_to(cum[:, head : head + 1], (Q, LANES))
    for pair in range(step_cols.shape[0]):
        even = jnp.broadcast_to(step[:, 2 * pair : 2 * pair + 1], (Q, LANES))
        odd = jnp.broadcast_to(step[:, 2 * pair + 1 : 2 * pair + 2], (Q, LANES))
        step_cols[pair] = jnp.where(lane < HEAD_DIM, even, odd)


def boundary(start, lengths_ref):
    position = start + lax.broadcasted_iota(jnp.int32, (Q, LANES), 0)
    seg = segment_at(position, lengths_ref)
    last = segment_at(jnp.full((1, LANES), start + Q - 1, jnp.int32), lengths_ref)
    before = segment_at(jnp.full((1, LANES), start - 1, jnp.int32), lengths_ref)
    before = jnp.where(start > 0, before, -1)
    return (seg == last), (seg == before), (last == before)


def softplus(values):
    return jnp.maximum(values, 0.0) + jnp.log1p(jnp.exp(-jnp.abs(values)))


def causal_taps(ext_ref, taps, bias, masks, columns):
    total = taps[3:4] * ext_ref[pl.ds(8, Q), columns]
    for shift in range(1, 4):
        total = total + taps[3 - shift : 4 - shift] * (ext_ref[pl.ds(8 - shift, Q), columns] * masks[shift - 1])
    return total + bias


def chunk_scalars(start, step_in, rate, lengths_ref, causal):
    step = softplus(step_in)
    log_decay = -step * jnp.exp(rate)
    cum = dot_nn(causal, log_decay, highest)
    return step, log_decay, cum


MESH = pl.DeviceIdType.MESH


def greet(groups, slots):
    group, slot = lax.axis_index("dp"), lax.axis_index("tensor")
    barrier = pltpu.get_barrier_semaphore()

    def along_dp(step, nothing):
        pl.semaphore_signal(barrier, inc=1, device_id=(lax.rem(group + step, groups), slot), device_id_type=MESH)
        return nothing

    lax.fori_loop(1, groups, along_dp, 0)
    for step in range(1, slots):
        pl.semaphore_signal(barrier, inc=1, device_id=(group, lax.rem(slot + step, slots)), device_id_type=MESH)
    pl.semaphore_wait(barrier, groups - 1 + slots - 1)


def head_kernel(
    send_run_ref, arrive_from_ref, lengths_ref, tokens, cotangent, wg_hbm, wv_hbm, ws_hbm, wt_hbm, wo_hbm,
    tapv_ref, taps_ref, heads_ref, small_ref,
    fulltok, fullcot, normed_out, dgate_out, dvalue_out, scaled_out, back_out, keep, out_part,
    dsmall_ref, inv_ref, dot_ref, sumv_ref, sums_ref, sumh_ref,
    wg, wv, ws, wt, wo, ptok, pcot, slots_buf, arr_tok, arr_cot, xbuf, nbuf, kbuf, gate_all, y_all,
    sraw_all, spre_all, stepin_all, states, d_carry, vext, dvext, sext, cum_cols, step_cols, cum_rows, neg_bias,
    scores, d_scores, d_entry, d_leave, acc_step, acc_cum, acc_dot, acc_prod, dsc, dgbuf, dvbuf, scbuf, bbuf, zbuf,
    sq_rows, ex_send, ex_recv, cols, masks, gathers,
    w_sem, in_sem, ts, tr, cs, cr, ags, agr, own_sem, x_sem, n_sem, keep_sem, o_sem, es, er,
):
    groups, slots = lax.axis_size("dp"), lax.axis_size("tensor")
    group, slot = lax.axis_index("dp"), lax.axis_index("tensor")
    runs, run, width = ptok.shape
    chunks = runs * run // Q
    per_chunk = Q // run
    pairs = d_carry.shape[0]
    gain_ref, ggain_ref, biasv_ref, biass_ref, skip_ref = (small_ref.at[row] for row in range(5))
    stepb_ref, rate_ref = heads_ref.at[0], heads_ref.at[1]
    last = slots - 1
    model = width * slots
    inner_total = wg.shape[1] * slots
    lane = lax.broadcasted_iota(jnp.int32, (Q, LANES), 1)
    first_half = lane < HEAD_DIM

    greet(groups, slots)
    weights = ((wg_hbm, wg), (wv_hbm, wv), (ws_hbm, ws), (wt_hbm, wt), (wo_hbm, wo))

    def weight_load(which):
        return pltpu.make_async_copy(weights[which][0], weights[which][1], w_sem.at[which])

    tok_in = pltpu.make_async_copy(tokens, ptok, in_sem.at[0])
    cot_in = pltpu.make_async_copy(cotangent, pcot, in_sem.at[1])
    tok_in.start()
    cot_in.start()
    for which in range(5):
        weight_load(which).start()

    def row_send(arrive, send_sem, recv_sem, step):
        other = lax.rem(group + step, groups)
        return pltpu.make_async_remote_copy(
            src_ref=slots_buf.at[other], dst_ref=arrive.at[group], send_sem=send_sem.at[other],
            recv_sem=recv_sem.at[group], device_id=(other, slot), device_id_type=MESH,
        )

    def send_rows(source, arrive, send_sem, recv_sem):
        def one(step, nothing):
            other = lax.rem(group + step, groups)
            slots_buf[other] = source[send_run_ref[other]]
            row_send(arrive, send_sem, recv_sem, step).start()
            return nothing

        lax.fori_loop(1, groups, one, 0)
        arrive[group] = source[send_run_ref[group]]

    def take_rows(packed, arrive, send_sem, recv_sem):
        def one(step, nothing):
            source = lax.rem(group + groups - step, groups)
            pltpu.make_async_remote_copy(
                src_ref=arrive.at[source], dst_ref=arrive.at[source], send_sem=send_sem.at[source],
                recv_sem=recv_sem.at[source], device_id=(group, slot), device_id_type=MESH,
            ).wait_recv()
            row_send(arrive, send_sem, recv_sem, step).wait_send()
            return nothing

        lax.fori_loop(1, groups, one, 0)
        for index in range(runs):
            packed[index] = arrive[arrive_from_ref[index]]

    def rows_of(packed, chunk):
        return packed.at[pl.ds(chunk * per_chunk, per_chunk)]

    def gather_push(kind, source, target, chunk, number, shard, to):
        return pltpu.make_async_remote_copy(
            src_ref=source, dst_ref=target.at[chunk, shard], send_sem=ags.at[kind, chunk, number],
            recv_sem=agr.at[kind, chunk, shard], device_id=(group, to), device_id_type=MESH,
        )

    far_to = ((2,), (), (), (1,))
    near_to = ((1,), (0, 2, 3), (3, 1, 0), (2,))

    def gather_direct(kind, packed, target, chunk, me, far):
        first = 0 if far else len(far_to[me])
        return [
            gather_push(kind, rows_of(packed, chunk), target, chunk, first + number, me, to)
            for number, to in enumerate(far_to[me] if far else near_to[me])
        ]

    def gather_forward(kind, target, chunk, me):
        shard, to = (3, 0) if me == 1 else (0, 3)
        return gather_push(kind, target.at[chunk, shard], target, chunk, 3, shard, to)

    def own_copy(kind, packed, target, chunk):
        return pltpu.make_async_copy(rows_of(packed, chunk), target.at[chunk, slot], own_sem.at[kind, chunk])

    def gather_far(kind, packed, target, chunk):
        for me in (0, 3):
            @pl.when(slot == me)
            def _(me=me):
                for copy in gather_direct(kind, packed, target, chunk, me, True):
                    copy.start()

    def gather_near(kind, packed, target, chunk):
        own_copy(kind, packed, target, chunk).start()
        for me in range(slots):
            @pl.when(slot == me)
            def _(me=me):
                for copy in gather_direct(kind, packed, target, chunk, me, False):
                    copy.start()

    def gather_arrived(kind, target, chunk, shard):
        pltpu.make_async_remote_copy(
            src_ref=target.at[chunk, shard], dst_ref=target.at[chunk, shard], send_sem=ags.at[kind, chunk, 0],
            recv_sem=agr.at[kind, chunk, shard], device_id=(group, slot), device_id_type=MESH,
        ).wait_recv()

    def gather_pass(kind, target, chunk):
        for me in (1, 2):
            @pl.when(slot == me)
            def _(me=me):
                gather_arrived(kind, target, chunk, 3 if me == 1 else 0)
                gather_forward(kind, target, chunk, me).start()

    def gather_wait(kind, packed, target, chunk):
        for me in range(slots):
            @pl.when(slot == me)
            def _(me=me):
                for shard in (1, 2) if me in (0, 3) else (0, 2) if me == 1 else (3, 1):
                    gather_arrived(kind, target, chunk, shard)
                if me in (0, 3):
                    gather_arrived(kind, target, chunk, 3 - me)
        own_copy(kind, packed, target, chunk).wait()

    def gather_drain(kind, packed, target):
        for chunk in range(chunks):
            for me in range(slots):
                @pl.when(slot == me)
                def _(me=me):
                    for copy in gather_direct(kind, packed, target, chunk, me, True):
                        copy.wait_send()
                    for copy in gather_direct(kind, packed, target, chunk, me, False):
                        copy.wait_send()
                    if me in (1, 2):
                        gather_forward(kind, target, chunk, me).wait_send()

    def keep_store(chunk, which):
        source = vext.at[pl.ds(8, Q)] if which == 0 else kbuf.at[1]
        return pltpu.make_async_copy(source, keep.at[chunk, which], keep_sem.at[which])

    def keep_load(chunk):
        return pltpu.make_async_copy(keep.at[chunk], kbuf, keep_sem.at[2])

    def normed_store(chunk):
        return pltpu.make_async_copy(nbuf, normed_out.at[chunk], n_sem)

    stores = ((dgbuf, dgate_out), (dvbuf, dvalue_out), (scbuf, scaled_out), (bbuf, back_out), (zbuf, out_part))

    def store(which, chunk):
        return pltpu.make_async_copy(stores[which][0], stores[which][1].at[chunk], o_sem.at[which])

    def x_load(source, chunk):
        return pltpu.make_async_copy(source.at[chunk], xbuf, x_sem)

    def ones_rows(values):
        return dot_nt(jnp.ones((8, LANES), f32), values, highest)

    def prepare(chunk, transposed):
        start = chunk * Q
        can_see = triangle(start, lengths_ref, transposed)
        neg_bias[...] = jnp.where(can_see, 0.0, -1e30)
        row = lax.broadcasted_iota(jnp.int32, (Q, Q), 0)
        col = lax.broadcasted_iota(jnp.int32, (Q, Q), 1)
        step_in = stepin_all[chunk]
        step, log_decay, cum = chunk_scalars(start, step_in, rate_ref[...], lengths_ref, (row >= col).astype(f32))
        cum_rows[...] = cum.T
        head_columns(cum, step, cum_cols, step_cols)
        return log_decay

    tok_in.wait()
    send_rows(ptok, arr_tok, ts, tr)
    states[0] = jnp.zeros_like(states[0])
    vext[pl.ds(0, 8)] = jnp.zeros((8, vext.shape[1]), f32)
    sext[pl.ds(0, 8)] = jnp.zeros((8, sext.shape[1]), f32)
    d_carry[...] = jnp.zeros_like(d_carry)
    dvext[pl.ds(Q, 8)] = jnp.zeros((8, dvext.shape[1]), f32)
    sumv_ref[...] = jnp.zeros_like(sumv_ref)
    sums_ref[...] = jnp.zeros_like(sums_ref)
    sumh_ref[...] = jnp.zeros_like(sumh_ref)
    place = lax.broadcasted_iota(jnp.int32, (2 * LANES, LANES), 1)
    source = lax.broadcasted_iota(jnp.int32, (2 * LANES, LANES), 0)
    source = (lax.rem(source, LANES) >= HEAD_DIM).astype(jnp.int32)
    for pair in range(pairs):
        gathers[pair] = (place == source + 2 * pair).astype(bf16)
    take_rows(ptok, arr_tok, ts, tr)
    gather_far(0, ptok, fulltok, 0)
    gather_near(0, ptok, fulltok, 0)
    gather_far(0, ptok, fulltok, 1)
    cot_in.wait()
    send_rows(pcot, arr_cot, cs, cr)
    for which in range(5):
        weight_load(which).wait()

    def forward_chunk(chunk, nothing):
        start = chunk * Q
        @pl.when(chunk == 0)
        def _():
            gather_pass(0, fulltok, 0)
            gather_near(0, ptok, fulltok, 1)
            gather_far(0, ptok, fulltok, 2)

        gather_wait(0, ptok, fulltok, chunk)
        x_load(fulltok, chunk).start()

        @pl.when(chunk + 2 < chunks)
        def _():
            gather_near(0, ptok, fulltok, chunk + 2)

        @pl.when(chunk + 3 < chunks)
        def _():
            gather_far(0, ptok, fulltok, chunk + 3)

        @pl.when(chunk + 3 == chunks)
        def _():
            take_rows(pcot, arr_cot, cs, cr)

        @pl.when(chunk + 3 >= chunks)
        def _():
            gather_far(1, pcot, fullcot, 2 * chunks - 4 - chunk)

        @pl.when(chunk + 2 >= chunks)
        def _():
            gather_near(1, pcot, fullcot, 2 * chunks - 3 - chunk)

        @pl.when(chunk > 0)
        def _():
            normed_store(chunk - 1).wait()
            keep_store(chunk - 1, 0).wait()
            keep_store(chunk - 1, 1).wait()
            vext[pl.ds(0, 8)] = vext[pl.ds(Q, 8)]
            sext[pl.ds(0, 8)] = sext[pl.ds(Q, 8)]

        x_load(fulltok, chunk).wait()
        squares = jnp.zeros((Q, 1), f32)
        for shard in range(slots):
            wide = xbuf[shard].reshape(Q, width).astype(f32)
            squares = squares + jnp.sum(wide * wide, axis=1, keepdims=True)
        inv = lax.rsqrt(squares * (1.0 / model) + epsilon)
        inv_ref[pl.ds(start, Q)] = inv
        for shard in range(slots):
            wide = xbuf[shard].reshape(Q, width).astype(f32)
            columns = slice(shard * width, (shard + 1) * width)
            nbuf[:, columns] = (wide * inv * gain_ref[:, columns]).astype(bf16)
        normed_store(chunk).start()
        gate_all[chunk] = dot_nn(nbuf[...], wg[...])
        vext[pl.ds(8, Q)] = dot_nn(nbuf[...], wv[...])
        sext[pl.ds(8, Q)] = dot_nn(nbuf[...], ws[...])
        stepin_all[chunk] = dot_nn(nbuf[...], wt[...]) + stepb_ref[...]
        keep_store(chunk, 0).start()
        sraw_all[chunk] = sext[pl.ds(8, Q)]
        prepare(chunk, False)
        for shift in range(1, 4):
            masks[shift - 1] = tap_mask(start, shift, Q, lengths_ref)

        for half in range(2):
            columns = slice(half * LANES, (half + 1) * LANES)
            spre_all[chunk, :, columns] = causal_taps(
                sext, taps_ref[:, columns], biass_ref[:, columns], masks, columns
            )
        spre = spre_all[chunk]
        state_conv = spre * sigmoid(spre)
        entry = state_conv[:, :LANES]
        leave = state_conv[:, LANES:]
        scores[...] = dot_nt(leave, entry, highest)
        entry_t = entry.T.astype(bf16)
        leave_low = leave.astype(bf16)
        @pl.when(chunk + 1 < chunks)
        def _():
            gather_pass(0, fulltok, chunk + 1)

        @pl.when(chunk + 1 == chunks)
        def _():
            gather_pass(1, fullcot, chunk)

        with_last, with_before, through = boundary(start, lengths_ref)
        to_last = with_last.astype(f32)
        from_before = with_before.astype(f32)
        passes = through.astype(f32)
        acc_dot[...] = jnp.zeros_like(acc_dot)

        def one_pair(pair, nothing):
            columns = pl.ds(pl.multiple_of(pair * LANES, LANES), LANES)
            pre = causal_taps(vext, tapv_ref[:, columns], biasv_ref[:, columns], masks, columns)
            kbuf[1, :, columns] = pre
            x = pre * sigmoid(pre)
            weighted = x * step_cols[pair]
            both = halves(weighted)
            results = []
            for half in range(2):
                head = 2 * pair + half
                c_col = cum_cols[head]
                c_row = cum_rows[pl.ds(head, 1), :]
                top = scores[:LANES, :LANES] * jnp.exp(c_col[:LANES] - c_row[:, :LANES] + neg_bias[:LANES, :LANES])
                low_left = scores[LANES:, :LANES] * jnp.exp(c_col[LANES:] - c_row[:, :LANES] + neg_bias[LANES:, :LANES])
                low_right = scores[LANES:, LANES:] * jnp.exp(
                    c_col[LANES:] - c_row[:, LANES:] + neg_bias[LANES:, LANES:]
                )
                upper = dot_nn(top.astype(bf16), both[:LANES])
                lower = dot_nn(jnp.concatenate([low_left, low_right], axis=1).astype(bf16), both)
                out = jnp.concatenate([upper, lower], axis=0)
                results.append(out[:, :LANES] + out[:, LANES:])
            inside = jnp.where(first_half, results[0], results[1])
            cum_pair = jnp.where(first_half, cum_cols[2 * pair], cum_cols[2 * pair + 1])
            cum_last = cum_pair[Q - 1 :]
            held = states[chunk, pair]
            carried = dot_halves(leave_low, held) * (jnp.exp(cum_pair) * from_before)
            y = inside + carried + skip_ref[:, columns] * x
            y_all[chunk, :, columns] = y
            to_end = jnp.exp(cum_last - cum_pair) * to_last
            states[chunk + 1, pair] = held * (jnp.exp(cum_last) * passes) + dot_halves(entry_t, to_end * weighted)
            gate = gate_all[chunk, :, columns]
            gated = y * (gate * sigmoid(gate))
            acc_dot[...] += gated * gated
            return nothing

        lax.fori_loop(0, pairs, one_pair, 0)
        keep_store(chunk, 1).start()
        sq_rows[chunk] = ones_rows(acc_dot[...])

        return nothing

    lax.fori_loop(0, chunks, forward_chunk, 0)
    normed_store(chunks - 1).wait()
    keep_store(chunks - 1, 0).wait()
    keep_store(chunks - 1, 1).wait()
    dsext = sext
    dsext[pl.ds(Q, 8)] = jnp.zeros((8, dsext.shape[1]), f32)

    def send_sums(chunk, step):
        return pltpu.make_async_remote_copy(
            src_ref=ex_send.at[chunk], dst_ref=ex_recv.at[chunk, slots - step], send_sem=es.at[chunk, step],
            recv_sem=er.at[chunk, slots - step], device_id=(group, lax.rem(slot + step, slots)), device_id_type=MESH,
        )

    def products(chunk):
        gather_wait(1, pcot, fullcot, chunk)
        x_load(fullcot, chunk).start()

        @pl.when(chunk >= 2)
        def _():
            gather_near(1, pcot, fullcot, chunk - 2)

        @pl.when(chunk >= 3)
        def _():
            gather_far(1, pcot, fullcot, chunk - 3)

        x_load(fullcot, chunk).wait()
        for half in range(2):
            columns = slice(half * (dsc.shape[1] // 2), (half + 1) * (dsc.shape[1] // 2))
            value = dot_nn(xbuf[0].reshape(Q, width), wo[pl.ds(0, width), columns])
            for shard in range(1, slots):
                value = value + dot_nn(xbuf[shard].reshape(Q, width), wo[pl.ds(shard * width, width), columns])
            dsc[:, columns] = value
        acc_prod[...] = jnp.zeros_like(acc_prod)

        def product(pair, nothing):
            columns = pl.ds(pl.multiple_of(pair * LANES, LANES), LANES)
            gate = gate_all[chunk, :, columns]
            gated = y_all[chunk, :, columns] * (gate * sigmoid(gate))
            acc_prod[...] += dsc[:, columns] * ggain_ref[:, columns] * gated
            return nothing

        lax.fori_loop(0, pairs, product, 0)
        ex_send[chunk, pl.ds(0, 8)] = sq_rows[chunk]
        ex_send[chunk, pl.ds(8, 8)] = ones_rows(acc_prod[...])
        for step in range(1, slots):
            send_sums(chunk, step).start()

    def backward_chunk(index, nothing):
        chunk = chunks - 1 - index
        start = chunk * Q
        keep_load(chunk).start()
        @pl.when(index > 0)
        def _():
            dvext[pl.ds(Q, 8)] = dvext[pl.ds(0, 8)]
            dsext[pl.ds(Q, 8)] = dsext[pl.ds(0, 8)]
            for which in range(5):
                store(which, chunk + 1).wait()

        def later_mask(shift):
            position = start + lax.broadcasted_iota(jnp.int32, (Q, LANES), 0)
            same = segment_at(position, lengths_ref) == segment_at(position + shift, lengths_ref)
            return (same & (position + shift < chunks * Q)).astype(f32)

        log_decay = prepare(chunk, True)
        for shift in range(1, 4):
            masks[shift - 1] = later_mask(shift)
        step_in = stepin_all[chunk]
        spre = spre_all[chunk]
        spre_sig = sigmoid(spre)
        state_conv = spre * spre_sig
        entry = state_conv[:, :LANES]
        leave = state_conv[:, LANES:]
        scores[...] = dot_nt(entry, leave, highest)
        entry_low = entry.astype(bf16)
        leave_t = leave.T.astype(bf16)
        @pl.when(chunk > 0)
        def _():
            gather_pass(1, fullcot, chunk - 1)

        with_last, with_before, through = boundary(start, lengths_ref)
        to_last = with_last.astype(f32)
        from_before = with_before.astype(f32)
        passes = through.astype(f32)
        row_lane = lax.broadcasted_iota(jnp.int32, (Q, LANES), 0)
        for ref in (d_scores, d_entry, d_leave, acc_step, acc_cum, acc_dot):
            ref[...] = jnp.zeros_like(ref)

        sums = ex_send[chunk]
        for step in range(1, slots):
            send_sums(chunk, step).wait()
        for step in range(1, slots):
            sums = sums + ex_recv[chunk, step]
        rms_row = lax.rsqrt(sums[0:1] * (1.0 / inner_total) + epsilon)
        coef_row = rms_row * rms_row * rms_row * sums[8:9] * (1.0 / inner_total)
        cols[0] = jnp.broadcast_to(rms_row, (LANES, Q)).T
        cols[1] = jnp.broadcast_to(coef_row, (LANES, Q)).T
        keep_load(chunk).wait()

        def one_pair(pair, nothing):
            columns = pl.ds(pl.multiple_of(pair * LANES, LANES), LANES)
            rms = cols[0]
            pre = kbuf[1, :, columns]
            pre_sig = sigmoid(pre)
            x = pre * pre_sig
            step_pair = step_cols[pair]
            weighted = x * step_pair
            gate = gate_all[chunk, :, columns]
            gate_sig = sigmoid(gate)
            gate_silu = gate * gate_sig
            y = y_all[chunk, :, columns]
            gated = y * gate_silu
            d_scaled = dsc[:, columns]
            ggain = ggain_ref[:, columns]
            normalized = gated * rms
            scbuf[:, columns] = (normalized * ggain).astype(bf16)
            d_gated = rms * (d_scaled * ggain) - gated * cols[1]
            sumv_ref[pl.ds(0, 8), columns] += fold_rows(d_scaled * normalized)
            d_gate = (d_gated * y * (gate_sig + gate_silu * (1.0 - gate_sig))).astype(bf16)
            dgbuf[:, columns] = d_gate
            acc_dot[...] += d_gate.astype(f32) * gate
            d_y = d_gated * gate_silu
            skip = skip_ref[:, columns]
            sumv_ref[pl.ds(8, 8), columns] += fold_rows(d_y * x)
            y_scan = y - skip * x

            d_y_t = d_y.T.astype(bf16)
            d_y_both = halves(d_y)
            weighted_low = weighted.astype(bf16)
            results = []
            for half in range(2):
                head = 2 * pair + half
                own = jnp.where(first_half if half == 0 else ~first_half, weighted_low, jnp.zeros_like(weighted_low))
                d_m_top = dot_nn(own[:LANES], d_y_t)
                d_m_low = dot_nn(own[LANES:], d_y_t[:, LANES:])
                c_col = cum_cols[head]
                c_row = cum_rows[pl.ds(head, 1), :]
                l_top = jnp.exp(c_row - jnp.concatenate([c_col[:LANES]] * 2, axis=1) + neg_bias[:LANES])
                l_low = jnp.exp(c_row[:, LANES:] - c_col[LANES:] + neg_bias[LANES:, LANES:])
                d_scores[:LANES] += d_m_top * l_top
                d_scores[LANES:, LANES:] += d_m_low * l_low
                m_top = (scores[:LANES] * l_top).astype(bf16)
                m_low = (scores[LANES:, LANES:] * l_low).astype(bf16)
                upper = dot_nn(m_top, d_y_both)
                lower = dot_nn(m_low, d_y_both[LANES:])
                out = jnp.concatenate([upper, lower], axis=0)
                results.append(out[:, :LANES] + out[:, LANES:])
            d_weighted = jnp.where(first_half, results[0], results[1])
            cum_pair = jnp.where(first_half, cum_cols[2 * pair], cum_cols[2 * pair + 1])
            cum_last = cum_pair[Q - 1 :]
            to_end = jnp.exp(cum_last - cum_pair) * to_last
            from_start = jnp.exp(cum_pair) * from_before
            d_state = d_carry[pair]
            held = states[chunk, pair]
            d_weighted = d_weighted + dot_halves(entry_low, d_state) * to_end
            d_entry[...] += dot_nt((to_end * weighted).astype(bf16), d_state.astype(bf16))
            moved = from_start * d_y
            d_leave[...] += dot_nt(moved.astype(bf16), held.astype(bf16))
            state_dot = jnp.sum(states[chunk + 1, pair] * d_state, axis=0, keepdims=True)
            d_carry[pair] = d_state * (jnp.exp(cum_last) * passes) + dot_halves(leave_t, moved)

            to_step = d_weighted * x
            to_cum = d_y * y_scan - to_step * step_pair + jnp.where(row_lane == Q - 1, state_dot, 0.0)
            acc_step[...] += dot_nn(halves(to_step), gathers[pair])
            acc_cum[...] += dot_nn(halves(to_cum), gathers[pair])

            d_x = d_weighted * step_pair + skip * d_y
            d_pre = d_x * (pre_sig + x * (1.0 - pre_sig))
            dvext[pl.ds(0, Q), columns] = d_pre
            sumv_ref[pl.ds(16, 8), columns] += fold_rows(d_pre)
            vraw = kbuf[0, :, columns]
            total = tapv_ref[3:4, columns] * d_pre
            sumv_ref[pl.ds(48, 8), columns] += fold_rows(vraw * d_pre)
            for shift in range(1, 4):
                moved_back = dvext[pl.ds(shift, Q), columns] * masks[shift - 1]
                total = total + tapv_ref[3 - shift : 4 - shift, columns] * moved_back
                sumv_ref[pl.ds(48 - 8 * shift, 8), columns] += fold_rows(vraw * moved_back)
            d_value = total.astype(bf16)
            dvbuf[:, columns] = d_value
            acc_dot[...] += d_value.astype(f32) * vraw
            return nothing

        lax.fori_loop(0, pairs, one_pair, 0)
        for which in range(3):
            store(which, chunk).start()

        @pl.when(chunk > 0)
        def _():
            products(chunk - 1)


        can_see = (neg_bias[...] == 0.0).astype(f32)
        d_log = dot_nn(can_see, acc_cum[...], highest)
        rate = jnp.exp(rate_ref[...])
        d_step_in = (acc_step[...] - d_log * rate) * sigmoid(step_in)
        d_step = d_step_in.astype(bf16)
        dsmall_ref[pl.ds(start, Q), 2 * LANES :] = d_step
        step_raw = step_in - stepb_ref[...]
        acc_dot[...] += jnp.where(lane < 2 * pairs, d_step.astype(f32) * step_raw, 0.0)
        sumh_ref[pl.ds(0, 8)] += fold_rows(d_step_in)
        sumh_ref[pl.ds(8, 8)] += fold_rows(d_log * log_decay)

        d_scores_now = d_scores[...]
        d_b = d_entry[...] + dot_halves(d_scores_now.astype(bf16), leave)
        d_c = d_leave[...] + dot_halves(d_scores_now.T.astype(bf16), entry)
        for half, grad in enumerate((d_b, d_c)):
            columns = slice(half * LANES, (half + 1) * LANES)
            part = spre_sig[:, columns]
            d_pre = grad * (part + state_conv[:, columns] * (1.0 - part))
            dsext[pl.ds(0, Q), columns] = d_pre
            sums_ref[pl.ds(0, 8), columns] += fold_rows(d_pre)
            sraw = sraw_all[chunk, :, columns]
            total = taps_ref[3:4, columns] * d_pre
            sums_ref[pl.ds(32, 8), columns] += fold_rows(sraw * d_pre)
            for shift in range(1, 4):
                moved_back = dsext[pl.ds(shift, Q), columns] * masks[shift - 1]
                total = total + taps_ref[3 - shift : 4 - shift, columns] * moved_back
                sums_ref[pl.ds(32 - 8 * shift, 8), columns] += fold_rows(sraw * moved_back)
            d_state_raw = total.astype(bf16)
            dsmall_ref[pl.ds(start, Q), columns] = d_state_raw
            acc_dot[...] += d_state_raw.astype(f32) * sraw
        dot_ref[chunk] = ones_rows(acc_dot[...])

        for shard in range(slots):
            here = pl.ds(shard * width, width)
            part = dot_nt(dgbuf[...], wg[here]) + dot_nt(dvbuf[...], wv[here])
            part = part + dot_nt(dsmall_ref[pl.ds(start, Q), : 2 * LANES], ws[here]) + dot_nt(d_step, wt[here])
            bbuf[:, shard * width : (shard + 1) * width] = part.astype(bf16)
        store(3, chunk).start()
        for shard in range(slots):
            part = dot_nt(scbuf[...], wo[pl.ds(shard * width, width)])
            zbuf[:, shard * width : (shard + 1) * width] = part.astype(bf16)
        store(4, chunk).start()
        return nothing

    products(chunks - 1)
    lax.fori_loop(0, chunks, backward_chunk, 0)
    for which in range(5):
        store(which, 0).wait()
    gather_drain(0, ptok, fulltok)
    gather_drain(1, pcot, fullcot)


def head(send_run, arrive_from, lengths, tokens, cotangent, wg, wv, ws, wt, wo, small):
    groups, slots = lax.axis_size("dp"), lax.axis_size("tensor")
    runs, run, width = tokens.shape
    rows = runs * run
    chunks, per_chunk = rows // Q, Q // run
    model, inner = wg.shape
    pairs = inner // LANES
    vmem, anywhere, smem = (pl.BlockSpec(memory_space=s) for s in (pltpu.VMEM, pl.ANY, pltpu.SMEM))
    dma = pltpu.SemaphoreType.DMA
    shape = jax.ShapeDtypeStruct
    return pl.pallas_call(
        head_kernel,
        out_shape=[
            shape((chunks, slots, per_chunk, run, width), bf16),
            shape((chunks, slots, per_chunk, run, width), bf16),
            shape((chunks, Q, model), bf16),
            shape((chunks, Q, inner), bf16),
            shape((chunks, Q, inner), bf16),
            shape((chunks, Q, inner), bf16),
            shape((chunks, Q, model), bf16),
            shape((chunks, 2, Q, inner), f32),
            shape((chunks, Q, model), bf16),
            shape((rows, 3 * LANES), bf16),
            shape((rows, 1), f32),
            shape((chunks, 8, Q), f32),
            shape((56, inner), f32),
            shape((40, 2 * LANES), f32),
            shape((16, LANES), f32),
        ],
        in_specs=[smem] * 3 + [anywhere] * 7 + [vmem] * len(small),
        out_specs=[anywhere] * 9 + [vmem] * 6,
        scratch_shapes=[
            pltpu.VMEM(wg.shape, bf16), pltpu.VMEM(wv.shape, bf16), pltpu.VMEM(ws.shape, bf16),
            pltpu.VMEM(wt.shape, bf16), pltpu.VMEM(wo.shape, bf16),
            pltpu.VMEM((runs, run, width), bf16),
            pltpu.VMEM((runs, run, width), bf16),
            pltpu.VMEM((groups, run, width), bf16),
            pltpu.VMEM((groups, run, width), bf16),
            pltpu.VMEM((groups, run, width), bf16),
            pltpu.VMEM((slots, per_chunk, run, width), bf16),
            pltpu.VMEM((Q, model), bf16),
            pltpu.VMEM((2, Q, inner), f32),
            pltpu.VMEM((chunks, Q, inner), f32),
            pltpu.VMEM((chunks, Q, inner), f32),
            pltpu.VMEM((chunks, Q, 2 * LANES), f32),
            pltpu.VMEM((chunks, Q, 2 * LANES), f32),
            pltpu.VMEM((chunks, Q, LANES), f32),
            pltpu.VMEM((chunks + 1, pairs, LANES, LANES), f32),
            pltpu.VMEM((pairs, LANES, LANES), f32),
            pltpu.VMEM((Q + 8, inner), f32),
            pltpu.VMEM((Q + 8, inner), f32),
            pltpu.VMEM((Q + 8, 2 * LANES), f32),
            pltpu.VMEM((2 * pairs, Q, LANES), f32),
            pltpu.VMEM((pairs, Q, LANES), f32),
            pltpu.VMEM((LANES, Q), f32),
            pltpu.VMEM((Q, Q), f32),
            pltpu.VMEM((Q, Q), f32),
            pltpu.VMEM((Q, Q), f32),
            pltpu.VMEM((Q, LANES), f32),
            pltpu.VMEM((Q, LANES), f32),
            pltpu.VMEM((Q, LANES), f32),
            pltpu.VMEM((Q, LANES), f32),
            pltpu.VMEM((Q, LANES), f32),
            pltpu.VMEM((Q, LANES), f32),
            pltpu.VMEM((Q, inner), f32),
            pltpu.VMEM((Q, inner), bf16),
            pltpu.VMEM((Q, inner), bf16),
            pltpu.VMEM((Q, inner), bf16),
            pltpu.VMEM((Q, model), bf16),
            pltpu.VMEM((Q, model), bf16),
            pltpu.VMEM((chunks, 8, Q), f32),
            pltpu.VMEM((chunks, 16, Q), f32),
            pltpu.VMEM((chunks, slots, 16, Q), f32),
            pltpu.VMEM((2, Q, LANES), f32),
            pltpu.VMEM((3, Q, LANES), f32),
            pltpu.VMEM((pairs, 2 * LANES, LANES), bf16),
            dma((5,)), dma((2,)), dma((groups,)), dma((groups,)), dma((groups,)), dma((groups,)),
            dma((2, chunks, 4)), dma((2, chunks, slots)), dma((2, chunks)), dma, dma, dma((3,)), dma((5,)),
            dma((chunks, slots)), dma((chunks, slots)),
        ],
        compiler_params=pltpu.CompilerParams(collective_id=2, has_side_effects=True, vmem_limit_bytes=HEAD_VMEM),
        name="head",
    )(send_run, arrive_from, lengths, tokens, cotangent, wg, wv, ws, wt, wo, *small)


def tail_kernel(
    back_run_ref, return_from_ref, out_part, back_part, normed, tokens, cotangent, scaled, d_gate, d_value,
    row_dot_ref, inv_ref, gain_ref, small_ref, small_z_ref, dsmall_ref,
    layer_ref, tgrad_ref, small_out, ngain_out, share0, share1, share2, state_out, step_out,
    z_recv, z_comb, z_own, z_mix, ptok, pcot, rd_recv, rd_col, row_buf, slots_buf, arrive_out, arrive_grad, left, right, full,
    core_recv, chip_recv, total, sz_recv, small_all, small_recv, ngain_all, ngain_recv,
    thin, thin_core, thin_chip, thin_own, thin_z,
    load_sem, mix_sem, left_sem, right_sem, zs, zr, zc, rds, rdr, szs, szr, sms, smr, ngs, ngr, rs, rr, cs, cr, hs, hr, tcs, ths, thr, tzs, tzr,
):
    groups, slots = lax.axis_size("dp"), lax.axis_size("tensor")
    group, slot = lax.axis_index("dp"), lax.axis_index("tensor")
    jobs = z_recv.shape[0]
    pieces = jobs // 2
    runs, run, width = layer_ref.shape
    rows = runs * run
    piece_run = run // pieces
    chips = groups // 2
    core = lax.rem(group, 2)
    chip = group // 2
    grow = share0.shape[0]
    per_block = 256 // grow
    blocks = full.shape[1] // per_block
    inner = share0.shape[1]
    last = slots - 1

    greet(groups, slots)

    def z_small(source, target, send_sem, recv_sem, step):
        return pltpu.make_async_remote_copy(
            src_ref=source, dst_ref=target.at[slots - step], send_sem=send_sem.at[step],
            recv_sem=recv_sem.at[slots - step], device_id=(group, lax.rem(slot + step, slots)), device_id_type=MESH,
        )

    def send_dot(step):
        return z_small(row_dot_ref, rd_recv, rds, rdr, step)

    def send_state(step):
        return z_small(small_z_ref, sz_recv, szs, szr, step)

    for step in range(1, slots):
        send_state(step).start()
        send_dot(step).start()

    def piece_of(job, shard):
        source = out_part if job < pieces else back_part
        return source.at[:, pl.ds((job % pieces) * piece_run, piece_run), pl.ds(shard * width, width)]

    def landing(job, me, to):
        return z_recv.at[job, me if me < to else me - 1], zr.at[job, me if me < to else me - 1]

    def z_push(job, number, shard, to, source, target, sem):
        return pltpu.make_async_remote_copy(
            src_ref=source, dst_ref=target, send_sem=zs.at[job, number], recv_sem=sem, device_id=(group, to),
            device_id_type=MESH,
        )

    def direct(job, me, early):
        def push(number, to):
            return z_push(job, number, to, to, piece_of(job, to), *landing(job, me, to))

        def to_mix(number, shard, to):
            return z_push(job, number, shard, to, piece_of(job, shard), z_comb.at[job], zc.at[job])

        if me == 0:
            return [to_mix(0, 3, 1)] if early else [push(1, 2), push(2, 1)]
        if me == last:
            return [to_mix(0, 0, 2)] if early else [push(1, 1), push(2, 2)]
        if early:
            return []
        return [push(0, 0), push(1, 2)] if me == 1 else [push(0, 3), push(1, 1)]

    def mixed(job, me):
        to = 3 if me == 1 else 0
        return z_push(job, 2, to, to, z_mix.at[job], *landing(job, me, to))

    def own_load(kind):
        source = back_part if kind else out_part
        return pltpu.make_async_copy(source.at[:, :, pl.ds(slot * width, width)], z_own.at[kind], load_sem.at[kind])

    def mix_load(job, me):
        return pltpu.make_async_copy(piece_of(job, 3 if me == 1 else 0), z_mix.at[job], mix_sem.at[job])

    def shard_load(which):
        source, target = ((tokens, ptok), (cotangent, pcot))[which]
        return pltpu.make_async_copy(source.at[:, slot], target, load_sem.at[2 + which])

    def push(job, early):
        for me in (0, last) if early else range(slots):
            @pl.when(slot == me)
            def _(me=me):
                for copy in direct(job, me, early):
                    copy.start()

    def combine(job):
        for me in (1, 2):
            @pl.when(slot == me)
            def _(me=me):
                mix_load(job, me).wait()
                z_push(job, 2, 0, 0, z_comb.at[job], z_comb.at[job], zc.at[job]).wait_recv()
                both = z_mix[job].astype(f32) + z_comb[job].astype(f32)
                z_mix[job] = both.astype(bf16)
                mixed(job, me).start()

    rights = (scaled, d_gate, d_value)
    shares = (share0, share1, share2)

    def right_load(which):
        return pltpu.make_async_copy(rights[which], right.at[which % 2], right_sem.at[which])

    def left_load(which, block, place):
        if which == 0:
            per_shard = width // 256
            columns = pl.ds(pl.multiple_of(lax.rem(block, per_shard) * 256, 256), 256)
            source = cotangent.at[:, block // per_shard, :, :, columns]
        else:
            source = normed.at[:, :, :, pl.ds(pl.multiple_of(block * 256, 256), 256)]
        return pltpu.make_async_copy(source, left.at[place], left_sem.at[place])

    def grad_blocks(which, begin, end):
        def one(block, nothing):
            place = lax.rem(block, 2)

            @pl.when(block + 1 < blocks)
            def _():
                left_load(which, block + 1, 1 - place).start()

            left_load(which, block, place).wait()
            value = lax.dot_general(
                left[place].reshape(rows, 256), right[which % 2], (((0,), (0,)), ((), ())), preferred_element_type=f32
            )
            full[which % 2, pl.ds(block * per_block, per_block)] = value.reshape(per_block, grow, -1).astype(bf16)
            if which == 1:
                value = lax.dot_general(
                    left[place].reshape(rows, 256), dsmall_ref[...], (((0,), (0,)), ((), ())), preferred_element_type=f32
                )
                thin[pl.ds(block * per_block, per_block)] = value.reshape(per_block, grow, -1)
            return nothing

        lax.fori_loop(begin, end, one, 0)

    partner = group + 1 - 2 * core

    def core_send(which):
        theirs = full.at[which % 2].reshape(chips, 2, grow, inner).at[:, 1 - core]
        return pltpu.make_async_remote_copy(
            src_ref=theirs, dst_ref=core_recv.at[which], send_sem=cs.at[which], recv_sem=cr.at[which],
            device_id=(partner, slot), device_id_type=MESH,
        )

    def chip_send(which, step):
        other = lax.rem(chip + step, chips)
        return pltpu.make_async_remote_copy(
            src_ref=full.at[which % 2, 2 * other + core], dst_ref=chip_recv.at[which, chips - step],
            send_sem=hs.at[which, step], recv_sem=hr.at[which, chips - step], device_id=(2 * other + core, slot),
            device_id_type=MESH,
        )

    def chip_pushes(which):
        core_send(which).wait()

        def one(step, nothing):
            other = lax.rem(chip + step, chips)
            mine = 2 * other + core
            both = full[which % 2, mine].astype(f32) + core_recv[which, other].astype(f32)
            full[which % 2, mine] = both.astype(bf16)
            chip_send(which, step).start()
            return nothing

        lax.fori_loop(1, chips, one, 0)
        shares[which][...] = full[which % 2, group].astype(f32) + core_recv[which, chip].astype(f32)

    def chip_drain(which):
        def drain(step, nothing):
            chip_send(which, step).wait_send()
            return nothing

        lax.fori_loop(1, chips, drain, 0)

    def chip_total(which):
        def one(step, nothing):
            pltpu.make_async_remote_copy(
                src_ref=chip_recv.at[which, step], dst_ref=chip_recv.at[which, step], send_sem=hs.at[which, step],
                recv_sem=hr.at[which, step], device_id=(group, slot), device_id_type=MESH,
            ).wait_recv()
            shares[which][...] += chip_recv[which, step].astype(f32)
            return nothing

        lax.fori_loop(1, chips, one, 0)

    def thin_core_send():
        theirs = thin.reshape(chips, 2, grow, thin.shape[2]).at[:, 1 - core]
        return pltpu.make_async_remote_copy(
            src_ref=theirs, dst_ref=thin_core, send_sem=tcs.at[0], recv_sem=tcs.at[1], device_id=(partner, slot),
            device_id_type=MESH,
        )

    def thin_chip_send(step):
        other = lax.rem(chip + step, chips)
        return pltpu.make_async_remote_copy(
            src_ref=thin.at[2 * other + core], dst_ref=thin_chip.at[chips - step], send_sem=ths.at[step],
            recv_sem=thr.at[chips - step], device_id=(2 * other + core, slot), device_id_type=MESH,
        )

    def thin_pushes():
        thin_core_send().wait()

        def one(step, nothing):
            other = lax.rem(chip + step, chips)
            thin[2 * other + core] = thin[2 * other + core] + thin_core[other]
            thin_chip_send(step).start()
            return nothing

        lax.fori_loop(1, chips, one, 0)
        thin_own[...] = thin[group] + thin_core[chip]

    def thin_z_send(step):
        other = lax.rem(slot + step, slots)
        part = state_out.shape[0]
        return pltpu.make_async_remote_copy(
            src_ref=thin_own.at[pl.ds(other * part, part), pl.ds(0, 2 * LANES)], dst_ref=thin_z.at[slots - step],
            send_sem=tzs.at[step], recv_sem=tzr.at[slots - step], device_id=(group, other), device_id_type=MESH,
        )

    def thin_total():
        def one(step, nothing):
            pltpu.make_async_remote_copy(
                src_ref=thin_chip.at[step], dst_ref=thin_chip.at[step], send_sem=ths.at[step], recv_sem=thr.at[step],
                device_id=(group, slot), device_id_type=MESH,
            ).wait_recv()
            thin_own[...] += thin_chip[step]
            return nothing

        lax.fori_loop(1, chips, one, 0)
        for step in range(1, slots):
            thin_z_send(step).start()
        step_out[...] = thin_own[:, 2 * LANES :]

    def thin_finish():
        part = state_out.shape[0]
        acc = thin_own[pl.ds(slot * part, part), : 2 * LANES]
        for step in range(1, slots):
            thin_z_send(step).wait()
        for step in range(1, slots):
            acc = acc + thin_z[step]
        state_out[...] = acc

        def drain(step, nothing):
            thin_chip_send(step).wait_send()
            return nothing

        lax.fori_loop(1, chips, drain, 0)

    def dp_small(source, target, send_sem, recv_sem, step):
        return pltpu.make_async_remote_copy(
            src_ref=source, dst_ref=target.at[groups - step], send_sem=send_sem.at[step],
            recv_sem=recv_sem.at[groups - step], device_id=(lax.rem(group + step, groups), slot), device_id_type=MESH,
        )

    def dp_small_start(source, target, send_sem, recv_sem):
        def one(step, nothing):
            dp_small(source, target, send_sem, recv_sem, step).start()
            return nothing

        lax.fori_loop(1, groups, one, 0)

    def dp_small_finish(source, target, send_sem, recv_sem, result):
        result[...] = source[...]

        def one(step, nothing):
            pltpu.make_async_remote_copy(
                src_ref=target.at[step], dst_ref=target.at[step], send_sem=send_sem.at[step],
                recv_sem=recv_sem.at[step], device_id=(group, slot), device_id_type=MESH,
            ).wait_recv()
            result[...] += target[step]
            return nothing

        lax.fori_loop(1, groups, one, 0)

        def drain(step, nothing):
            dp_small(source, target, send_sem, recv_sem, step).wait_send()
            return nothing

        lax.fori_loop(1, groups, drain, 0)

    arrives = (arrive_out, arrive_grad)

    def row_send(job, step):
        other = lax.rem(group + step, groups)
        return pltpu.make_async_remote_copy(
            src_ref=slots_buf.at[job % pieces, other], dst_ref=arrives[job // pieces].at[job % pieces, group], send_sem=rs.at[job, other],
            recv_sem=rr.at[job, group], device_id=(other, slot), device_id_type=MESH,
        )

    def rows_drain(job):
        def one(step, nothing):
            row_send(job, step).wait_send()
            return nothing

        lax.fori_loop(1, groups, one, 0)

    def finish(job):
        kind, piece = job // pieces, job % pieces
        here = pl.ds(piece * piece_run, piece_run)
        tall = runs * piece_run
        for me in range(slots):
            @pl.when(slot == me)
            def _(me=me):
                acc = z_own[kind, :, here, :].astype(f32)
                for source in ((1, 2) if me in (0, 3) else tuple(s for s in range(slots) if s != me)):
                    place, sem = landing(job, source, me)
                    z_push(job, 0, 0, 0, place, place, sem).wait_recv()
                    acc = acc + place[...].astype(f32)
                total[...] = acc
        summed = total[...].reshape(tall, width)
        kept = ptok[:, :, here, :].reshape(tall, width).astype(f32)
        if kind == 0:
            result = kept + summed
        else:
            inv = inv_ref[:, here, :].reshape(tall, 1)
            unit = kept * inv
            ngain_all[...] += fold_rows(summed * unit)
            dot_cols = rd_col[:, here, :].reshape(tall, LANES)
            dot_cols = jnp.concatenate([dot_cols] * (width // LANES), axis=1)
            cot = pcot[:, :, here, :].reshape(tall, width).astype(f32)
            result = cot + inv * (summed * gain_ref[...] - unit * dot_cols)
        row_buf[...] = result.astype(bf16).reshape(runs, piece_run, width)

        def fill(step, nothing):
            other = lax.rem(group + step, groups)
            slots_buf[job % pieces, other] = row_buf[back_run_ref[other]]
            row_send(job, step).start()
            return nothing

        if kind == 1:
            rows_drain(job - pieces)
        lax.fori_loop(1, groups, fill, 0)
        arrives[kind][piece, group] = row_buf[back_run_ref[group]]

    def rows_wait(kind):
        for job in range(kind * pieces, (kind + 1) * pieces):
            def one(step, nothing, job=job):
                source = lax.rem(group + groups - step, groups)
                pltpu.make_async_remote_copy(
                    src_ref=arrives[kind].at[job % pieces, source], dst_ref=arrives[kind].at[job % pieces, source],
                    send_sem=rs.at[job, source],
                    recv_sem=rr.at[job, source], device_id=(group, slot), device_id_type=MESH,
                ).wait_recv()
                return nothing

            lax.fori_loop(1, groups, one, 0)

    def rows_take(kind, target):
        for piece in range(pieces):
            for index in range(runs):
                target[index, pl.ds(piece * piece_run, piece_run)] = arrives[kind][piece, return_from_ref[index]]

    def let_in(job):
        if job < jobs:
            push(job, False)
            combine(job)

    def step_of(job):
        if job + EARLY < jobs:
            push(job + EARLY, True)
        let_in(job + WINDOW)
        finish(job)

    for job in range(min(EARLY, jobs)):
        push(job, True)
    own_load(0).start()
    own_load(1).start()
    shard_load(0).start()
    shard_load(1).start()
    for me in (1, 2):
        @pl.when(slot == me)
        def _(me=me):
            for job in range(jobs):
                mix_load(job, me).start()
    right_load(0).start()
    left_load(0, 0, 0).start()
    right_load(1).start()
    ngain_all[...] = jnp.zeros_like(ngain_all)

    half = blocks // 2
    right_load(0).wait()
    grad_blocks(0, 0, half)
    small_z = small_z_ref[...]
    for step in range(1, slots):
        send_state(step).wait()
    for step in range(1, slots):
        small_z = small_z + sz_recv[step]
    small_all[:, pl.ds(0, inner)] = small_ref[...]
    small_all[:, pl.ds(inner, 2 * LANES)] = small_z
    dp_small_start(small_all, small_recv, sms, smr)
    grad_blocks(0, half, blocks)
    core_send(0).start()
    right_load(2).start()
    for kind in range(2):
        own_load(kind).wait()
        shard_load(kind).wait()
    left_load(1, 0, 0).start()
    push(0, False)
    right_load(1).wait()
    grad_blocks(1, 0, half)
    chip_pushes(0)
    grad_blocks(1, half, blocks)
    core_send(1).start()
    thin_core_send().start()
    left_load(2, 0, 0).start()
    rd_total = row_dot_ref[...]
    for step in range(1, slots):
        send_dot(step).wait()
    for step in range(1, slots):
        rd_total = rd_total + rd_recv[step]
    rd_total = rd_total * (1.0 / (width * slots))
    for block in range(rows // 256):
        piece_row = jnp.broadcast_to(rd_total[0:1, block * 256 : (block + 1) * 256], (LANES, 256))
        count = 256 // run
        rd_col[pl.ds(block * count, count)] = piece_row.T.reshape(count, run, LANES)
    combine(0)
    right_load(2).wait()
    chip_drain(0)
    let_in(1)
    grad_blocks(2, 0, half)
    chip_pushes(1)
    thin_pushes()
    grad_blocks(2, half, blocks)
    core_send(2).start()
    for job in range(2, WINDOW):
        let_in(job)
    def out_rows():
        rows_wait(0)
        rows_take(0, layer_ref)

    meanwhile = [
        thin_total,
        lambda: [chip_total(which) for which in range(3)],
        lambda: dp_small_finish(small_all, small_recv, sms, smr, small_out),
    ]
    for job in range(jobs):
        if job == 1:
            chip_pushes(2)
        if job == jobs - 1:
            out_rows()
        step_of(job)
        if job >= jobs // 2 and meanwhile:
            meanwhile.pop(0)()
    dp_small_start(ngain_all, ngain_recv, ngs, ngr)
    for action in meanwhile:
        action()
    rows_wait(1)
    for job in range(pieces, jobs):
        rows_drain(job)
    rows_take(1, tgrad_ref)
    thin_finish()
    chip_drain(1)
    chip_drain(2)
    dp_small_finish(ngain_all, ngain_recv, ngs, ngr, ngain_out)
    for me in range(slots):
        @pl.when(slot == me)
        def _(me=me):
            for job in range(jobs):
                for copy in direct(job, me, True) + direct(job, me, False):
                    copy.wait_send()
                if me in (1, 2):
                    mixed(job, me).wait_send()


def tail(back_run, return_from, out_part, back_part, normed, tokens, cotangent, scaled, d_gate, d_value, row_dot, inv,
         gain, small, small_z, d_small):
    groups, slots = lax.axis_size("dp"), lax.axis_size("tensor")
    runs, run, model = out_part.shape
    width = model // slots
    rows = runs * run
    inner = scaled.shape[1]
    pieces = min(4, run // 16)
    jobs = 2 * pieces
    piece_run = run // pieces
    grow = model // groups
    chips = groups // 2
    vmem, anywhere, smem = (pl.BlockSpec(memory_space=s) for s in (pltpu.VMEM, pl.ANY, pltpu.SMEM))
    dma = pltpu.SemaphoreType.DMA
    shape = jax.ShapeDtypeStruct
    by_chunk = tokens.shape[:1] + tokens.shape[2:]
    part = (runs, piece_run, width)
    return pl.pallas_call(
        tail_kernel,
        out_shape=[
            shape((runs, run, width), bf16), shape((runs, run, width), bf16), shape((8, inner + 2 * LANES), f32),
            shape((8, width), f32),
        ] + [shape((grow, inner), f32)] * 3 + [shape((grow // slots, 2 * LANES), f32), shape((grow, LANES), f32)],
        in_specs=[smem] * 2 + [anywhere] * 8 + [vmem] * 6,
        out_specs=[vmem] * 9,
        scratch_shapes=[
            pltpu.VMEM((jobs, slots - 1) + part, bf16),
            pltpu.VMEM((jobs,) + part, bf16),
            pltpu.VMEM((2, runs, run, width), bf16),
            pltpu.VMEM((jobs,) + part, bf16),
            pltpu.VMEM(by_chunk, bf16),
            pltpu.VMEM(by_chunk, bf16),
            pltpu.VMEM((slots, 8, rows), f32),
            pltpu.VMEM((runs, run, LANES), f32),
            pltpu.VMEM(part, bf16),
            pltpu.VMEM((pieces, groups, piece_run, width), bf16),
            pltpu.VMEM((pieces, groups, piece_run, width), bf16),
            pltpu.VMEM((pieces, groups, piece_run, width), bf16),
            pltpu.VMEM((2,) + by_chunk[:-1] + (256,), bf16),
            pltpu.VMEM((2, rows, inner), bf16),
            pltpu.VMEM((2, groups, grow, inner), bf16),
            pltpu.VMEM((3, chips, grow, inner), bf16),
            pltpu.VMEM((3, chips, grow, inner), bf16),
            pltpu.VMEM(part, f32),
            pltpu.VMEM((slots, 8, 2 * LANES), f32),
            pltpu.VMEM((8, inner + 2 * LANES), f32),
            pltpu.VMEM((groups, 8, inner + 2 * LANES), f32),
            pltpu.VMEM((8, width), f32),
            pltpu.VMEM((groups, 8, width), f32),
            pltpu.VMEM((groups, grow, 3 * LANES), f32),
            pltpu.VMEM((chips, grow, 3 * LANES), f32),
            pltpu.VMEM((chips, grow, 3 * LANES), f32),
            pltpu.VMEM((grow, 3 * LANES), f32),
            pltpu.VMEM((slots, grow // slots, 2 * LANES), f32),
            dma((4,)), dma((jobs,)), dma((2,)), dma((3,)),
            dma((jobs, 3)), dma((jobs, slots - 1)), dma((jobs,)),
            dma((slots,)), dma((slots,)), dma((slots,)), dma((slots,)),
            dma((groups,)), dma((groups,)), dma((groups,)), dma((groups,)),
            dma((jobs, groups)), dma((jobs, groups)),
            dma((3,)), dma((3,)), dma((3, chips)), dma((3, chips)),
            dma((2,)), dma((chips,)), dma((chips,)), dma((slots,)), dma((slots,)),
        ],
        compiler_params=pltpu.CompilerParams(collective_id=3, has_side_effects=True, vmem_limit_bytes=64 << 20),
        name="tail",
    )(back_run, return_from, out_part, back_part, normed, tokens, cotangent, scaled, d_gate, d_value, row_dot, inv, gain,
      small, small_z, d_small)


def pad_heads(values):
    return jnp.pad(values, ((0, 0), (0, LANES - values.shape[1])))


def per_device(
    tokens, cotangent, norm_gain, gate_proj, value_proj, state_proj, step_proj, conv_value, conv_value_bias,
    conv_state, conv_state_bias, step_bias, decay_log, skip_gain, gate_gain, out_proj, token_order, lengths,
):
    groups = lax.axis_size("dp")
    group = lax.axis_index("dp")
    slots = lax.axis_size("tensor")
    slot = lax.axis_index("tensor")
    rows, width = tokens.shape
    model = width * slots
    inner = gate_proj.shape[1]
    heads = step_bias.shape[0]
    run = 2 * rows // groups
    runs = rows // run

    source_run = token_order.reshape(groups, runs, run)[:, :, 0] // run
    source_group = source_run // runs
    from_here = source_group == group
    send_run = jnp.sum(jnp.where(from_here, source_run % runs, 0), axis=1)
    arrive_from = lax.dynamic_index_in_dim(source_group, group, 0, keepdims=False)
    every = jnp.arange(groups, dtype=jnp.int32)
    back_run = jnp.sum(
        jnp.where(arrive_from[None, :] == every[:, None], jnp.arange(runs, dtype=jnp.int32)[None, :], 0), axis=1
    )
    local_run = group * runs + jnp.arange(runs, dtype=jnp.int32)
    return_from = jnp.sum(
        jnp.where(source_run[None] == local_run[:, None, None], every[None, :, None], 0), axis=(1, 2)
    )

    def cut(values):
        return values.reshape(runs, run, values.shape[1])

    gain_full = norm_gain.astype(f32)
    def row(values):
        return jnp.pad(values.astype(f32), (0, model - values.shape[0]))

    rows_of = (norm_gain, gate_gain, conv_value_bias, conv_state_bias, jnp.repeat(skip_gain, HEAD_DIM))
    small = (
        conv_value.astype(f32),
        conv_state.astype(f32),
        pad_heads(jnp.stack([step_bias, decay_log])).reshape(2, 1, LANES),
        jnp.stack([row(v) for v in rows_of]).reshape(len(rows_of), 1, model),
    )
    (full_tokens, full_cotangent, normed, d_gate, d_value, scaled, back_partial, _, out_partial, d_small,
     inv_rms, row_dot, sumv, sums, sumh) = head(
        send_run, arrive_from, lengths, cut(tokens), cut(cotangent), gate_proj, value_proj, state_proj,
        pad_heads(step_proj), out_proj, small,
    )
    row_dot = row_dot.transpose(1, 0, 2).reshape(8, rows)
    normed_cut = normed.reshape(full_tokens.shape[0], full_tokens.shape[2], run, model)
    d_gate, d_value, scaled, back_partial, out_partial = (
        v.reshape(rows, v.shape[2]) for v in (d_gate, d_value, scaled, back_partial, out_partial)
    )
    gain_share = lax.dynamic_slice_in_dim(gain_full, slot * width, width, 0)
    by_head = jnp.pad(sumh.reshape(2, 8, LANES).sum(1).reshape(1, 2 * LANES), ((0, 0), (0, inner - 2 * LANES)))
    small = jnp.concatenate([sumv.reshape(7, 8, inner).sum(1), by_head])
    small_z = jnp.pad(sums.reshape(5, 8, 2 * LANES).sum(1), ((0, 3), (0, 0)))
    layer_output, tokens_grad, small, norm_gain_rows, out_grad_share, gate_share, value_share, state_share, step_share = tail(
        back_run, return_from, cut(out_partial), cut(back_partial), normed_cut, full_tokens, full_cotangent, scaled,
        d_gate, d_value, row_dot, cut(inv_rms), gain_share[None], small, small_z, d_small,
    )
    state_sums = small[:, inner:]
    return (
        layer_output.reshape(rows, width),
        tokens_grad.reshape(rows, width),
        jnp.sum(norm_gain_rows, axis=0),
        gate_share,
        value_share,
        state_share,
        step_share[:, :heads],
        small[3:7, :inner],
        small[2, :inner],
        state_sums[1:5],
        state_sums[0],
        small[7, :heads],
        small[7, LANES : LANES + heads],
        jnp.sum(small[1, :inner].reshape(heads, HEAD_DIM), axis=1),
        small[0, :inner],
        out_grad_share,
    )


def solution(mesh):
    across = P(None, "tensor")
    both = P("dp", "tensor")
    heads = P("tensor")
    return jax.shard_map(
        per_device,
        mesh=mesh,
        in_specs=(
            both, both, P(), across, across, P(), across, across, heads, P(), P(), heads, heads, heads, heads, across,
            P(), P("dp", None),
        ),
        out_specs=(
            both, both, heads, both, both, P(("dp", "tensor"), None), both, across, heads, P(), P(), heads, heads, heads,
            heads, both,
        ),
        check_vma=False,
    )
```

```python
import jax
import jax.numpy as jnp
from jax import lax
from jax.experimental import pallas as pl
from jax.experimental.pallas import tpu as pltpu
from jax.sharding import PartitionSpec as P

f32 = jnp.float32
bf16 = jnp.bfloat16
Q = 256
LANES = 128
HEAD_DIM = 64
WINDOW = 3
EARLY = 6
HEAD_VMEM = 64 << 20
highest = lax.Precision.HIGHEST
epsilon = 1e-05


def dot_nn(a, b, precision=None):
    return lax.dot_general(a, b, (((1,), (0,)), ((), ())), precision=precision, preferred_element_type=f32)


def dot_nt(a, b, precision=None):
    return lax.dot_general(a, b, (((1,), (1,)), ((), ())), precision=precision, preferred_element_type=f32)


def halves(values):
    high = values.astype(bf16)
    return jnp.concatenate([high, (values - high.astype(f32)).astype(bf16)], axis=1)


def dot_halves(a, values):
    both = dot_nn(a, halves(values))
    return both[:, :LANES] + both[:, LANES:]


def sigmoid(values):
    return 0.5 * jnp.tanh(0.5 * values) + 0.5


def fold_rows(values):
    return jnp.sum(values.reshape(-1, 8, values.shape[-1]), axis=0)


def segment_at(position, lengths_ref):
    total = lengths_ref[0, 0]
    seg = (position >= total).astype(jnp.int32)
    for index in range(1, lengths_ref.shape[1]):
        total = total + lengths_ref[0, index]
        seg = seg + (position >= total).astype(jnp.int32)
    return seg


def tap_mask(start, shift, rows, lengths_ref):
    position = start + lax.broadcasted_iota(jnp.int32, (rows, LANES), 0)
    same = (segment_at(position, lengths_ref) == segment_at(position - shift, lengths_ref)) & (position >= shift)
    return same.astype(f32)


def triangle(start, lengths_ref, transposed):
    first = lax.broadcasted_iota(jnp.int32, (Q, Q), 0)
    second = lax.broadcasted_iota(jnp.int32, (Q, Q), 1)
    same = segment_at(start + first, lengths_ref) == segment_at(start + second, lengths_ref)
    order = (second >= first) if transposed else (first >= second)
    return same & order


def head_columns(cum, step, cum_cols, step_cols):
    lane = lax.broadcasted_iota(jnp.int32, (Q, LANES), 1)
    for head in range(cum_cols.shape[0]):
        cum_cols[head] = jnp.broadcast_to(cum[:, head : head + 1], (Q, LANES))
    for pair in range(step_cols.shape[0]):
        even = jnp.broadcast_to(step[:, 2 * pair : 2 * pair + 1], (Q, LANES))
        odd = jnp.broadcast_to(step[:, 2 * pair + 1 : 2 * pair + 2], (Q, LANES))
        step_cols[pair] = jnp.where(lane < HEAD_DIM, even, odd)


def boundary(start, lengths_ref):
    position = start + lax.broadcasted_iota(jnp.int32, (Q, LANES), 0)
    seg = segment_at(position, lengths_ref)
    last = segment_at(jnp.full((1, LANES), start + Q - 1, jnp.int32), lengths_ref)
    before = segment_at(jnp.full((1, LANES), start - 1, jnp.int32), lengths_ref)
    before = jnp.where(start > 0, before, -1)
    return (seg == last), (seg == before), (last == before)


def softplus(values):
    return jnp.maximum(values, 0.0) + jnp.log1p(jnp.exp(-jnp.abs(values)))


def causal_taps(ext_ref, taps, bias, masks, columns):
    total = taps[3:4] * ext_ref[pl.ds(8, Q), columns]
    for shift in range(1, 4):
        total = total + taps[3 - shift : 4 - shift] * (ext_ref[pl.ds(8 - shift, Q), columns] * masks[shift - 1])
    return total + bias


def chunk_scalars(start, step_in, rate, lengths_ref, causal):
    step = softplus(step_in)
    log_decay = -step * jnp.exp(rate)
    cum = dot_nn(causal, log_decay, highest)
    return step, log_decay, cum


MESH = pl.DeviceIdType.MESH


def greet(groups, slots):
    group, slot = lax.axis_index("dp"), lax.axis_index("tensor")
    barrier = pltpu.get_barrier_semaphore()

    def along_dp(step, nothing):
        pl.semaphore_signal(barrier, inc=1, device_id=(lax.rem(group + step, groups), slot), device_id_type=MESH)
        return nothing

    lax.fori_loop(1, groups, along_dp, 0)
    for step in range(1, slots):
        pl.semaphore_signal(barrier, inc=1, device_id=(group, lax.rem(slot + step, slots)), device_id_type=MESH)
    pl.semaphore_wait(barrier, groups - 1 + slots - 1)


def head_kernel(
    send_run_ref, arrive_from_ref, lengths_ref, tokens, cotangent, wg_hbm, wv_hbm, ws_hbm, wt_hbm, wo_hbm,
    tapv_ref, taps_ref, heads_ref, small_ref,
    fulltok, fullcot, normed_out, dgate_out, dvalue_out, scaled_out, back_out, keep, out_part,
    dsmall_ref, inv_ref, dot_ref, sumv_ref, sums_ref, sumh_ref,
    wg, wv, ws, wt, wo, ptok, pcot, slots_buf, arr_tok, arr_cot, xbuf, nbuf, kbuf, gate_all, y_all,
    sraw_all, spre_all, stepin_all, states, d_carry, vext, dvext, sext, cum_cols, step_cols, cum_rows, neg_bias,
    scores, d_scores, d_entry, d_leave, acc_step, acc_cum, acc_dot, acc_prod, dsc, dgbuf, dvbuf, scbuf, bbuf, zbuf,
    sq_rows, ex_send, ex_recv, cols, masks, gathers,
    w_sem, in_sem, ts, tr, cs, cr, ags, agr, own_sem, x_sem, n_sem, keep_sem, o_sem, es, er,
):
    groups, slots = lax.axis_size("dp"), lax.axis_size("tensor")
    group, slot = lax.axis_index("dp"), lax.axis_index("tensor")
    runs, run, width = ptok.shape
    chunks = runs * run // Q
    per_chunk = Q // run
    pairs = d_carry.shape[0]
    gain_ref, ggain_ref, biasv_ref, biass_ref, skip_ref = (small_ref.at[row] for row in range(5))
    stepb_ref, rate_ref = heads_ref.at[0], heads_ref.at[1]
    last = slots - 1
    model = width * slots
    inner_total = wg.shape[1] * slots
    lane = lax.broadcasted_iota(jnp.int32, (Q, LANES), 1)
    first_half = lane < HEAD_DIM

    greet(groups, slots)
    weights = ((wg_hbm, wg), (wv_hbm, wv), (ws_hbm, ws), (wt_hbm, wt), (wo_hbm, wo))

    def weight_load(which):
        return pltpu.make_async_copy(weights[which][0], weights[which][1], w_sem.at[which])

    tok_in = pltpu.make_async_copy(tokens, ptok, in_sem.at[0])
    cot_in = pltpu.make_async_copy(cotangent, pcot, in_sem.at[1])
    tok_in.start()
    cot_in.start()
    for which in range(5):
        weight_load(which).start()

    def row_send(arrive, send_sem, recv_sem, step):
        other = lax.rem(group + step, groups)
        return pltpu.make_async_remote_copy(
            src_ref=slots_buf.at[other], dst_ref=arrive.at[group], send_sem=send_sem.at[other],
            recv_sem=recv_sem.at[group], device_id=(other, slot), device_id_type=MESH,
        )

    def send_rows(source, arrive, send_sem, recv_sem):
        def one(step, nothing):
            other = lax.rem(group + step, groups)
            slots_buf[other] = source[send_run_ref[other]]
            row_send(arrive, send_sem, recv_sem, step).start()
            return nothing

        lax.fori_loop(1, groups, one, 0)
        arrive[group] = source[send_run_ref[group]]

    def take_rows(packed, arrive, send_sem, recv_sem):
        def one(step, nothing):
            source = lax.rem(group + groups - step, groups)
            pltpu.make_async_remote_copy(
                src_ref=arrive.at[source], dst_ref=arrive.at[source], send_sem=send_sem.at[source],
                recv_sem=recv_sem.at[source], device_id=(group, slot), device_id_type=MESH,
            ).wait_recv()
            row_send(arrive, send_sem, recv_sem, step).wait_send()
            return nothing

        lax.fori_loop(1, groups, one, 0)
        for index in range(runs):
            packed[index] = arrive[arrive_from_ref[index]]

    def rows_of(packed, chunk):
        return packed.at[pl.ds(chunk * per_chunk, per_chunk)]

    def gather_push(kind, source, target, chunk, number, shard, to):
        return pltpu.make_async_remote_copy(
            src_ref=source, dst_ref=target.at[chunk, shard], send_sem=ags.at[kind, chunk, number],
            recv_sem=agr.at[kind, chunk, shard], device_id=(group, to), device_id_type=MESH,
        )

    far_to = ((2,), (), (), (1,))
    near_to = ((1,), (0, 2, 3), (3, 1, 0), (2,))

    def gather_direct(kind, packed, target, chunk, me, far):
        first = 0 if far else len(far_to[me])
        return [
            gather_push(kind, rows_of(packed, chunk), target, chunk, first + number, me, to)
            for number, to in enumerate(far_to[me] if far else near_to[me])
        ]

    def gather_forward(kind, target, chunk, me):
        shard, to = (3, 0) if me == 1 else (0, 3)
        return gather_push(kind, target.at[chunk, shard], target, chunk, 3, shard, to)

    def own_copy(kind, packed, target, chunk):
        return pltpu.make_async_copy(rows_of(packed, chunk), target.at[chunk, slot], own_sem.at[kind, chunk])

    def gather_far(kind, packed, target, chunk):
        for me in (0, 3):
            @pl.when(slot == me)
            def _(me=me):
                for copy in gather_direct(kind, packed, target, chunk, me, True):
                    copy.start()

    def gather_near(kind, packed, target, chunk):
        own_copy(kind, packed, target, chunk).start()
        for me in range(slots):
            @pl.when(slot == me)
            def _(me=me):
                for copy in gather_direct(kind, packed, target, chunk, me, False):
                    copy.start()

    def gather_arrived(kind, target, chunk, shard):
        pltpu.make_async_remote_copy(
            src_ref=target.at[chunk, shard], dst_ref=target.at[chunk, shard], send_sem=ags.at[kind, chunk, 0],
            recv_sem=agr.at[kind, chunk, shard], device_id=(group, slot), device_id_type=MESH,
        ).wait_recv()

    def gather_pass(kind, target, chunk):
        for me in (1, 2):
            @pl.when(slot == me)
            def _(me=me):
                gather_arrived(kind, target, chunk, 3 if me == 1 else 0)
                gather_forward(kind, target, chunk, me).start()

    def gather_wait(kind, packed, target, chunk):
        for me in range(slots):
            @pl.when(slot == me)
            def _(me=me):
                for shard in (1, 2) if me in (0, 3) else (0, 2) if me == 1 else (3, 1):
                    gather_arrived(kind, target, chunk, shard)
                if me in (0, 3):
                    gather_arrived(kind, target, chunk, 3 - me)
        own_copy(kind, packed, target, chunk).wait()

    def gather_drain(kind, packed, target):
        for chunk in range(chunks):
            for me in range(slots):
                @pl.when(slot == me)
                def _(me=me):
                    for copy in gather_direct(kind, packed, target, chunk, me, True):
                        copy.wait_send()
                    for copy in gather_direct(kind, packed, target, chunk, me, False):
                        copy.wait_send()
                    if me in (1, 2):
                        gather_forward(kind, target, chunk, me).wait_send()

    def keep_store(chunk, which):
        source = vext.at[pl.ds(8, Q)] if which == 0 else kbuf.at[1]
        return pltpu.make_async_copy(source, keep.at[chunk, which], keep_sem.at[which])

    def keep_load(chunk):
        return pltpu.make_async_copy(keep.at[chunk], kbuf, keep_sem.at[2])

    def normed_store(chunk):
        return pltpu.make_async_copy(nbuf, normed_out.at[chunk], n_sem)

    stores = ((dgbuf, dgate_out), (dvbuf, dvalue_out), (scbuf, scaled_out), (bbuf, back_out), (zbuf, out_part))

    def store(which, chunk):
        return pltpu.make_async_copy(stores[which][0], stores[which][1].at[chunk], o_sem.at[which])

    def x_load(source, chunk):
        return pltpu.make_async_copy(source.at[chunk], xbuf, x_sem)

    def ones_rows(values):
        return dot_nt(jnp.ones((8, LANES), f32), values, highest)

    def prepare(chunk, transposed):
        start = chunk * Q
        can_see = triangle(start, lengths_ref, transposed)
        neg_bias[...] = jnp.where(can_see, 0.0, -1e30)
        row = lax.broadcasted_iota(jnp.int32, (Q, Q), 0)
        col = lax.broadcasted_iota(jnp.int32, (Q, Q), 1)
        step_in = stepin_all[chunk]
        step, log_decay, cum = chunk_scalars(start, step_in, rate_ref[...], lengths_ref, (row >= col).astype(f32))
        cum_rows[...] = cum.T
        head_columns(cum, step, cum_cols, step_cols)
        return log_decay

    tok_in.wait()
    send_rows(ptok, arr_tok, ts, tr)
    states[0] = jnp.zeros_like(states[0])
    vext[pl.ds(0, 8)] = jnp.zeros((8, vext.shape[1]), f32)
    sext[pl.ds(0, 8)] = jnp.zeros((8, sext.shape[1]), f32)
    d_carry[...] = jnp.zeros_like(d_carry)
    dvext[pl.ds(Q, 8)] = jnp.zeros((8, dvext.shape[1]), f32)
    sumv_ref[...] = jnp.zeros_like(sumv_ref)
    sums_ref[...] = jnp.zeros_like(sums_ref)
    sumh_ref[...] = jnp.zeros_like(sumh_ref)
    place = lax.broadcasted_iota(jnp.int32, (2 * LANES, LANES), 1)
    source = lax.broadcasted_iota(jnp.int32, (2 * LANES, LANES), 0)
    source = (lax.rem(source, LANES) >= HEAD_DIM).astype(jnp.int32)
    for pair in range(pairs):
        gathers[pair] = (place == source + 2 * pair).astype(bf16)
    take_rows(ptok, arr_tok, ts, tr)
    gather_far(0, ptok, fulltok, 0)
    gather_near(0, ptok, fulltok, 0)
    gather_far(0, ptok, fulltok, 1)
    cot_in.wait()
    send_rows(pcot, arr_cot, cs, cr)
    for which in range(5):
        weight_load(which).wait()

    def forward_chunk(chunk, nothing):
        start = chunk * Q
        @pl.when(chunk == 0)
        def _():
            gather_pass(0, fulltok, 0)
            gather_near(0, ptok, fulltok, 1)
            gather_far(0, ptok, fulltok, 2)

        gather_wait(0, ptok, fulltok, chunk)
        x_load(fulltok, chunk).start()

        @pl.when(chunk + 2 < chunks)
        def _():
            gather_near(0, ptok, fulltok, chunk + 2)

        @pl.when(chunk + 3 < chunks)
        def _():
            gather_far(0, ptok, fulltok, chunk + 3)

        @pl.when(chunk + 3 == chunks)
        def _():
            take_rows(pcot, arr_cot, cs, cr)

        @pl.when(chunk + 3 >= chunks)
        def _():
            gather_far(1, pcot, fullcot, 2 * chunks - 4 - chunk)

        @pl.when(chunk + 2 >= chunks)
        def _():
            gather_near(1, pcot, fullcot, 2 * chunks - 3 - chunk)

        @pl.when(chunk > 0)
        def _():
            normed_store(chunk - 1).wait()
            keep_store(chunk - 1, 0).wait()
            keep_store(chunk - 1, 1).wait()
            vext[pl.ds(0, 8)] = vext[pl.ds(Q, 8)]
            sext[pl.ds(0, 8)] = sext[pl.ds(Q, 8)]

        x_load(fulltok, chunk).wait()
        squares = jnp.zeros((Q, 1), f32)
        for shard in range(slots):
            wide = xbuf[shard].reshape(Q, width).astype(f32)
            squares = squares + jnp.sum(wide * wide, axis=1, keepdims=True)
        inv = lax.rsqrt(squares * (1.0 / model) + epsilon)
        inv_ref[pl.ds(start, Q)] = inv
        for shard in range(slots):
            wide = xbuf[shard].reshape(Q, width).astype(f32)
            columns = slice(shard * width, (shard + 1) * width)
            nbuf[:, columns] = (wide * inv * gain_ref[:, columns]).astype(bf16)
        normed_store(chunk).start()
        gate_all[chunk] = dot_nn(nbuf[...], wg[...])
        vext[pl.ds(8, Q)] = dot_nn(nbuf[...], wv[...])
        sext[pl.ds(8, Q)] = dot_nn(nbuf[...], ws[...])
        stepin_all[chunk] = dot_nn(nbuf[...], wt[...]) + stepb_ref[...]
        keep_store(chunk, 0).start()
        sraw_all[chunk] = sext[pl.ds(8, Q)]
        prepare(chunk, False)
        for shift in range(1, 4):
            masks[shift - 1] = tap_mask(start, shift, Q, lengths_ref)

        for half in range(2):
            columns = slice(half * LANES, (half + 1) * LANES)
            spre_all[chunk, :, columns] = causal_taps(
                sext, taps_ref[:, columns], biass_ref[:, columns], masks, columns
            )
        spre = spre_all[chunk]
        state_conv = spre * sigmoid(spre)
        entry = state_conv[:, :LANES]
        leave = state_conv[:, LANES:]
        scores[...] = dot_nt(leave, entry, highest)
        entry_t = entry.T.astype(bf16)
        leave_low = leave.astype(bf16)
        @pl.when(chunk + 1 < chunks)
        def _():
            gather_pass(0, fulltok, chunk + 1)

        @pl.when(chunk + 1 == chunks)
        def _():
            gather_pass(1, fullcot, chunk)

        with_last, with_before, through = boundary(start, lengths_ref)
        to_last = with_last.astype(f32)
        from_before = with_before.astype(f32)
        passes = through.astype(f32)
        acc_dot[...] = jnp.zeros_like(acc_dot)

        def one_pair(pair, nothing):
            columns = pl.ds(pl.multiple_of(pair * LANES, LANES), LANES)
            pre = causal_taps(vext, tapv_ref[:, columns], biasv_ref[:, columns], masks, columns)
            kbuf[1, :, columns] = pre
            x = pre * sigmoid(pre)
            weighted = x * step_cols[pair]
            both = halves(weighted)
            results = []
            for half in range(2):
                head = 2 * pair + half
                c_col = cum_cols[head]
                c_row = cum_rows[pl.ds(head, 1), :]
                top = scores[:LANES, :LANES] * jnp.exp(c_col[:LANES] - c_row[:, :LANES] + neg_bias[:LANES, :LANES])
                low_left = scores[LANES:, :LANES] * jnp.exp(c_col[LANES:] - c_row[:, :LANES] + neg_bias[LANES:, :LANES])
                low_right = scores[LANES:, LANES:] * jnp.exp(
                    c_col[LANES:] - c_row[:, LANES:] + neg_bias[LANES:, LANES:]
                )
                upper = dot_nn(top.astype(bf16), both[:LANES])
                lower = dot_nn(jnp.concatenate([low_left, low_right], axis=1).astype(bf16), both)
                out = jnp.concatenate([upper, lower], axis=0)
                results.append(out[:, :LANES] + out[:, LANES:])
            inside = jnp.where(first_half, results[0], results[1])
            cum_pair = jnp.where(first_half, cum_cols[2 * pair], cum_cols[2 * pair + 1])
            cum_last = cum_pair[Q - 1 :]
            held = states[chunk, pair]
            carried = dot_halves(leave_low, held) * (jnp.exp(cum_pair) * from_before)
            y = inside + carried + skip_ref[:, columns] * x
            y_all[chunk, :, columns] = y
            to_end = jnp.exp(cum_last - cum_pair) * to_last
            states[chunk + 1, pair] = held * (jnp.exp(cum_last) * passes) + dot_halves(entry_t, to_end * weighted)
            gate = gate_all[chunk, :, columns]
            gated = y * (gate * sigmoid(gate))
            acc_dot[...] += gated * gated
            return nothing

        lax.fori_loop(0, pairs, one_pair, 0)
        keep_store(chunk, 1).start()
        sq_rows[chunk] = ones_rows(acc_dot[...])

        return nothing

    lax.fori_loop(0, chunks, forward_chunk, 0)
    normed_store(chunks - 1).wait()
    keep_store(chunks - 1, 0).wait()
    keep_store(chunks - 1, 1).wait()
    dsext = sext
    dsext[pl.ds(Q, 8)] = jnp.zeros((8, dsext.shape[1]), f32)

    def send_sums(chunk, step):
        return pltpu.make_async_remote_copy(
            src_ref=ex_send.at[chunk], dst_ref=ex_recv.at[chunk, slots - step], send_sem=es.at[chunk, step],
            recv_sem=er.at[chunk, slots - step], device_id=(group, lax.rem(slot + step, slots)), device_id_type=MESH,
        )

    def products(chunk):
        gather_wait(1, pcot, fullcot, chunk)
        x_load(fullcot, chunk).start()

        @pl.when(chunk >= 2)
        def _():
            gather_near(1, pcot, fullcot, chunk - 2)

        @pl.when(chunk >= 3)
        def _():
            gather_far(1, pcot, fullcot, chunk - 3)

        x_load(fullcot, chunk).wait()
        for half in range(2):
            columns = slice(half * (dsc.shape[1] // 2), (half + 1) * (dsc.shape[1] // 2))
            value = dot_nn(xbuf[0].reshape(Q, width), wo[pl.ds(0, width), columns])
            for shard in range(1, slots):
                value = value + dot_nn(xbuf[shard].reshape(Q, width), wo[pl.ds(shard * width, width), columns])
            dsc[:, columns] = value
        acc_prod[...] = jnp.zeros_like(acc_prod)

        def product(pair, nothing):
            columns = pl.ds(pl.multiple_of(pair * LANES, LANES), LANES)
            gate = gate_all[chunk, :, columns]
            gated = y_all[chunk, :, columns] * (gate * sigmoid(gate))
            acc_prod[...] += dsc[:, columns] * ggain_ref[:, columns] * gated
            return nothing

        lax.fori_loop(0, pairs, product, 0)
        ex_send[chunk, pl.ds(0, 8)] = sq_rows[chunk]
        ex_send[chunk, pl.ds(8, 8)] = ones_rows(acc_prod[...])
        for step in range(1, slots):
            send_sums(chunk, step).start()

    def backward_chunk(index, nothing):
        chunk = chunks - 1 - index
        start = chunk * Q
        keep_load(chunk).start()
        @pl.when(index > 0)
        def _():
            dvext[pl.ds(Q, 8)] = dvext[pl.ds(0, 8)]
            dsext[pl.ds(Q, 8)] = dsext[pl.ds(0, 8)]
            for which in range(5):
                store(which, chunk + 1).wait()

        def later_mask(shift):
            position = start + lax.broadcasted_iota(jnp.int32, (Q, LANES), 0)
            same = segment_at(position, lengths_ref) == segment_at(position + shift, lengths_ref)
            return (same & (position + shift < chunks * Q)).astype(f32)

        log_decay = prepare(chunk, True)
        for shift in range(1, 4):
            masks[shift - 1] = later_mask(shift)
        step_in = stepin_all[chunk]
        spre = spre_all[chunk]
        spre_sig = sigmoid(spre)
        state_conv = spre * spre_sig
        entry = state_conv[:, :LANES]
        leave = state_conv[:, LANES:]
        scores[...] = dot_nt(entry, leave, highest)
        entry_low = entry.astype(bf16)
        leave_t = leave.T.astype(bf16)
        @pl.when(chunk > 0)
        def _():
            gather_pass(1, fullcot, chunk - 1)

        with_last, with_before, through = boundary(start, lengths_ref)
        to_last = with_last.astype(f32)
        from_before = with_before.astype(f32)
        passes = through.astype(f32)
        row_lane = lax.broadcasted_iota(jnp.int32, (Q, LANES), 0)
        for ref in (d_scores, d_entry, d_leave, acc_step, acc_cum, acc_dot):
            ref[...] = jnp.zeros_like(ref)

        sums = ex_send[chunk]
        for step in range(1, slots):
            send_sums(chunk, step).wait()
        for step in range(1, slots):
            sums = sums + ex_recv[chunk, step]
        rms_row = lax.rsqrt(sums[0:1] * (1.0 / inner_total) + epsilon)
        coef_row = rms_row * rms_row * rms_row * sums[8:9] * (1.0 / inner_total)
        cols[0] = jnp.broadcast_to(rms_row, (LANES, Q)).T
        cols[1] = jnp.broadcast_to(coef_row, (LANES, Q)).T
        keep_load(chunk).wait()

        def one_pair(pair, nothing):
            columns = pl.ds(pl.multiple_of(pair * LANES, LANES), LANES)
            rms = cols[0]
            pre = kbuf[1, :, columns]
            pre_sig = sigmoid(pre)
            x = pre * pre_sig
            step_pair = step_cols[pair]
            weighted = x * step_pair
            gate = gate_all[chunk, :, columns]
            gate_sig = sigmoid(gate)
            gate_silu = gate * gate_sig
            y = y_all[chunk, :, columns]
            gated = y * gate_silu
            d_scaled = dsc[:, columns]
            ggain = ggain_ref[:, columns]
            normalized = gated * rms
            scbuf[:, columns] = (normalized * ggain).astype(bf16)
            d_gated = rms * (d_scaled * ggain) - gated * cols[1]
            sumv_ref[pl.ds(0, 8), columns] += fold_rows(d_scaled * normalized)
            d_gate = (d_gated * y * (gate_sig + gate_silu * (1.0 - gate_sig))).astype(bf16)
            dgbuf[:, columns] = d_gate
            acc_dot[...] += d_gate.astype(f32) * gate
            d_y = d_gated * gate_silu
            skip = skip_ref[:, columns]
            sumv_ref[pl.ds(8, 8), columns] += fold_rows(d_y * x)
            y_scan = y - skip * x

            d_y_t = d_y.T.astype(bf16)
            d_y_both = halves(d_y)
            weighted_low = weighted.astype(bf16)
            results = []
            for half in range(2):
                head = 2 * pair + half
                own = jnp.where(first_half if half == 0 else ~first_half, weighted_low, jnp.zeros_like(weighted_low))
                d_m_top = dot_nn(own[:LANES], d_y_t)
                d_m_low = dot_nn(own[LANES:], d_y_t[:, LANES:])
                c_col = cum_cols[head]
                c_row = cum_rows[pl.ds(head, 1), :]
                l_top = jnp.exp(c_row - jnp.concatenate([c_col[:LANES]] * 2, axis=1) + neg_bias[:LANES])
                l_low = jnp.exp(c_row[:, LANES:] - c_col[LANES:] + neg_bias[LANES:, LANES:])
                d_scores[:LANES] += d_m_top * l_top
                d_scores[LANES:, LANES:] += d_m_low * l_low
                m_top = (scores[:LANES] * l_top).astype(bf16)
                m_low = (scores[LANES:, LANES:] * l_low).astype(bf16)
                upper = dot_nn(m_top, d_y_both)
                lower = dot_nn(m_low, d_y_both[LANES:])
                out = jnp.concatenate([upper, lower], axis=0)
                results.append(out[:, :LANES] + out[:, LANES:])
            d_weighted = jnp.where(first_half, results[0], results[1])
            cum_pair = jnp.where(first_half, cum_cols[2 * pair], cum_cols[2 * pair + 1])
            cum_last = cum_pair[Q - 1 :]
            to_end = jnp.exp(cum_last - cum_pair) * to_last
            from_start = jnp.exp(cum_pair) * from_before
            d_state = d_carry[pair]
            held = states[chunk, pair]
            d_weighted = d_weighted + dot_halves(entry_low, d_state) * to_end
            d_entry[...] += dot_nt((to_end * weighted).astype(bf16), d_state.astype(bf16))
            moved = from_start * d_y
            d_leave[...] += dot_nt(moved.astype(bf16), held.astype(bf16))
            state_dot = jnp.sum(states[chunk + 1, pair] * d_state, axis=0, keepdims=True)
            d_carry[pair] = d_state * (jnp.exp(cum_last) * passes) + dot_halves(leave_t, moved)

            to_step = d_weighted * x
            to_cum = d_y * y_scan - to_step * step_pair + jnp.where(row_lane == Q - 1, state_dot, 0.0)
            acc_step[...] += dot_nn(halves(to_step), gathers[pair])
            acc_cum[...] += dot_nn(halves(to_cum), gathers[pair])

            d_x = d_weighted * step_pair + skip * d_y
            d_pre = d_x * (pre_sig + x * (1.0 - pre_sig))
            dvext[pl.ds(0, Q), columns] = d_pre
            sumv_ref[pl.ds(16, 8), columns] += fold_rows(d_pre)
            vraw = kbuf[0, :, columns]
            total = tapv_ref[3:4, columns] * d_pre
            sumv_ref[pl.ds(48, 8), columns] += fold_rows(vraw * d_pre)
            for shift in range(1, 4):
                moved_back = dvext[pl.ds(shift, Q), columns] * masks[shift - 1]
                total = total + tapv_ref[3 - shift : 4 - shift, columns] * moved_back
                sumv_ref[pl.ds(48 - 8 * shift, 8), columns] += fold_rows(vraw * moved_back)
            d_value = total.astype(bf16)
            dvbuf[:, columns] = d_value
            acc_dot[...] += d_value.astype(f32) * vraw
            return nothing

        lax.fori_loop(0, pairs, one_pair, 0)
        for which in range(3):
            store(which, chunk).start()

        @pl.when(chunk > 0)
        def _():
            products(chunk - 1)


        can_see = (neg_bias[...] == 0.0).astype(f32)
        d_log = dot_nn(can_see, acc_cum[...], highest)
        rate = jnp.exp(rate_ref[...])
        d_step_in = (acc_step[...] - d_log * rate) * sigmoid(step_in)
        d_step = d_step_in.astype(bf16)
        dsmall_ref[pl.ds(start, Q), 2 * LANES :] = d_step
        step_raw = step_in - stepb_ref[...]
        acc_dot[...] += jnp.where(lane < 2 * pairs, d_step.astype(f32) * step_raw, 0.0)
        sumh_ref[pl.ds(0, 8)] += fold_rows(d_step_in)
        sumh_ref[pl.ds(8, 8)] += fold_rows(d_log * log_decay)

        d_scores_now = d_scores[...]
        d_b = d_entry[...] + dot_halves(d_scores_now.astype(bf16), leave)
        d_c = d_leave[...] + dot_halves(d_scores_now.T.astype(bf16), entry)
        for half, grad in enumerate((d_b, d_c)):
            columns = slice(half * LANES, (half + 1) * LANES)
            part = spre_sig[:, columns]
            d_pre = grad * (part + state_conv[:, columns] * (1.0 - part))
            dsext[pl.ds(0, Q), columns] = d_pre
            sums_ref[pl.ds(0, 8), columns] += fold_rows(d_pre)
            sraw = sraw_all[chunk, :, columns]
            total = taps_ref[3:4, columns] * d_pre
            sums_ref[pl.ds(32, 8), columns] += fold_rows(sraw * d_pre)
            for shift in range(1, 4):
                moved_back = dsext[pl.ds(shift, Q), columns] * masks[shift - 1]
                total = total + taps_ref[3 - shift : 4 - shift, columns] * moved_back
                sums_ref[pl.ds(32 - 8 * shift, 8), columns] += fold_rows(sraw * moved_back)
            d_state_raw = total.astype(bf16)
            dsmall_ref[pl.ds(start, Q), columns] = d_state_raw
            acc_dot[...] += d_state_raw.astype(f32) * sraw
        dot_ref[chunk] = ones_rows(acc_dot[...])

        for shard in range(slots):
            here = pl.ds(shard * width, width)
            part = dot_nt(dgbuf[...], wg[here]) + dot_nt(dvbuf[...], wv[here])
            part = part + dot_nt(dsmall_ref[pl.ds(start, Q), : 2 * LANES], ws[here]) + dot_nt(d_step, wt[here])
            bbuf[:, shard * width : (shard + 1) * width] = part.astype(bf16)
        store(3, chunk).start()
        for shard in range(slots):
            part = dot_nt(scbuf[...], wo[pl.ds(shard * width, width)])
            zbuf[:, shard * width : (shard + 1) * width] = part.astype(bf16)
        store(4, chunk).start()
        return nothing

    products(chunks - 1)
    lax.fori_loop(0, chunks, backward_chunk, 0)
    for which in range(5):
        store(which, 0).wait()
    gather_drain(0, ptok, fulltok)
    gather_drain(1, pcot, fullcot)


def head(send_run, arrive_from, lengths, tokens, cotangent, wg, wv, ws, wt, wo, small):
    groups, slots = lax.axis_size("dp"), lax.axis_size("tensor")
    runs, run, width = tokens.shape
    rows = runs * run
    chunks, per_chunk = rows // Q, Q // run
    model, inner = wg.shape
    pairs = inner // LANES
    vmem, anywhere, smem = (pl.BlockSpec(memory_space=s) for s in (pltpu.VMEM, pl.ANY, pltpu.SMEM))
    dma = pltpu.SemaphoreType.DMA
    shape = jax.ShapeDtypeStruct
    return pl.pallas_call(
        head_kernel,
        out_shape=[
            shape((chunks, slots, per_chunk, run, width), bf16),
            shape((chunks, slots, per_chunk, run, width), bf16),
            shape((chunks, Q, model), bf16),
            shape((chunks, Q, inner), bf16),
            shape((chunks, Q, inner), bf16),
            shape((chunks, Q, inner), bf16),
            shape((chunks, Q, model), bf16),
            shape((chunks, 2, Q, inner), f32),
            shape((chunks, Q, model), bf16),
            shape((rows, 3 * LANES), bf16),
            shape((rows, 1), f32),
            shape((chunks, 8, Q), f32),
            shape((56, inner), f32),
            shape((40, 2 * LANES), f32),
            shape((16, LANES), f32),
        ],
        in_specs=[smem] * 3 + [anywhere] * 7 + [vmem] * len(small),
        out_specs=[anywhere] * 9 + [vmem] * 6,
        scratch_shapes=[
            pltpu.VMEM(wg.shape, bf16), pltpu.VMEM(wv.shape, bf16), pltpu.VMEM(ws.shape, bf16),
            pltpu.VMEM(wt.shape, bf16), pltpu.VMEM(wo.shape, bf16),
            pltpu.VMEM((runs, run, width), bf16),
            pltpu.VMEM((runs, run, width), bf16),
            pltpu.VMEM((groups, run, width), bf16),
            pltpu.VMEM((groups, run, width), bf16),
            pltpu.VMEM((groups, run, width), bf16),
            pltpu.VMEM((slots, per_chunk, run, width), bf16),
            pltpu.VMEM((Q, model), bf16),
            pltpu.VMEM((2, Q, inner), f32),
            pltpu.VMEM((chunks, Q, inner), f32),
            pltpu.VMEM((chunks, Q, inner), f32),
            pltpu.VMEM((chunks, Q, 2 * LANES), f32),
            pltpu.VMEM((chunks, Q, 2 * LANES), f32),
            pltpu.VMEM((chunks, Q, LANES), f32),
            pltpu.VMEM((chunks + 1, pairs, LANES, LANES), f32),
            pltpu.VMEM((pairs, LANES, LANES), f32),
            pltpu.VMEM((Q + 8, inner), f32),
            pltpu.VMEM((Q + 8, inner), f32),
            pltpu.VMEM((Q + 8, 2 * LANES), f32),
            pltpu.VMEM((2 * pairs, Q, LANES), f32),
            pltpu.VMEM((pairs, Q, LANES), f32),
            pltpu.VMEM((LANES, Q), f32),
            pltpu.VMEM((Q, Q), f32),
            pltpu.VMEM((Q, Q), f32),
            pltpu.VMEM((Q, Q), f32),
            pltpu.VMEM((Q, LANES), f32),
            pltpu.VMEM((Q, LANES), f32),
            pltpu.VMEM((Q, LANES), f32),
            pltpu.VMEM((Q, LANES), f32),
            pltpu.VMEM((Q, LANES), f32),
            pltpu.VMEM((Q, LANES), f32),
            pltpu.VMEM((Q, inner), f32),
            pltpu.VMEM((Q, inner), bf16),
            pltpu.VMEM((Q, inner), bf16),
            pltpu.VMEM((Q, inner), bf16),
            pltpu.VMEM((Q, model), bf16),
            pltpu.VMEM((Q, model), bf16),
            pltpu.VMEM((chunks, 8, Q), f32),
            pltpu.VMEM((chunks, 16, Q), f32),
            pltpu.VMEM((chunks, slots, 16, Q), f32),
            pltpu.VMEM((2, Q, LANES), f32),
            pltpu.VMEM((3, Q, LANES), f32),
            pltpu.VMEM((pairs, 2 * LANES, LANES), bf16),
            dma((5,)), dma((2,)), dma((groups,)), dma((groups,)), dma((groups,)), dma((groups,)),
            dma((2, chunks, 4)), dma((2, chunks, slots)), dma((2, chunks)), dma, dma, dma((3,)), dma((5,)),
            dma((chunks, slots)), dma((chunks, slots)),
        ],
        compiler_params=pltpu.CompilerParams(collective_id=2, has_side_effects=True, vmem_limit_bytes=HEAD_VMEM),
        name="head",
    )(send_run, arrive_from, lengths, tokens, cotangent, wg, wv, ws, wt, wo, *small)


def tail_kernel(
    back_run_ref, return_from_ref, out_part, back_part, normed, tokens, cotangent, scaled, d_gate, d_value,
    row_dot_ref, inv_ref, gain_ref, small_ref, small_z_ref, dsmall_ref,
    layer_ref, tgrad_ref, small_out, ngain_out, share0, share1, share2, state_out, step_out,
    z_recv, z_comb, z_own, z_mix, ptok, pcot, rd_recv, rd_col, row_buf, slots_buf, arrive_out, arrive_grad, left, right, full,
    core_recv, chip_recv, total, sz_recv, small_all, small_recv, ngain_all, ngain_recv,
    thin, thin_core, thin_chip, thin_own, thin_z,
    load_sem, mix_sem, left_sem, right_sem, zs, zr, zc, rds, rdr, szs, szr, sms, smr, ngs, ngr, rs, rr, cs, cr, hs, hr, tcs, ths, thr, tzs, tzr,
):
    groups, slots = lax.axis_size("dp"), lax.axis_size("tensor")
    group, slot = lax.axis_index("dp"), lax.axis_index("tensor")
    jobs = z_recv.shape[0]
    pieces = jobs // 2
    runs, run, width = layer_ref.shape
    rows = runs * run
    piece_run = run // pieces
    chips = groups // 2
    core = lax.rem(group, 2)
    chip = group // 2
    grow = share0.shape[0]
    per_block = 256 // grow
    blocks = full.shape[1] // per_block
    inner = share0.shape[1]
    last = slots - 1

    greet(groups, slots)

    def z_small(source, target, send_sem, recv_sem, step):
        return pltpu.make_async_remote_copy(
            src_ref=source, dst_ref=target.at[slots - step], send_sem=send_sem.at[step],
            recv_sem=recv_sem.at[slots - step], device_id=(group, lax.rem(slot + step, slots)), device_id_type=MESH,
        )

    def send_dot(step):
        return z_small(row_dot_ref, rd_recv, rds, rdr, step)

    def send_state(step):
        return z_small(small_z_ref, sz_recv, szs, szr, step)

    for step in range(1, slots):
        send_state(step).start()
        send_dot(step).start()

    def piece_of(job, shard):
        source = out_part if job < pieces else back_part
        return source.at[:, pl.ds((job % pieces) * piece_run, piece_run), pl.ds(shard * width, width)]

    def landing(job, me, to):
        return z_recv.at[job, me if me < to else me - 1], zr.at[job, me if me < to else me - 1]

    def z_push(job, number, shard, to, source, target, sem):
        return pltpu.make_async_remote_copy(
            src_ref=source, dst_ref=target, send_sem=zs.at[job, number], recv_sem=sem, device_id=(group, to),
            device_id_type=MESH,
        )

    def direct(job, me, early):
        def push(number, to):
            return z_push(job, number, to, to, piece_of(job, to), *landing(job, me, to))

        def to_mix(number, shard, to):
            return z_push(job, number, shard, to, piece_of(job, shard), z_comb.at[job], zc.at[job])

        if me == 0:
            return [to_mix(0, 3, 1)] if early else [push(1, 2), push(2, 1)]
        if me == last:
            return [to_mix(0, 0, 2)] if early else [push(1, 1), push(2, 2)]
        if early:
            return []
        return [push(0, 0), push(1, 2)] if me == 1 else [push(0, 3), push(1, 1)]

    def mixed(job, me):
        to = 3 if me == 1 else 0
        return z_push(job, 2, to, to, z_mix.at[job], *landing(job, me, to))

    def own_load(kind):
        source = back_part if kind else out_part
        return pltpu.make_async_copy(source.at[:, :, pl.ds(slot * width, width)], z_own.at[kind], load_sem.at[kind])

    def mix_load(job, me):
        return pltpu.make_async_copy(piece_of(job, 3 if me == 1 else 0), z_mix.at[job], mix_sem.at[job])

    def shard_load(which):
        source, target = ((tokens, ptok), (cotangent, pcot))[which]
        return pltpu.make_async_copy(source.at[:, slot], target, load_sem.at[2 + which])

    def push(job, early):
        for me in (0, last) if early else range(slots):
            @pl.when(slot == me)
            def _(me=me):
                for copy in direct(job, me, early):
                    copy.start()

    def combine(job):
        for me in (1, 2):
            @pl.when(slot == me)
            def _(me=me):
                mix_load(job, me).wait()
                z_push(job, 2, 0, 0, z_comb.at[job], z_comb.at[job], zc.at[job]).wait_recv()
                both = z_mix[job].astype(f32) + z_comb[job].astype(f32)
                z_mix[job] = both.astype(bf16)
                mixed(job, me).start()

    rights = (scaled, d_gate, d_value)
    shares = (share0, share1, share2)

    def right_load(which):
        return pltpu.make_async_copy(rights[which], right.at[which % 2], right_sem.at[which])

    def left_load(which, block, place):
        if which == 0:
            per_shard = width // 256
            columns = pl.ds(pl.multiple_of(lax.rem(block, per_shard) * 256, 256), 256)
            source = cotangent.at[:, block // per_shard, :, :, columns]
        else:
            source = normed.at[:, :, :, pl.ds(pl.multiple_of(block * 256, 256), 256)]
        return pltpu.make_async_copy(source, left.at[place], left_sem.at[place])

    def grad_blocks(which, begin, end):
        def one(block, nothing):
            place = lax.rem(block, 2)

            @pl.when(block + 1 < blocks)
            def _():
                left_load(which, block + 1, 1 - place).start()

            left_load(which, block, place).wait()
            value = lax.dot_general(
                left[place].reshape(rows, 256), right[which % 2], (((0,), (0,)), ((), ())), preferred_element_type=f32
            )
            full[which % 2, pl.ds(block * per_block, per_block)] = value.reshape(per_block, grow, -1).astype(bf16)
            if which == 1:
                value = lax.dot_general(
                    left[place].reshape(rows, 256), dsmall_ref[...], (((0,), (0,)), ((), ())), preferred_element_type=f32
                )
                thin[pl.ds(block * per_block, per_block)] = value.reshape(per_block, grow, -1)
            return nothing

        lax.fori_loop(begin, end, one, 0)

    partner = group + 1 - 2 * core

    def core_send(which):
        theirs = full.at[which % 2].reshape(chips, 2, grow, inner).at[:, 1 - core]
        return pltpu.make_async_remote_copy(
            src_ref=theirs, dst_ref=core_recv.at[which], send_sem=cs.at[which], recv_sem=cr.at[which],
            device_id=(partner, slot), device_id_type=MESH,
        )

    def chip_send(which, step):
        other = lax.rem(chip + step, chips)
        return pltpu.make_async_remote_copy(
            src_ref=full.at[which % 2, 2 * other + core], dst_ref=chip_recv.at[which, chips - step],
            send_sem=hs.at[which, step], recv_sem=hr.at[which, chips - step], device_id=(2 * other + core, slot),
            device_id_type=MESH,
        )

    def chip_pushes(which):
        core_send(which).wait()

        def one(step, nothing):
            other = lax.rem(chip + step, chips)
            mine = 2 * other + core
            both = full[which % 2, mine].astype(f32) + core_recv[which, other].astype(f32)
            full[which % 2, mine] = both.astype(bf16)
            chip_send(which, step).start()
            return nothing

        lax.fori_loop(1, chips, one, 0)
        shares[which][...] = full[which % 2, group].astype(f32) + core_recv[which, chip].astype(f32)

    def chip_drain(which):
        def drain(step, nothing):
            chip_send(which, step).wait_send()
            return nothing

        lax.fori_loop(1, chips, drain, 0)

    def chip_total(which):
        def one(step, nothing):
            pltpu.make_async_remote_copy(
                src_ref=chip_recv.at[which, step], dst_ref=chip_recv.at[which, step], send_sem=hs.at[which, step],
                recv_sem=hr.at[which, step], device_id=(group, slot), device_id_type=MESH,
            ).wait_recv()
            shares[which][...] += chip_recv[which, step].astype(f32)
            return nothing

        lax.fori_loop(1, chips, one, 0)

    def thin_core_send():
        theirs = thin.reshape(chips, 2, grow, thin.shape[2]).at[:, 1 - core]
        return pltpu.make_async_remote_copy(
            src_ref=theirs, dst_ref=thin_core, send_sem=tcs.at[0], recv_sem=tcs.at[1], device_id=(partner, slot),
            device_id_type=MESH,
        )

    def thin_chip_send(step):
        other = lax.rem(chip + step, chips)
        return pltpu.make_async_remote_copy(
            src_ref=thin.at[2 * other + core], dst_ref=thin_chip.at[chips - step], send_sem=ths.at[step],
            recv_sem=thr.at[chips - step], device_id=(2 * other + core, slot), device_id_type=MESH,
        )

    def thin_pushes():
        thin_core_send().wait()

        def one(step, nothing):
            other = lax.rem(chip + step, chips)
            thin[2 * other + core] = thin[2 * other + core] + thin_core[other]
            thin_chip_send(step).start()
            return nothing

        lax.fori_loop(1, chips, one, 0)
        thin_own[...] = thin[group] + thin_core[chip]

    def thin_z_send(step):
        other = lax.rem(slot + step, slots)
        part = state_out.shape[0]
        return pltpu.make_async_remote_copy(
            src_ref=thin_own.at[pl.ds(other * part, part), pl.ds(0, 2 * LANES)], dst_ref=thin_z.at[slots - step],
            send_sem=tzs.at[step], recv_sem=tzr.at[slots - step], device_id=(group, other), device_id_type=MESH,
        )

    def thin_total():
        def one(step, nothing):
            pltpu.make_async_remote_copy(
                src_ref=thin_chip.at[step], dst_ref=thin_chip.at[step], send_sem=ths.at[step], recv_sem=thr.at[step],
                device_id=(group, slot), device_id_type=MESH,
            ).wait_recv()
            thin_own[...] += thin_chip[step]
            return nothing

        lax.fori_loop(1, chips, one, 0)
        for step in range(1, slots):
            thin_z_send(step).start()
        step_out[...] = thin_own[:, 2 * LANES :]

    def thin_finish():
        part = state_out.shape[0]
        acc = thin_own[pl.ds(slot * part, part), : 2 * LANES]
        for step in range(1, slots):
            thin_z_send(step).wait()
        for step in range(1, slots):
            acc = acc + thin_z[step]
        state_out[...] = acc

        def drain(step, nothing):
            thin_chip_send(step).wait_send()
            return nothing

        lax.fori_loop(1, chips, drain, 0)

    def dp_small(source, target, send_sem, recv_sem, step):
        return pltpu.make_async_remote_copy(
            src_ref=source, dst_ref=target.at[groups - step], send_sem=send_sem.at[step],
            recv_sem=recv_sem.at[groups - step], device_id=(lax.rem(group + step, groups), slot), device_id_type=MESH,
        )

    def dp_small_start(source, target, send_sem, recv_sem):
        def one(step, nothing):
            dp_small(source, target, send_sem, recv_sem, step).start()
            return nothing

        lax.fori_loop(1, groups, one, 0)

    def dp_small_finish(source, target, send_sem, recv_sem, result):
        result[...] = source[...]

        def one(step, nothing):
            pltpu.make_async_remote_copy(
                src_ref=target.at[step], dst_ref=target.at[step], send_sem=send_sem.at[step],
                recv_sem=recv_sem.at[step], device_id=(group, slot), device_id_type=MESH,
            ).wait_recv()
            result[...] += target[step]
            return nothing

        lax.fori_loop(1, groups, one, 0)

        def drain(step, nothing):
            dp_small(source, target, send_sem, recv_sem, step).wait_send()
            return nothing

        lax.fori_loop(1, groups, drain, 0)

    arrives = (arrive_out, arrive_grad)

    def row_send(job, step):
        other = lax.rem(group + step, groups)
        return pltpu.make_async_remote_copy(
            src_ref=slots_buf.at[job % pieces, other], dst_ref=arrives[job // pieces].at[job % pieces, group], send_sem=rs.at[job, other],
            recv_sem=rr.at[job, group], device_id=(other, slot), device_id_type=MESH,
        )

    def rows_drain(job):
        def one(step, nothing):
            row_send(job, step).wait_send()
            return nothing

        lax.fori_loop(1, groups, one, 0)

    def finish(job):
        kind, piece = job // pieces, job % pieces
        here = pl.ds(piece * piece_run, piece_run)
        tall = runs * piece_run
        for me in range(slots):
            @pl.when(slot == me)
            def _(me=me):
                acc = z_own[kind, :, here, :].astype(f32)
                for source in ((1, 2) if me in (0, 3) else tuple(s for s in range(slots) if s != me)):
                    place, sem = landing(job, source, me)
                    z_push(job, 0, 0, 0, place, place, sem).wait_recv()
                    acc = acc + place[...].astype(f32)
                total[...] = acc
        summed = total[...].reshape(tall, width)
        kept = ptok[:, :, here, :].reshape(tall, width).astype(f32)
        if kind == 0:
            result = kept + summed
        else:
            inv = inv_ref[:, here, :].reshape(tall, 1)
            unit = kept * inv
            ngain_all[...] += fold_rows(summed * unit)
            dot_cols = rd_col[:, here, :].reshape(tall, LANES)
            dot_cols = jnp.concatenate([dot_cols] * (width // LANES), axis=1)
            cot = pcot[:, :, here, :].reshape(tall, width).astype(f32)
            result = cot + inv * (summed * gain_ref[...] - unit * dot_cols)
        row_buf[...] = result.astype(bf16).reshape(runs, piece_run, width)

        def fill(step, nothing):
            other = lax.rem(group + step, groups)
            slots_buf[job % pieces, other] = row_buf[back_run_ref[other]]
            row_send(job, step).start()
            return nothing

        if kind == 1:
            rows_drain(job - pieces)
        lax.fori_loop(1, groups, fill, 0)
        arrives[kind][piece, group] = row_buf[back_run_ref[group]]

    def rows_wait(kind):
        for job in range(kind * pieces, (kind + 1) * pieces):
            def one(step, nothing, job=job):
                source = lax.rem(group + groups - step, groups)
                pltpu.make_async_remote_copy(
                    src_ref=arrives[kind].at[job % pieces, source], dst_ref=arrives[kind].at[job % pieces, source],
                    send_sem=rs.at[job, source],
                    recv_sem=rr.at[job, source], device_id=(group, slot), device_id_type=MESH,
                ).wait_recv()
                return nothing

            lax.fori_loop(1, groups, one, 0)

    def rows_take(kind, target):
        for piece in range(pieces):
            for index in range(runs):
                target[index, pl.ds(piece * piece_run, piece_run)] = arrives[kind][piece, return_from_ref[index]]

    def let_in(job):
        if job < jobs:
            push(job, False)
            combine(job)

    def step_of(job):
        if job + EARLY < jobs:
            push(job + EARLY, True)
        let_in(job + WINDOW)
        finish(job)

    for job in range(min(EARLY, jobs)):
        push(job, True)
    for job in range(2):
        push(job, False)
    own_load(0).start()
    own_load(1).start()
    shard_load(0).start()
    shard_load(1).start()
    for me in (1, 2):
        @pl.when(slot == me)
        def _(me=me):
            for job in range(jobs):
                mix_load(job, me).start()
    right_load(0).start()
    left_load(0, 0, 0).start()
    right_load(1).start()
    ngain_all[...] = jnp.zeros_like(ngain_all)

    half = blocks // 2
    right_load(0).wait()
    grad_blocks(0, 0, half)
    small_z = small_z_ref[...]
    for step in range(1, slots):
        send_state(step).wait()
    for step in range(1, slots):
        small_z = small_z + sz_recv[step]
    small_all[:, pl.ds(0, inner)] = small_ref[...]
    small_all[:, pl.ds(inner, 2 * LANES)] = small_z
    dp_small_start(small_all, small_recv, sms, smr)
    grad_blocks(0, half, blocks)
    core_send(0).start()
    right_load(2).start()
    for kind in range(2):
        own_load(kind).wait()
        shard_load(kind).wait()
    left_load(1, 0, 0).start()
    combine(0)
    right_load(1).wait()
    grad_blocks(1, 0, half)
    chip_pushes(0)
    grad_blocks(1, half, blocks)
    core_send(1).start()
    thin_core_send().start()
    left_load(2, 0, 0).start()
    rd_total = row_dot_ref[...]
    for step in range(1, slots):
        send_dot(step).wait()
    for step in range(1, slots):
        rd_total = rd_total + rd_recv[step]
    rd_total = rd_total * (1.0 / (width * slots))
    for block in range(rows // 256):
        piece_row = jnp.broadcast_to(rd_total[0:1, block * 256 : (block + 1) * 256], (LANES, 256))
        count = 256 // run
        rd_col[pl.ds(block * count, count)] = piece_row.T.reshape(count, run, LANES)
    combine(1)
    let_in(2)
    right_load(2).wait()
    chip_drain(0)
    grad_blocks(2, 0, half)
    chip_pushes(1)
    thin_pushes()
    grad_blocks(2, half, blocks)
    core_send(2).start()
    for job in range(3, WINDOW):
        let_in(job)
    def out_rows():
        rows_wait(0)
        rows_take(0, layer_ref)

    meanwhile = [
        thin_total,
        lambda: [chip_total(which) for which in range(3)],
        lambda: dp_small_finish(small_all, small_recv, sms, smr, small_out),
    ]
    for job in range(jobs):
        if job == 1:
            chip_pushes(2)
        if job == jobs - 1:
            out_rows()
        step_of(job)
        if job >= jobs // 2 and meanwhile:
            meanwhile.pop(0)()
    dp_small_start(ngain_all, ngain_recv, ngs, ngr)
    for action in meanwhile:
        action()
    rows_wait(1)
    for job in range(pieces, jobs):
        rows_drain(job)
    rows_take(1, tgrad_ref)
    thin_finish()
    chip_drain(1)
    chip_drain(2)
    dp_small_finish(ngain_all, ngain_recv, ngs, ngr, ngain_out)
    for me in range(slots):
        @pl.when(slot == me)
        def _(me=me):
            for job in range(jobs):
                for copy in direct(job, me, True) + direct(job, me, False):
                    copy.wait_send()
                if me in (1, 2):
                    mixed(job, me).wait_send()


def tail(back_run, return_from, out_part, back_part, normed, tokens, cotangent, scaled, d_gate, d_value, row_dot, inv,
         gain, small, small_z, d_small):
    groups, slots = lax.axis_size("dp"), lax.axis_size("tensor")
    runs, run, model = out_part.shape
    width = model // slots
    rows = runs * run
    inner = scaled.shape[1]
    pieces = min(4, run // 16)
    jobs = 2 * pieces
    piece_run = run // pieces
    grow = model // groups
    chips = groups // 2
    vmem, anywhere, smem = (pl.BlockSpec(memory_space=s) for s in (pltpu.VMEM, pl.ANY, pltpu.SMEM))
    dma = pltpu.SemaphoreType.DMA
    shape = jax.ShapeDtypeStruct
    by_chunk = tokens.shape[:1] + tokens.shape[2:]
    part = (runs, piece_run, width)
    return pl.pallas_call(
        tail_kernel,
        out_shape=[
            shape((runs, run, width), bf16), shape((runs, run, width), bf16), shape((8, inner + 2 * LANES), f32),
            shape((8, width), f32),
        ] + [shape((grow, inner), f32)] * 3 + [shape((grow // slots, 2 * LANES), f32), shape((grow, LANES), f32)],
        in_specs=[smem] * 2 + [anywhere] * 8 + [vmem] * 6,
        out_specs=[vmem] * 9,
        scratch_shapes=[
            pltpu.VMEM((jobs, slots - 1) + part, bf16),
            pltpu.VMEM((jobs,) + part, bf16),
            pltpu.VMEM((2, runs, run, width), bf16),
            pltpu.VMEM((jobs,) + part, bf16),
            pltpu.VMEM(by_chunk, bf16),
            pltpu.VMEM(by_chunk, bf16),
            pltpu.VMEM((slots, 8, rows), f32),
            pltpu.VMEM((runs, run, LANES), f32),
            pltpu.VMEM(part, bf16),
            pltpu.VMEM((pieces, groups, piece_run, width), bf16),
            pltpu.VMEM((pieces, groups, piece_run, width), bf16),
            pltpu.VMEM((pieces, groups, piece_run, width), bf16),
            pltpu.VMEM((2,) + by_chunk[:-1] + (256,), bf16),
            pltpu.VMEM((2, rows, inner), bf16),
            pltpu.VMEM((2, groups, grow, inner), bf16),
            pltpu.VMEM((3, chips, grow, inner), bf16),
            pltpu.VMEM((3, chips, grow, inner), bf16),
            pltpu.VMEM(part, f32),
            pltpu.VMEM((slots, 8, 2 * LANES), f32),
            pltpu.VMEM((8, inner + 2 * LANES), f32),
            pltpu.VMEM((groups, 8, inner + 2 * LANES), f32),
            pltpu.VMEM((8, width), f32),
            pltpu.VMEM((groups, 8, width), f32),
            pltpu.VMEM((groups, grow, 3 * LANES), f32),
            pltpu.VMEM((chips, grow, 3 * LANES), f32),
            pltpu.VMEM((chips, grow, 3 * LANES), f32),
            pltpu.VMEM((grow, 3 * LANES), f32),
            pltpu.VMEM((slots, grow // slots, 2 * LANES), f32),
            dma((4,)), dma((jobs,)), dma((2,)), dma((3,)),
            dma((jobs, 3)), dma((jobs, slots - 1)), dma((jobs,)),
            dma((slots,)), dma((slots,)), dma((slots,)), dma((slots,)),
            dma((groups,)), dma((groups,)), dma((groups,)), dma((groups,)),
            dma((jobs, groups)), dma((jobs, groups)),
            dma((3,)), dma((3,)), dma((3, chips)), dma((3, chips)),
            dma((2,)), dma((chips,)), dma((chips,)), dma((slots,)), dma((slots,)),
        ],
        compiler_params=pltpu.CompilerParams(collective_id=3, has_side_effects=True, vmem_limit_bytes=64 << 20),
        name="tail",
    )(back_run, return_from, out_part, back_part, normed, tokens, cotangent, scaled, d_gate, d_value, row_dot, inv, gain,
      small, small_z, d_small)


def pad_heads(values):
    return jnp.pad(values, ((0, 0), (0, LANES - values.shape[1])))


def per_device(
    tokens, cotangent, norm_gain, gate_proj, value_proj, state_proj, step_proj, conv_value, conv_value_bias,
    conv_state, conv_state_bias, step_bias, decay_log, skip_gain, gate_gain, out_proj, token_order, lengths,
):
    groups = lax.axis_size("dp")
    group = lax.axis_index("dp")
    slots = lax.axis_size("tensor")
    slot = lax.axis_index("tensor")
    rows, width = tokens.shape
    model = width * slots
    inner = gate_proj.shape[1]
    heads = step_bias.shape[0]
    run = 2 * rows // groups
    runs = rows // run

    source_run = token_order.reshape(groups, runs, run)[:, :, 0] // run
    source_group = source_run // runs
    from_here = source_group == group
    send_run = jnp.sum(jnp.where(from_here, source_run % runs, 0), axis=1)
    arrive_from = lax.dynamic_index_in_dim(source_group, group, 0, keepdims=False)
    every = jnp.arange(groups, dtype=jnp.int32)
    back_run = jnp.sum(
        jnp.where(arrive_from[None, :] == every[:, None], jnp.arange(runs, dtype=jnp.int32)[None, :], 0), axis=1
    )
    local_run = group * runs + jnp.arange(runs, dtype=jnp.int32)
    return_from = jnp.sum(
        jnp.where(source_run[None] == local_run[:, None, None], every[None, :, None], 0), axis=(1, 2)
    )

    def cut(values):
        return values.reshape(runs, run, values.shape[1])

    gain_full = norm_gain.astype(f32)
    def row(values):
        return jnp.pad(values.astype(f32), (0, model - values.shape[0]))

    rows_of = (norm_gain, gate_gain, conv_value_bias, conv_state_bias, jnp.repeat(skip_gain, HEAD_DIM))
    small = (
        conv_value.astype(f32),
        conv_state.astype(f32),
        pad_heads(jnp.stack([step_bias, decay_log])).reshape(2, 1, LANES),
        jnp.stack([row(v) for v in rows_of]).reshape(len(rows_of), 1, model),
    )
    (full_tokens, full_cotangent, normed, d_gate, d_value, scaled, back_partial, _, out_partial, d_small,
     inv_rms, row_dot, sumv, sums, sumh) = head(
        send_run, arrive_from, lengths, cut(tokens), cut(cotangent), gate_proj, value_proj, state_proj,
        pad_heads(step_proj), out_proj, small,
    )
    row_dot = row_dot.transpose(1, 0, 2).reshape(8, rows)
    normed_cut = normed.reshape(full_tokens.shape[0], full_tokens.shape[2], run, model)
    d_gate, d_value, scaled, back_partial, out_partial = (
        v.reshape(rows, v.shape[2]) for v in (d_gate, d_value, scaled, back_partial, out_partial)
    )
    gain_share = lax.dynamic_slice_in_dim(gain_full, slot * width, width, 0)
    by_head = jnp.pad(sumh.reshape(2, 8, LANES).sum(1).reshape(1, 2 * LANES), ((0, 0), (0, inner - 2 * LANES)))
    small = jnp.concatenate([sumv.reshape(7, 8, inner).sum(1), by_head])
    small_z = jnp.pad(sums.reshape(5, 8, 2 * LANES).sum(1), ((0, 3), (0, 0)))
    layer_output, tokens_grad, small, norm_gain_rows, out_grad_share, gate_share, value_share, state_share, step_share = tail(
        back_run, return_from, cut(out_partial), cut(back_partial), normed_cut, full_tokens, full_cotangent, scaled,
        d_gate, d_value, row_dot, cut(inv_rms), gain_share[None], small, small_z, d_small,
    )
    state_sums = small[:, inner:]
    return (
        layer_output.reshape(rows, width),
        tokens_grad.reshape(rows, width),
        jnp.sum(norm_gain_rows, axis=0),
        gate_share,
        value_share,
        state_share,
        step_share[:, :heads],
        small[3:7, :inner],
        small[2, :inner],
        state_sums[1:5],
        state_sums[0],
        small[7, :heads],
        small[7, LANES : LANES + heads],
        jnp.sum(small[1, :inner].reshape(heads, HEAD_DIM), axis=1),
        small[0, :inner],
        out_grad_share,
    )


def solution(mesh):
    across = P(None, "tensor")
    both = P("dp", "tensor")
    heads = P("tensor")
    return jax.shard_map(
        per_device,
        mesh=mesh,
        in_specs=(
            both, both, P(), across, across, P(), across, across, heads, P(), P(), heads, heads, heads, heads, across,
            P(), P("dp", None),
        ),
        out_specs=(
            both, both, heads, both, both, P(("dp", "tensor"), None), both, across, heads, P(), P(), heads, heads, heads,
            heads, both,
        ),
        check_vma=False,
    )
```
